32 devices in a mesh: shot: 16 (over z, y, core), tm: 2 (over x).
Axes of the slice: x: 2, y: 2, z: 4, core: 2. Of those that a mesh axis runs over, the one named last changes fastest.
Arguments:
- blended: float32 [64, 32, 2048], P(None, 'shot', 'tm'), may hold values from -12 to 12
- delays: int32 [32, 2], replicated, may hold values from 0 to 127, as said below
- thresholds: float32 [2, 64], replicated, may hold values from 0.2 to 1.6
Outputs:
- deblended: bfloat16 [64, 64, 2048], P(None, 'shot', 'tm')
The draws below stay inside these ranges and needn't reach their ends.
Inputs may be any that keep to these rules, and one draw needn't show every extreme that they name: delays[e, k] is the delay of source 2 e + k in experiment e; some source has delay 0 and some has delay 128 - 1.
All inputs are finite; a program needn't handle non-finite values.
Results may differ from the reference program's by a relative error of at most 0.0066.
Values may be sent and summed in bfloat16 or wider, within the bound.
No kernel may reach another device: no remote copies, remote signals or barrier semaphores. Data moves between devices by JAX's collectives and lax.ppermute only.
A program may use at most 64 MiB of HBM per device.

```python
import math
import jax
import jax.numpy as jnp
from jax import lax

SRC = 64
SRC_EXP = 2
WIN = 256
BLK = 128
ITERS = 2
EXPS = 32
RCV = 64
NT = 2048


def draw_delays(key, part):
    entries = EXPS * SRC_EXP
    initial = jax.random.randint(key, (entries,), 0, BLK)
    highest = jax.random.randint(jax.random.fold_in(key, 11), (), 0, entries)
    stride = jax.random.randint(jax.random.fold_in(key, 12), (), 1, entries)
    lowest = (highest + stride) % entries
    values = initial.at[highest].set(BLK - 1).at[lowest].set(0)
    return values.reshape(EXPS, SRC_EXP).astype(jnp.int32)


def block_levels(stream_key, shape, cuts, smallest, high):
    level = 1.0
    for axis_at, parts in cuts:
        draws = jax.random.uniform(jax.random.fold_in(jax.random.fold_in(stream_key, 6), axis_at), (parts,), jnp.float32, smallest / len(cuts), high / len(cuts))
        level = level * jnp.repeat(jnp.exp(draws), shape[axis_at] // parts).reshape((-1,) + (1,) * (len(shape) - 1 - axis_at))
    return level


def noise(key, dims, width, most, pieces=(), held_as=jnp.bfloat16):
    values = width * jax.random.normal(key, dims, jnp.float32)
    if pieces:
        values = values * block_levels(key, dims, pieces, -0.22, 0.18)
    return jnp.clip(values, -most, most).astype(held_as)


def setup_inputs(seed: int = 0) -> dict:
    key_of = jax.random.split(jax.random.key(seed), 4)
    blended = noise(key_of[0], (RCV, EXPS, NT), 2.0, 12.0, ((1, 16), (2, 2)), jnp.float32)
    delays = draw_delays(jax.random.fold_in(key_of[3], 71), 0)
    thresholds = jnp.clip(jnp.exp(jax.random.uniform(key_of[2], (ITERS, SRC), jnp.float32, math.log(0.2), math.log(1.6))), 0.2, 1.6)
    return dict(blended=blended, delays=delays, thresholds=thresholds)


RELAX = 0.5

def blend_one(estimate, delays):
    samples = estimate.shape[1]
    moment = jnp.arange(samples, dtype=jnp.int32)
    source_rows = estimate.reshape(EXPS, SRC_EXP, samples).astype(jnp.float32)
    anchor = moment[None, None, :] - delays[:, :, None]
    picked = jnp.take_along_axis(source_rows, jnp.clip(anchor, 0, samples - 1).astype(jnp.int32), axis=2)
    picked = jnp.where(anchor >= 0, picked, jnp.zeros_like(picked))
    return lax.optimization_barrier(jnp.sum(picked, axis=1))

def spread_one(residual, delays):
    samples = residual.shape[1]
    moment = jnp.arange(samples, dtype=jnp.int32)
    target = moment[None, None, :] + delays[:, :, None]
    widened = jnp.broadcast_to(residual.astype(jnp.float32)[:, None, :], (EXPS, SRC_EXP, samples))
    picked = jnp.take_along_axis(widened, jnp.clip(target, 0, samples - 1).astype(jnp.int32), axis=2)
    picked = jnp.where(target < samples, picked, jnp.zeros_like(picked))
    return picked.reshape(SRC, samples)

def time_tables():
    first_index = jnp.arange(WIN, dtype=jnp.int32)[:, None]
    second_index = jnp.arange(WIN, dtype=jnp.int32)[None, :]
    angle = (first_index * second_index % WIN).astype(jnp.float32) * (2.0 * math.pi / WIN)
    return (jnp.cos(angle).astype(jnp.bfloat16), jnp.sin(angle).astype(jnp.bfloat16))

def filter_one(update, limits):
    samples = update.shape[1]
    windows = samples // WIN
    cos_table, sin_table = time_tables()
    signal = update.astype(jnp.bfloat16).reshape(SRC * windows, WIN)
    scale = 1.0 / math.sqrt(WIN)
    real_time = jnp.dot(signal, cos_table, preferred_element_type=jnp.float32) * scale
    imag_time = -jnp.dot(signal, sin_table, preferred_element_type=jnp.float32) * scale
    halfway = (real_time + 1j * imag_time).reshape(SRC, windows, WIN)
    coeffs = jnp.fft.fft(halfway, axis=0, norm='ortho')
    magnitude = jnp.abs(coeffs)
    bound = limits[:, None, None]
    factor = jnp.maximum(magnitude - bound, 0.0) / jnp.maximum(magnitude, bound)
    restored = jnp.fft.ifft2(coeffs * factor, axes=(0, 2), norm='ortho')
    return jnp.real(restored).reshape(SRC, samples)

def reference(blended, delays, thresholds):

    def receiver(records):
        estimate = jnp.zeros((SRC, records.shape[1]), jnp.bfloat16)
        for sweep in range(ITERS):
            residual = (records - blend_one(estimate, delays)).astype(jnp.bfloat16)
            update = (estimate.astype(jnp.float32) + RELAX * spread_one(residual, delays)).astype(jnp.bfloat16)
            estimate = filter_one(update, thresholds[sweep]).astype(jnp.bfloat16)
        return estimate
    return lax.map(receiver, blended)
```

```python
import functools
import math

import jax
import jax.numpy as jnp
import ml_dtypes
import numpy as np
from jax import lax
from jax.experimental import pallas as pl
from jax.experimental.pallas import tpu as pltpu
from jax.sharding import PartitionSpec as P

SRC = 64
SRC_EXP = 2
WIN = 256
BLK = 128
ITERS = 2


RELAX = 0.5
HALF = WIN // 2
SUB = 8


def split_table(table):
    high = table.astype(ml_dtypes.bfloat16)
    low = (table - high.astype(np.float64)).astype(ml_dtypes.bfloat16)
    return high, low


def half_spectrum_tables():
    moment = np.arange(WIN)
    angle = (moment[:, None] * np.arange(HALF)[None, :] % WIN) * (2.0 * math.pi / WIN)
    nyquist = np.where(moment % 2 == 0, 1.0, -1.0)
    sine = -np.sin(angle)
    sine[:, 0] = nyquist
    forward = np.concatenate([np.cos(angle), sine], axis=1).astype(ml_dtypes.bfloat16)
    inverse = np.concatenate([np.cos(angle), sine], axis=1).T / math.sqrt(WIN)
    inverse[0] *= 0.5
    inverse[HALF] *= 0.5
    source = np.arange(SRC)
    turn = (source[:, None] * source[None, :] % SRC) * (2.0 * math.pi / SRC)
    cosine, sine = np.cos(turn) / math.sqrt(SRC), np.sin(turn) / math.sqrt(SRC)
    onward = np.block([[cosine, sine], [-sine, cosine]])
    pair = []
    for table in (onward / math.sqrt(WIN), onward.T):
        high, low = split_table(table)
        pair.append(np.block([[high, high], [low, low]]))
    return (forward, *split_table(inverse), *pair)


def halves(value):
    high = value.astype(jnp.bfloat16)
    return high, (value - high.astype(jnp.float32)).astype(jnp.bfloat16)


def bfloat(value):
    return value.astype(jnp.bfloat16).astype(jnp.float32)


def product(left, right):
    return jnp.dot(left, right, preferred_element_type=jnp.float32)


def gather_kernel(
    shots,
    delays,
    limits,
    received,
    forward,
    inverse_high,
    inverse_low,
    onward,
    backward,
    out,
    records,
    field,
    mixed,
    back_high,
    back_low,
    traces,
):
    count, receivers, rows, _ = received.shape
    blocks_of_time = count // shots
    experiments, sources = delays.shape[0], SRC
    own = experiments // shots
    windows = records.shape[2] // (2 * own)
    groups = receivers * windows
    parts = windows // blocks_of_time
    lane = lax.broadcasted_iota(jnp.int32, (windows, BLK), 1)
    row = lax.broadcasted_iota(jnp.int32, (windows, BLK), 0)
    lane_of_group = lax.broadcasted_iota(jnp.int32, (sources, HALF), 1)

    for shot in range(shots):
        for block in range(blocks_of_time):
            arrived = received[shot * blocks_of_time + block].astype(jnp.float32)
            for r in range(receivers):
                records[r, shot, block * rows : (block + 1) * rows, :] = arrived[r]

    def record(r, shot, e):
        return tuple(
            records[r, shot, pl.ds(half * own + e, windows, stride=2 * own), :]
            for half in range(2)
        )

    def trace_rows(r, s):
        return pl.ds(r * windows * sources + s, windows, stride=sources)

    def load(r, s):
        return tuple(traces[half, trace_rows(r, s), :] for half in range(2))

    def store(r, s, values):
        for half in range(2):
            traces[half, trace_rows(r, s), :] = values[half]

    def advanced(even, odd, delay):
        by = (BLK - delay) & (BLK - 1)
        even, odd = pltpu.roll(even, by, 1), pltpu.roll(odd, by, 1)
        after = jnp.where(row < windows - 1, pltpu.roll(even, windows - 1, 0), 0.0)
        same = lane < BLK - delay
        return jnp.where(same, even, odd), jnp.where(same, odd, after)

    def delayed(even, odd, delay):
        even, odd = pltpu.roll(even, delay, 1), pltpu.roll(odd, delay, 1)
        before = jnp.where(row > 0, pltpu.roll(odd, 1, 0), 0.0)
        same = lane >= delay
        return jnp.where(same, even, before), jnp.where(same, odd, even)

    def update(sweep):
        def one(shot, carry):
            for e in range(own):
                first = (shot * own + e) * SRC_EXP
                lags = [delays[shot * own + e, k] for k in range(SRC_EXP)]
                for r in range(receivers):
                    even, odd = record(r, shot, e)
                    if sweep > 0:
                        estimate = [load(r, first + k) for k in range(SRC_EXP)]
                        late = [delayed(*estimate[k], lags[k]) for k in range(SRC_EXP)]
                        even = bfloat(even - sum(x[0] for x in late))
                        odd = bfloat(odd - sum(x[1] for x in late))
                    for k in range(SRC_EXP):
                        early = advanced(even, odd, lags[k])
                        values = [RELAX * x for x in early]
                        if sweep > 0:
                            values = [a + b for a, b in zip(estimate[k], values)]
                        store(r, first + k, values)
            return carry

        lax.fori_loop(0, shots, one, 0, unroll=2)

    def columns(group, many=1):
        return slice(group * HALF, (group + many) * HALF)

    def forward_in_time():
        nyquist = jnp.zeros((sources, HALF), jnp.float32)
        for group in range(groups):
            rows_of_group = slice(group * sources, (group + 1) * sources)
            signal = jnp.concatenate([traces[half, rows_of_group, :] for half in range(2)], axis=1)
            signal = signal.astype(jnp.bfloat16)
            spectrum = product(signal, forward[...])
            real, imag = spectrum[:, :HALF], spectrum[:, HALF:]
            moved = pltpu.roll(imag, group, 1) if group else imag
            nyquist = jnp.where(lane_of_group == group, moved, nyquist)
            imag = jnp.where(lane_of_group == 0, 0.0, imag)
            put(field, columns(group), real, imag)
        put(field, columns(groups), nyquist, jnp.zeros_like(nyquist))

    def put(ref, where, real, imag):
        real_high, real_low = halves(real)
        imag_high, imag_low = halves(imag)
        for at, value in enumerate((real_high, imag_high, real_low, imag_low)):
            ref[at * sources : (at + 1) * sources, where] = value

    def chunks():
        yield columns(groups)
        for group in range(0, groups, 2):
            yield columns(group, 2)

    def mixing(table, ref, where):
        both = product(table[...], ref[:, where])
        total = both[: 2 * sources] + both[2 * sources :]
        return total[:sources], total[sources:]

    def shrink(sweep):
        limit = limits[sweep : sweep + 1, :]
        p = lax.broadcasted_iota(jnp.int32, (sources, sources), 0)
        q = lax.broadcasted_iota(jnp.int32, (sources, sources), 1)
        bound = jnp.sum(jnp.where(p == q, limit, 0.0), axis=1, keepdims=True)
        mirrored = (p + q == 0) | (p + q == sources)
        bound_mirrored = jnp.sum(jnp.where(mirrored, limit, 0.0), axis=1, keepdims=True)
        for where in chunks():
            real, imag = mixing(onward, field, where)
            inverse_size = lax.rsqrt(real * real + imag * imag)
            factor = jnp.maximum(1.0 - bound * inverse_size, 0.0) + jnp.maximum(
                1.0 - bound_mirrored * inverse_size, 0.0
            )
            put(mixed, where, real * factor, imag * factor)

    def back_in_source():
        nyquist = None
        group = 0
        for where in chunks():
            real, imag = mixing(backward, mixed, where)
            if nyquist is None:
                nyquist = real
                continue
            for part in range(2):
                own_real, own_imag = real[:, columns(part)], imag[:, columns(part)]
                moved = pltpu.roll(nyquist, HALF - group, 1) if group else nyquist
                own_imag = jnp.where(lane_of_group == 0, moved, own_imag)
                rows_of_group = slice(group * sources, (group + 1) * sources)
                for half, value in enumerate((own_real, own_imag)):
                    high, low = halves(value)
                    back_high[rows_of_group, columns(half)] = high
                    back_low[rows_of_group, columns(half)] = low
                group += 1

    def back_in_time(rows_of_pair):
        high = back_high[rows_of_pair, :]
        return (
            product(high, inverse_high[...])
            + product(back_low[rows_of_pair, :], inverse_high[...])
            + product(high, inverse_low[...])
        )

    def swapped(value):
        return pltpu.roll(value, SUB // 2, 1)

    def deliver(r, w, restored):
        low = lax.broadcasted_iota(jnp.int32, (sources // SUB, SUB, BLK), 1) < SUB // 2
        pieces = []
        for part in range(2):
            window = restored[part * sources : (part + 1) * sources]
            even = window[:, :BLK].reshape(sources // SUB, SUB, BLK)
            odd = window[:, BLK:].reshape(sources // SUB, SUB, BLK)
            pieces.append(
                (jnp.where(low, even, swapped(odd)), jnp.where(low, swapped(even), odd))
            )
        block, inside = w // parts, w % parts
        for side in range(2):
            both = jnp.concatenate([pieces[0][side], pieces[1][side]], axis=1)
            both = both.astype(jnp.bfloat16)
            for k in range(sources // SUB):
                target = (2 * k + side) * blocks_of_time + block
                out[target, r, inside * SUB : (inside + 2) * SUB, :] = both[k]

    for sweep in range(ITERS):
        update(sweep)
        forward_in_time()
        shrink(sweep)
        back_in_source()
        for group in range(0, groups, 2):
            rows_of_pair = slice(group * sources, (group + 2) * sources)
            restored = back_in_time(rows_of_pair)
            if sweep < ITERS - 1:
                for half in range(2):
                    traces[half, rows_of_pair, :] = bfloat(restored[:, columns(half)])
            else:
                deliver(group // windows, group % windows, restored)


def gathers_of_all_samples(shots, blended, delays, thresholds):
    receivers, own, samples = blended.shape
    blocks_of_time = lax.axis_size("tm")
    count = shots * blocks_of_time
    each = receivers // count
    blocks = samples // BLK
    windows = samples * blocks_of_time // WIN
    groups = each * windows
    rows = blocks * own
    sent = blended.reshape(receivers, own, blocks, BLK).transpose(0, 2, 1, 3)
    sent = sent.astype(jnp.bfloat16).reshape(count, each, rows, BLK)
    received = lax.all_to_all(sent, ("shot", "tm"), split_axis=0, concat_axis=0, tiled=True)
    tables = [jnp.asarray(table) for table in half_spectrum_tables()]
    vmem = pl.BlockSpec(memory_space=pltpu.VMEM)
    held = SRC // shots
    restored = pl.pallas_call(
        functools.partial(gather_kernel, shots),
        out_shape=jax.ShapeDtypeStruct((count, each, blocks * held, BLK), jnp.bfloat16),
        in_specs=[pl.BlockSpec(memory_space=pltpu.SMEM)] + [vmem] * 7,
        out_specs=vmem,
        scratch_shapes=[
            pltpu.VMEM((each, shots, blocks_of_time * rows, BLK), jnp.float32),
            pltpu.VMEM((4 * SRC, (groups + 1) * HALF), jnp.bfloat16),
            pltpu.VMEM((4 * SRC, (groups + 1) * HALF), jnp.bfloat16),
            pltpu.VMEM((groups * SRC, WIN), jnp.bfloat16),
            pltpu.VMEM((groups * SRC, WIN), jnp.bfloat16),
            pltpu.VMEM((2, groups * SRC, BLK), jnp.float32),
        ],
        compiler_params=pltpu.CompilerParams(vmem_limit_bytes=40 * 1024 * 1024),
        cost_estimate=pl.CostEstimate(
            flops=2 * ITERS * groups * SRC * WIN * WIN * 9,
            bytes_accessed=2 * 1024 * 1024,
            transcendentals=ITERS * groups * SRC * HALF,
        ),
    )(delays, thresholds, received, *tables)
    final = lax.all_to_all(restored, ("shot", "tm"), split_axis=0, concat_axis=0, tiled=True)
    final = final.reshape(receivers, blocks, held, BLK).transpose(0, 2, 1, 3)
    return final.reshape(receivers, held, samples)


def shifted(array, axis, by):
    count = lax.axis_size(axis)
    pairs = [(i, i + by) for i in range(count) if 0 <= i + by < count]
    return lax.ppermute(array, axis, pairs)


def phase_table(length_first, length_second, period):
    first_index = jnp.arange(length_first, dtype=jnp.int32)[:, None]
    second_index = jnp.arange(length_second, dtype=jnp.int32)[None, :]
    return (first_index * second_index % period).astype(jnp.float32) * (2.0 * math.pi / period)


def make_tables():
    time_angle = phase_table(WIN, WIN, WIN)
    time_scale = 1.0 / math.sqrt(WIN)
    cos_forward = jnp.cos(time_angle).astype(jnp.bfloat16)
    sin_forward = -jnp.sin(time_angle).astype(jnp.bfloat16)
    cos_inverse = jnp.cos(time_angle) * time_scale
    sin_inverse = -jnp.sin(time_angle) * time_scale
    source_angle = phase_table(SRC, SRC, SRC)
    cos_source = jnp.cos(source_angle) / math.sqrt(SRC)
    sin_source = jnp.sin(source_angle) / math.sqrt(SRC)
    return (cos_forward, sin_forward, cos_inverse, sin_inverse, cos_source, sin_source)


def blend(estimate, own_delays):
    receivers, sources, samples = estimate.shape
    blocks = samples // BLK
    experiments = sources // SRC_EXP
    earlier = shifted(estimate[:, :, samples - BLK :], "tm", 1)
    upper = estimate.reshape(receivers, sources, blocks, BLK)
    shifts = own_delays.reshape(-1)
    row_index = jnp.arange(BLK, dtype=jnp.int32)[None, :, None]
    column_index = jnp.arange(BLK, dtype=jnp.int32)[None, None, :]
    select_same = (row_index == column_index - shifts[:, None, None]).astype(jnp.bfloat16)
    select_prior = (row_index == BLK + column_index - shifts[:, None, None]).astype(jnp.bfloat16)
    same = jnp.einsum("rsnb,sbi->rsni", upper, select_same, preferred_element_type=jnp.float32)
    onward = jnp.einsum("rsnb,sbi->rsni", upper, select_prior, preferred_element_type=jnp.float32)
    edge_part = jnp.einsum(
        "rsb,sbi->rsi", earlier, select_prior, preferred_element_type=jnp.float32
    )
    same = jnp.sum(same.reshape(receivers, experiments, SRC_EXP, blocks, BLK), axis=2)
    onward = jnp.sum(onward.reshape(receivers, experiments, SRC_EXP, blocks, BLK), axis=2)
    edge_part = jnp.sum(edge_part.reshape(receivers, experiments, SRC_EXP, BLK), axis=2)
    carried = jnp.concatenate([edge_part[:, :, None], onward[:, :, : blocks - 1]], axis=2)
    return (same + carried).reshape(receivers, experiments, samples)


def spread(residual, own_delays):
    receivers, experiments, samples = residual.shape
    blocks = samples // BLK
    later = shifted(residual[:, :, :BLK], "tm", -1)
    lower = residual.reshape(receivers, experiments, blocks, BLK)
    row_index = jnp.arange(BLK, dtype=jnp.int32)[None, None, :, None]
    column_index = jnp.arange(BLK, dtype=jnp.int32)[None, None, None, :]
    select_same = (row_index == column_index + own_delays[:, :, None, None]).astype(jnp.bfloat16)
    select_next = (row_index + BLK == column_index + own_delays[:, :, None, None]).astype(
        jnp.bfloat16
    )
    same = jnp.einsum("rena,ekai->rekni", lower, select_same, preferred_element_type=jnp.float32)
    backward = jnp.einsum(
        "rena,ekai->rekni", lower, select_next, preferred_element_type=jnp.float32
    )
    edge_part = jnp.einsum("rea,ekai->reki", later, select_next, preferred_element_type=jnp.float32)
    carried = jnp.concatenate([backward[:, :, :, 1:], edge_part[:, :, :, None]], axis=3)
    return (same + carried).reshape(receivers, experiments * SRC_EXP, samples)


def coherence(gathers, limits, tables):
    cos_forward, sin_forward, cos_inverse, sin_inverse, cos_source, sin_source = tables
    receivers, sources, samples = gathers.shape
    windows = samples // WIN
    careful = lax.Precision.HIGH
    scale = 1.0 / math.sqrt(WIN)
    signal = gathers.reshape(receivers * sources * windows, WIN)
    real_time = (jnp.dot(signal, cos_forward, preferred_element_type=jnp.float32) * scale).reshape(
        receivers, sources, samples
    )
    imag_time = (jnp.dot(signal, sin_forward, preferred_element_type=jnp.float32) * scale).reshape(
        receivers, sources, samples
    )

    def mixing(table, field):
        return jnp.einsum(
            "ps,rsx->rpx", table, field, precision=careful, preferred_element_type=jnp.float32
        )

    real_part = mixing(cos_source, real_time) + mixing(sin_source, imag_time)
    imag_part = mixing(cos_source, imag_time) - mixing(sin_source, real_time)
    magnitude = jnp.sqrt(real_part * real_part + imag_part * imag_part)
    bound = limits[None, :, None]
    factor = jnp.maximum(magnitude - bound, 0.0) / jnp.maximum(magnitude, bound)
    kept_real = real_part * factor
    kept_imag = imag_part * factor
    back_real = mixing(cos_source, kept_real) - mixing(sin_source, kept_imag)
    back_imag = mixing(cos_source, kept_imag) + mixing(sin_source, kept_real)
    restored = jnp.dot(
        back_real.reshape(-1, WIN),
        cos_inverse,
        precision=careful,
        preferred_element_type=jnp.float32,
    )
    restored = restored + jnp.dot(
        back_imag.reshape(-1, WIN),
        sin_inverse,
        precision=careful,
        preferred_element_type=jnp.float32,
    )
    return restored.reshape(receivers, sources, samples)


def gathers_of_own_samples(blended, delays, thresholds):
    tables = make_tables()
    local_count = blended.shape[1]
    own_delays = lax.dynamic_slice_in_dim(
        delays, lax.axis_index("shot") * local_count, local_count, 0
    )
    estimate = None
    for sweep in range(ITERS):
        if sweep == 0:
            residual = blended.astype(jnp.bfloat16)
            update = (RELAX * spread(residual, own_delays)).astype(jnp.bfloat16)
        else:
            residual = (blended - blend(estimate, own_delays)).astype(jnp.bfloat16)
            update = (estimate.astype(jnp.float32) + RELAX * spread(residual, own_delays)).astype(
                jnp.bfloat16
            )
        gathers = lax.all_to_all(update, "shot", split_axis=0, concat_axis=1, tiled=True)
        filtered = coherence(gathers, thresholds[sweep], tables).astype(jnp.bfloat16)
        estimate = lax.all_to_all(filtered, "shot", split_axis=1, concat_axis=0, tiled=True)
    return estimate


def whole_receivers_fit(shots, blocks_of_time, receivers, samples):
    held, windows = SRC // shots, samples // WIN
    return (
        receivers % (shots * blocks_of_time) == 0
        and held * 2 == SUB
        and windows % 2 == 0
        and windows * blocks_of_time == SUB
        and receivers // (shots * blocks_of_time) * SUB <= HALF
    )


def local(blended, delays, thresholds):
    shots, blocks_of_time = lax.axis_size("shot"), lax.axis_size("tm")
    if whole_receivers_fit(shots, blocks_of_time, blended.shape[0], blended.shape[2]):
        return gathers_of_all_samples(shots, blended, delays, thresholds)
    return gathers_of_own_samples(blended, delays, thresholds)


def solution(mesh):
    return jax.shard_map(
        local,
        mesh=mesh,
        in_specs=(P(None, "shot", "tm"), P(), P()),
        out_specs=P(None, "shot", "tm"),
        check_vma=False,
    )
```

```python
import functools
import math

import jax
import jax.numpy as jnp
import ml_dtypes
import numpy as np
from jax import lax
from jax.experimental import pallas as pl
from jax.experimental.pallas import tpu as pltpu
from jax.sharding import PartitionSpec as P

SRC = 64
SRC_EXP = 2
WIN = 256
BLK = 128
ITERS = 2


RELAX = 0.5
HALF = WIN // 2
SUB = 8
SPAN = 4


def split_table(table):
    high = table.astype(ml_dtypes.bfloat16)
    low = (table - high.astype(np.float64)).astype(ml_dtypes.bfloat16)
    return high, low


def half_spectrum_tables():
    moment = np.arange(WIN)
    angle = (moment[:, None] * np.arange(HALF)[None, :] % WIN) * (2.0 * math.pi / WIN)
    nyquist = np.where(moment % 2 == 0, 1.0, -1.0)
    sine = -np.sin(angle)
    sine[:, 0] = nyquist
    forward = np.concatenate([np.cos(angle), sine], axis=1).astype(ml_dtypes.bfloat16)
    inverse = np.concatenate([np.cos(angle), sine], axis=1).T / math.sqrt(WIN)
    inverse[0] *= 0.5
    inverse[HALF] *= 0.5
    source = np.arange(SRC)
    turn = (source[:, None] * source[None, :] % SRC) * (2.0 * math.pi / SRC)
    cosine, sine = np.cos(turn) / math.sqrt(SRC), np.sin(turn) / math.sqrt(SRC)
    onward = np.block([[cosine, sine], [-sine, cosine]])
    pair = []
    for table in (onward / math.sqrt(WIN), onward.T):
        high, low = split_table(table)
        pair.append(np.block([[high, high], [low, low]]))
    return (forward, *split_table(inverse), *pair)


def halves(value):
    high = value.astype(jnp.bfloat16)
    return high, (value - high.astype(jnp.float32)).astype(jnp.bfloat16)


def bfloat(value):
    return value.astype(jnp.bfloat16).astype(jnp.float32)


def product(left, right):
    return jnp.dot(left, right, preferred_element_type=jnp.float32)


def gather_kernel(
    shots,
    delays,
    limits,
    received,
    forward,
    inverse_high,
    inverse_low,
    onward,
    backward,
    out,
    records,
    field,
    mixed,
    back_high,
    back_low,
    traces,
):
    count, receivers, rows, _ = received.shape
    blocks_of_time = count // shots
    experiments, sources = delays.shape[0], SRC
    own = experiments // shots
    windows = records.shape[2] // (2 * own)
    groups = receivers * windows
    parts = windows // blocks_of_time
    lane = lax.broadcasted_iota(jnp.int32, (windows, BLK), 1)
    row = lax.broadcasted_iota(jnp.int32, (windows, BLK), 0)
    lane_of_group = lax.broadcasted_iota(jnp.int32, (sources, HALF), 1)

    for shot in range(shots):
        for block in range(blocks_of_time):
            arrived = received[shot * blocks_of_time + block].astype(jnp.float32)
            for r in range(receivers):
                records[r, shot, block * rows : (block + 1) * rows, :] = arrived[r]

    def record(r, shot, e):
        return tuple(
            records[r, shot, pl.ds(half * own + e, windows, stride=2 * own), :]
            for half in range(2)
        )

    def trace_rows(r, s):
        return pl.ds(r * windows * sources + s, windows, stride=sources)

    def load(r, s):
        return tuple(traces[half, trace_rows(r, s), :] for half in range(2))

    def store(r, s, values):
        for half in range(2):
            traces[half, trace_rows(r, s), :] = values[half]

    def advanced(even, odd, delay):
        by = (BLK - delay) & (BLK - 1)
        even, odd = pltpu.roll(even, by, 1), pltpu.roll(odd, by, 1)
        after = jnp.where(row < windows - 1, pltpu.roll(even, windows - 1, 0), 0.0)
        same = lane < BLK - delay
        return jnp.where(same, even, odd), jnp.where(same, odd, after)

    def delayed(even, odd, delay):
        even, odd = pltpu.roll(even, delay, 1), pltpu.roll(odd, delay, 1)
        before = jnp.where(row > 0, pltpu.roll(odd, 1, 0), 0.0)
        same = lane >= delay
        return jnp.where(same, even, before), jnp.where(same, odd, even)

    def update(sweep):
        for experiment in range(experiments):
            shot, e = experiment // own, experiment % own
            first = experiment * SRC_EXP
            lags = [delays[experiment, k] for k in range(SRC_EXP)]
            for r in range(receivers):
                even, odd = record(r, shot, e)
                if sweep > 0:
                    estimate = [load(r, first + k) for k in range(SRC_EXP)]
                    late = [delayed(*estimate[k], lags[k]) for k in range(SRC_EXP)]
                    even = bfloat(even - sum(x[0] for x in late))
                    odd = bfloat(odd - sum(x[1] for x in late))
                for k in range(SRC_EXP):
                    values = [RELAX * x for x in advanced(even, odd, lags[k])]
                    if sweep > 0:
                        values = [a + b for a, b in zip(estimate[k], values)]
                    store(r, first + k, values)

    def columns(group, many=1):
        return slice(group * HALF, (group + many) * HALF)

    def forward_in_time():
        nyquist = jnp.zeros((sources, HALF), jnp.float32)
        for group in range(groups):
            if group % SPAN == 0:
                rows_of_span = slice(group * sources, (group + SPAN) * sources)
                signal = jnp.concatenate(
                    [traces[half, rows_of_span, :].astype(jnp.bfloat16) for half in range(2)],
                    axis=1,
                )
                spectra = product(signal, forward[...])
            spectrum = spectra[group % SPAN * sources : (group % SPAN + 1) * sources]
            real, imag = spectrum[:, :HALF], spectrum[:, HALF:]
            moved = pltpu.roll(imag, group, 1) if group else imag
            nyquist = jnp.where(lane_of_group == group, moved, nyquist)
            imag = jnp.where(lane_of_group == 0, 0.0, imag)
            put(field, columns(group), real, imag)
        put(field, columns(groups), nyquist, jnp.zeros_like(nyquist))

    def put(ref, where, real, imag):
        real_high, real_low = halves(real)
        imag_high, imag_low = halves(imag)
        for at, value in enumerate((real_high, imag_high, real_low, imag_low)):
            ref[at * sources : (at + 1) * sources, where] = value

    def chunks():
        yield columns(groups)
        for group in range(0, groups, 2):
            yield columns(group, 2)

    def mixing(table, ref, where):
        both = product(table[...], ref[:, where])
        total = both[: 2 * sources] + both[2 * sources :]
        return total[:sources], total[sources:]

    def shrink(sweep):
        limit = limits[sweep : sweep + 1, :]
        p = lax.broadcasted_iota(jnp.int32, (sources, sources), 0)
        q = lax.broadcasted_iota(jnp.int32, (sources, sources), 1)
        bound = jnp.sum(jnp.where(p == q, limit, 0.0), axis=1, keepdims=True)
        mirrored = (p + q == 0) | (p + q == sources)
        bound_mirrored = jnp.sum(jnp.where(mirrored, limit, 0.0), axis=1, keepdims=True)
        for where in chunks():
            real, imag = mixing(onward, field, where)
            inverse_size = lax.rsqrt(real * real + imag * imag)
            factor = jnp.maximum(1.0 - bound * inverse_size, 0.0) + jnp.maximum(
                1.0 - bound_mirrored * inverse_size, 0.0
            )
            put(mixed, where, real * factor, imag * factor)

    def back_in_source():
        nyquist = None
        group = 0
        for where in chunks():
            real, imag = mixing(backward, mixed, where)
            if nyquist is None:
                nyquist = real
                continue
            for part in range(2):
                own_real, own_imag = real[:, columns(part)], imag[:, columns(part)]
                moved = pltpu.roll(nyquist, HALF - group, 1) if group else nyquist
                own_imag = jnp.where(lane_of_group == 0, moved, own_imag)
                rows_of_group = slice(group * sources, (group + 1) * sources)
                for half, value in enumerate((own_real, own_imag)):
                    high, low = halves(value)
                    back_high[rows_of_group, columns(half)] = high
                    back_low[rows_of_group, columns(half)] = low
                group += 1

    def back_in_time(rows_of_span):
        high = back_high[rows_of_span, :]
        return (
            product(high, inverse_high[...])
            + product(back_low[rows_of_span, :], inverse_high[...])
            + product(high, inverse_low[...])
        )

    def swapped(value):
        return pltpu.roll(value, SUB // 2, 1)

    def deliver(r, w, restored):
        low = lax.broadcasted_iota(jnp.int32, (sources // SUB, SUB, BLK), 1) < SUB // 2
        pieces = []
        for part in range(2):
            window = restored[part * sources : (part + 1) * sources]
            even = window[:, :BLK].reshape(sources // SUB, SUB, BLK)
            odd = window[:, BLK:].reshape(sources // SUB, SUB, BLK)
            pieces.append(
                (jnp.where(low, even, swapped(odd)), jnp.where(low, swapped(even), odd))
            )
        block, inside = w // parts, w % parts
        for side in range(2):
            both = jnp.concatenate([pieces[0][side], pieces[1][side]], axis=1)
            both = both.astype(jnp.bfloat16)
            for k in range(sources // SUB):
                target = (2 * k + side) * blocks_of_time + block
                out[target, r, inside * SUB : (inside + 2) * SUB, :] = both[k]

    for sweep in range(ITERS):
        update(sweep)
        forward_in_time()
        shrink(sweep)
        back_in_source()
        for start in range(0, groups, SPAN):
            rows_of_span = slice(start * sources, (start + SPAN) * sources)
            restored = back_in_time(rows_of_span)
            if sweep < ITERS - 1:
                for half in range(2):
                    traces[half, rows_of_span, :] = bfloat(restored[:, columns(half)])
                continue
            for group in range(0, SPAN, 2):
                pair = restored[group * sources : (group + 2) * sources]
                deliver((start + group) // windows, (start + group) % windows, pair)


def gathers_of_all_samples(shots, blended, delays, thresholds):
    receivers, own, samples = blended.shape
    blocks_of_time = lax.axis_size("tm")
    count = shots * blocks_of_time
    each = receivers // count
    blocks = samples // BLK
    windows = samples * blocks_of_time // WIN
    groups = each * windows
    rows = blocks * own
    sent = blended.reshape(receivers, own, blocks, BLK).transpose(0, 2, 1, 3)
    sent = lax.optimization_barrier(sent.reshape(count, each, rows, BLK)).astype(jnp.bfloat16)
    received = lax.all_to_all(sent, ("shot", "tm"), split_axis=0, concat_axis=0, tiled=True)
    tables = [jnp.asarray(table) for table in half_spectrum_tables()]
    vmem = pl.BlockSpec(memory_space=pltpu.VMEM)
    held = SRC // shots
    restored = pl.pallas_call(
        functools.partial(gather_kernel, shots),
        out_shape=jax.ShapeDtypeStruct((count, each, blocks * held, BLK), jnp.bfloat16),
        in_specs=[pl.BlockSpec(memory_space=pltpu.SMEM)] + [vmem] * 7,
        out_specs=vmem,
        scratch_shapes=[
            pltpu.VMEM((each, shots, blocks_of_time * rows, BLK), jnp.float32),
            pltpu.VMEM((4 * SRC, (groups + 1) * HALF), jnp.bfloat16),
            pltpu.VMEM((4 * SRC, (groups + 1) * HALF), jnp.bfloat16),
            pltpu.VMEM((groups * SRC, WIN), jnp.bfloat16),
            pltpu.VMEM((groups * SRC, WIN), jnp.bfloat16),
            pltpu.VMEM((2, groups * SRC, BLK), jnp.float32),
        ],
        compiler_params=pltpu.CompilerParams(vmem_limit_bytes=40 * 1024 * 1024),
        cost_estimate=pl.CostEstimate(
            flops=2 * ITERS * groups * SRC * WIN * WIN * 9,
            bytes_accessed=2 * 1024 * 1024,
            transcendentals=ITERS * groups * SRC * HALF,
        ),
    )(delays, thresholds, received, *tables)
    final = lax.all_to_all(restored, ("shot", "tm"), split_axis=0, concat_axis=0, tiled=True)
    final = final.reshape(receivers, blocks, held, BLK).transpose(0, 2, 1, 3)
    return final.reshape(receivers, held, samples)


def shifted(array, axis, by):
    count = lax.axis_size(axis)
    pairs = [(i, i + by) for i in range(count) if 0 <= i + by < count]
    return lax.ppermute(array, axis, pairs)


def phase_table(length_first, length_second, period):
    first_index = jnp.arange(length_first, dtype=jnp.int32)[:, None]
    second_index = jnp.arange(length_second, dtype=jnp.int32)[None, :]
    return (first_index * second_index % period).astype(jnp.float32) * (2.0 * math.pi / period)


def make_tables():
    time_angle = phase_table(WIN, WIN, WIN)
    time_scale = 1.0 / math.sqrt(WIN)
    cos_forward = jnp.cos(time_angle).astype(jnp.bfloat16)
    sin_forward = -jnp.sin(time_angle).astype(jnp.bfloat16)
    cos_inverse = jnp.cos(time_angle) * time_scale
    sin_inverse = -jnp.sin(time_angle) * time_scale
    source_angle = phase_table(SRC, SRC, SRC)
    cos_source = jnp.cos(source_angle) / math.sqrt(SRC)
    sin_source = jnp.sin(source_angle) / math.sqrt(SRC)
    return (cos_forward, sin_forward, cos_inverse, sin_inverse, cos_source, sin_source)


def blend(estimate, own_delays):
    receivers, sources, samples = estimate.shape
    blocks = samples // BLK
    experiments = sources // SRC_EXP
    earlier = shifted(estimate[:, :, samples - BLK :], "tm", 1)
    upper = estimate.reshape(receivers, sources, blocks, BLK)
    shifts = own_delays.reshape(-1)
    row_index = jnp.arange(BLK, dtype=jnp.int32)[None, :, None]
    column_index = jnp.arange(BLK, dtype=jnp.int32)[None, None, :]
    select_same = (row_index == column_index - shifts[:, None, None]).astype(jnp.bfloat16)
    select_prior = (row_index == BLK + column_index - shifts[:, None, None]).astype(jnp.bfloat16)
    same = jnp.einsum("rsnb,sbi->rsni", upper, select_same, preferred_element_type=jnp.float32)
    onward = jnp.einsum("rsnb,sbi->rsni", upper, select_prior, preferred_element_type=jnp.float32)
    edge_part = jnp.einsum(
        "rsb,sbi->rsi", earlier, select_prior, preferred_element_type=jnp.float32
    )
    same = jnp.sum(same.reshape(receivers, experiments, SRC_EXP, blocks, BLK), axis=2)
    onward = jnp.sum(onward.reshape(receivers, experiments, SRC_EXP, blocks, BLK), axis=2)
    edge_part = jnp.sum(edge_part.reshape(receivers, experiments, SRC_EXP, BLK), axis=2)
    carried = jnp.concatenate([edge_part[:, :, None], onward[:, :, : blocks - 1]], axis=2)
    return (same + carried).reshape(receivers, experiments, samples)


def spread(residual, own_delays):
    receivers, experiments, samples = residual.shape
    blocks = samples // BLK
    later = shifted(residual[:, :, :BLK], "tm", -1)
    lower = residual.reshape(receivers, experiments, blocks, BLK)
    row_index = jnp.arange(BLK, dtype=jnp.int32)[None, None, :, None]
    column_index = jnp.arange(BLK, dtype=jnp.int32)[None, None, None, :]
    select_same = (row_index == column_index + own_delays[:, :, None, None]).astype(jnp.bfloat16)
    select_next = (row_index + BLK == column_index + own_delays[:, :, None, None]).astype(
        jnp.bfloat16
    )
    same = jnp.einsum("rena,ekai->rekni", lower, select_same, preferred_element_type=jnp.float32)
    backward = jnp.einsum(
        "rena,ekai->rekni", lower, select_next, preferred_element_type=jnp.float32
    )
    edge_part = jnp.einsum("rea,ekai->reki", later, select_next, preferred_element_type=jnp.float32)
    carried = jnp.concatenate([backward[:, :, :, 1:], edge_part[:, :, :, None]], axis=3)
    return (same + carried).reshape(receivers, experiments * SRC_EXP, samples)


def coherence(gathers, limits, tables):
    cos_forward, sin_forward, cos_inverse, sin_inverse, cos_source, sin_source = tables
    receivers, sources, samples = gathers.shape
    windows = samples // WIN
    careful = lax.Precision.HIGH
    scale = 1.0 / math.sqrt(WIN)
    signal = gathers.reshape(receivers * sources * windows, WIN)
    real_time = (jnp.dot(signal, cos_forward, preferred_element_type=jnp.float32) * scale).reshape(
        receivers, sources, samples
    )
    imag_time = (jnp.dot(signal, sin_forward, preferred_element_type=jnp.float32) * scale).reshape(
        receivers, sources, samples
    )

    def mixing(table, field):
        return jnp.einsum(
            "ps,rsx->rpx", table, field, precision=careful, preferred_element_type=jnp.float32
        )

    real_part = mixing(cos_source, real_time) + mixing(sin_source, imag_time)
    imag_part = mixing(cos_source, imag_time) - mixing(sin_source, real_time)
    magnitude = jnp.sqrt(real_part * real_part + imag_part * imag_part)
    bound = limits[None, :, None]
    factor = jnp.maximum(magnitude - bound, 0.0) / jnp.maximum(magnitude, bound)
    kept_real = real_part * factor
    kept_imag = imag_part * factor
    back_real = mixing(cos_source, kept_real) - mixing(sin_source, kept_imag)
    back_imag = mixing(cos_source, kept_imag) + mixing(sin_source, kept_real)
    restored = jnp.dot(
        back_real.reshape(-1, WIN),
        cos_inverse,
        precision=careful,
        preferred_element_type=jnp.float32,
    )
    restored = restored + jnp.dot(
        back_imag.reshape(-1, WIN),
        sin_inverse,
        precision=careful,
        preferred_element_type=jnp.float32,
    )
    return restored.reshape(receivers, sources, samples)


def gathers_of_own_samples(blended, delays, thresholds):
    tables = make_tables()
    local_count = blended.shape[1]
    own_delays = lax.dynamic_slice_in_dim(
        delays, lax.axis_index("shot") * local_count, local_count, 0
    )
    estimate = None
    for sweep in range(ITERS):
        if sweep == 0:
            residual = blended.astype(jnp.bfloat16)
            update = (RELAX * spread(residual, own_delays)).astype(jnp.bfloat16)
        else:
            residual = (blended - blend(estimate, own_delays)).astype(jnp.bfloat16)
            update = (estimate.astype(jnp.float32) + RELAX * spread(residual, own_delays)).astype(
                jnp.bfloat16
            )
        gathers = lax.all_to_all(update, "shot", split_axis=0, concat_axis=1, tiled=True)
        filtered = coherence(gathers, thresholds[sweep], tables).astype(jnp.bfloat16)
        estimate = lax.all_to_all(filtered, "shot", split_axis=1, concat_axis=0, tiled=True)
    return estimate


def whole_receivers_fit(shots, blocks_of_time, receivers, samples):
    held, windows = SRC // shots, samples // WIN
    return (
        receivers % (shots * blocks_of_time) == 0
        and held * 2 == SUB
        and windows % 2 == 0
        and windows * blocks_of_time == SUB
        and receivers // (shots * blocks_of_time) * SUB <= HALF
    )


def local(blended, delays, thresholds):
    shots, blocks_of_time = lax.axis_size("shot"), lax.axis_size("tm")
    if whole_receivers_fit(shots, blocks_of_time, blended.shape[0], blended.shape[2]):
        return gathers_of_all_samples(shots, blended, delays, thresholds)
    return gathers_of_own_samples(blended, delays, thresholds)


def solution(mesh):
    return jax.shard_map(
        local,
        mesh=mesh,
        in_specs=(P(None, "shot", "tm"), P(), P()),
        out_specs=P(None, "shot", "tm"),
        check_vma=False,
    )
```

```python
import functools
import math

import jax
import jax.numpy as jnp
import ml_dtypes
import numpy as np
from jax import lax
from jax.experimental import pallas as pl
from jax.experimental.pallas import tpu as pltpu
from jax.sharding import PartitionSpec as P

SRC = 64
SRC_EXP = 2
WIN = 256
BLK = 128
ITERS = 2


RELAX = 0.5
HALF = WIN // 2
SUB = 8
SPAN = 4


def split_table(table):
    high = table.astype(ml_dtypes.bfloat16)
    low = (table - high.astype(np.float64)).astype(ml_dtypes.bfloat16)
    return high, low


def half_spectrum_tables():
    moment = np.arange(WIN)
    angle = (moment[:, None] * np.arange(HALF)[None, :] % WIN) * (2.0 * math.pi / WIN)
    nyquist = np.where(moment % 2 == 0, 1.0, -1.0)
    sine = -np.sin(angle)
    sine[:, 0] = nyquist
    forward = np.concatenate([np.cos(angle), sine], axis=1).astype(ml_dtypes.bfloat16)
    inverse = np.concatenate([np.cos(angle), sine], axis=1).T / math.sqrt(WIN)
    inverse[0] *= 0.5
    inverse[HALF] *= 0.5
    source = np.arange(SRC)
    turn = (source[:, None] * source[None, :] % SRC) * (2.0 * math.pi / SRC)
    cosine, sine = np.cos(turn) / math.sqrt(SRC), np.sin(turn) / math.sqrt(SRC)
    onward = np.block([[cosine, sine], [-sine, cosine]])
    pair = []
    for table in (onward / math.sqrt(WIN), onward.T):
        high, low = split_table(table)
        pair.append(np.block([[high, high], [low, low]]))
    return (forward, *split_table(inverse), *pair)


def halves(value):
    high = value.astype(jnp.bfloat16)
    return high, (value - high.astype(jnp.float32)).astype(jnp.bfloat16)


def bfloat(value):
    return value.astype(jnp.bfloat16).astype(jnp.float32)


def product(left, right):
    return jnp.dot(left, right, preferred_element_type=jnp.float32)


def gather_kernel(
    shots,
    delays,
    limits,
    received,
    forward,
    inverse_high,
    inverse_low,
    onward,
    backward,
    out,
    records,
    field,
    mixed,
    back_high,
    back_low,
    traces,
):
    count, receivers, rows, _ = received.shape
    blocks_of_time = count // shots
    experiments, sources = delays.shape[0], SRC
    own = experiments // shots
    windows = records.shape[2] // (2 * own)
    groups = receivers * windows
    parts = windows // blocks_of_time
    lane = lax.broadcasted_iota(jnp.int32, (windows, BLK), 1)
    row = lax.broadcasted_iota(jnp.int32, (windows, BLK), 0)
    lane_of_group = lax.broadcasted_iota(jnp.int32, (sources, HALF), 1)

    for shot in range(shots):
        for block in range(blocks_of_time):
            arrived = received[shot * blocks_of_time + block].astype(jnp.float32)
            for r in range(receivers):
                records[r, shot, block * rows : (block + 1) * rows, :] = arrived[r]

    def record(r, shot, e):
        return tuple(
            records[r, shot, pl.ds(half * own + e, windows, stride=2 * own), :]
            for half in range(2)
        )

    def trace_rows(r, s):
        return pl.ds(r * windows * sources + s, windows, stride=sources)

    def load(r, s):
        return tuple(traces[half, trace_rows(r, s), :] for half in range(2))

    def store(r, s, values):
        for half in range(2):
            traces[half, trace_rows(r, s), :] = values[half]

    def advanced(even, odd, delay):
        by = (BLK - delay) & (BLK - 1)
        even, odd = pltpu.roll(even, by, 1), pltpu.roll(odd, by, 1)
        after = jnp.where(row < windows - 1, pltpu.roll(even, windows - 1, 0), 0.0)
        same = lane < BLK - delay
        return jnp.where(same, even, odd), jnp.where(same, odd, after)

    def delayed(even, odd, delay):
        even, odd = pltpu.roll(even, delay, 1), pltpu.roll(odd, delay, 1)
        before = jnp.where(row > 0, pltpu.roll(odd, 1, 0), 0.0)
        same = lane >= delay
        return jnp.where(same, even, before), jnp.where(same, odd, even)

    def update(sweep):
        for experiment in range(experiments):
            shot, e = experiment // own, experiment % own
            first = experiment * SRC_EXP
            lags = [delays[experiment, k] for k in range(SRC_EXP)]
            for r in range(receivers):
                even, odd = record(r, shot, e)
                if sweep > 0:
                    estimate = [load(r, first + k) for k in range(SRC_EXP)]
                    late = [delayed(*estimate[k], lags[k]) for k in range(SRC_EXP)]
                    even = bfloat(even - sum(x[0] for x in late))
                    odd = bfloat(odd - sum(x[1] for x in late))
                for k in range(SRC_EXP):
                    values = [RELAX * x for x in advanced(even, odd, lags[k])]
                    if sweep > 0:
                        values = [a + b for a, b in zip(estimate[k], values)]
                    store(r, first + k, values)

    def columns(group, many=1):
        return slice(group * HALF, (group + many) * HALF)

    def forward_in_time():
        nyquist = jnp.zeros((sources, HALF), jnp.float32)
        for group in range(groups):
            if group % SPAN == 0:
                rows_of_span = slice(group * sources, (group + SPAN) * sources)
                signal = jnp.concatenate(
                    [traces[half, rows_of_span, :].astype(jnp.bfloat16) for half in range(2)],
                    axis=1,
                )
                spectra = product(signal, forward[...])
            spectrum = spectra[group % SPAN * sources : (group % SPAN + 1) * sources]
            real, imag = spectrum[:, :HALF], spectrum[:, HALF:]
            moved = pltpu.roll(imag, group, 1) if group else imag
            nyquist = jnp.where(lane_of_group == group, moved, nyquist)
            imag = jnp.where(lane_of_group == 0, 0.0, imag)
            put(field, columns(group), real, imag)
        put(field, columns(groups), nyquist, jnp.zeros_like(nyquist))

    def put(ref, where, real, imag):
        real_high, real_low = halves(real)
        imag_high, imag_low = halves(imag)
        for at, value in enumerate((real_high, imag_high, real_low, imag_low)):
            ref[at * sources : (at + 1) * sources, where] = value

    def chunks():
        yield columns(groups)
        for group in range(0, groups, 2):
            yield columns(group, 2)

    def mixing(table, ref, where):
        both = product(table[...], ref[:, where])
        total = both[: 2 * sources] + both[2 * sources :]
        return total[:sources], total[sources:]

    def shrink(sweep):
        limit = limits[sweep : sweep + 1, :]
        p = lax.broadcasted_iota(jnp.int32, (sources, sources), 0)
        q = lax.broadcasted_iota(jnp.int32, (sources, sources), 1)
        bound = jnp.sum(jnp.where(p == q, limit, 0.0), axis=1, keepdims=True)
        mirrored = (p + q == 0) | (p + q == sources)
        bound_mirrored = jnp.sum(jnp.where(mirrored, limit, 0.0), axis=1, keepdims=True)
        for where in chunks():
            real, imag = mixing(onward, field, where)
            inverse_size = lax.rsqrt(real * real + imag * imag)
            factor = jnp.maximum(1.0 - bound * inverse_size, 0.0) + jnp.maximum(
                1.0 - bound_mirrored * inverse_size, 0.0
            )
            put(mixed, where, real * factor, imag * factor)

    def back_in_source():
        nyquist = None
        group = 0
        for where in chunks():
            real, imag = mixing(backward, mixed, where)
            if nyquist is None:
                nyquist = real
                continue
            for part in range(2):
                own_real, own_imag = real[:, columns(part)], imag[:, columns(part)]
                moved = pltpu.roll(nyquist, HALF - group, 1) if group else nyquist
                own_imag = jnp.where(lane_of_group == 0, moved, own_imag)
                rows_of_group = slice(group * sources, (group + 1) * sources)
                for half, value in enumerate((own_real, own_imag)):
                    high, low = halves(value)
                    back_high[rows_of_group, columns(half)] = high
                    back_low[rows_of_group, columns(half)] = low
                group += 1

    def back_in_time(rows_of_span):
        high = back_high[rows_of_span, :]
        return (
            product(high, inverse_high[...])
            + product(back_low[rows_of_span, :], inverse_high[...])
            + product(high, inverse_low[...])
        )

    def swapped(value):
        return pltpu.roll(value, SUB // 2, 1)

    def deliver(r, w, restored):
        low = lax.broadcasted_iota(jnp.int32, (sources // SUB, SUB, BLK), 1) < SUB // 2
        pieces = []
        for part in range(2):
            window = restored[part * sources : (part + 1) * sources]
            even = window[:, :BLK].reshape(sources // SUB, SUB, BLK)
            odd = window[:, BLK:].reshape(sources // SUB, SUB, BLK)
            pieces.append(
                (jnp.where(low, even, swapped(odd)), jnp.where(low, swapped(even), odd))
            )
        block, inside = w // parts, w % parts
        for side in range(2):
            both = jnp.concatenate([pieces[0][side], pieces[1][side]], axis=1)
            both = both.astype(jnp.bfloat16)
            for k in range(sources // SUB):
                target = (2 * k + side) * blocks_of_time + block
                out[target, r, inside * SUB : (inside + 2) * SUB, :] = both[k]

    for sweep in range(ITERS):
        update(sweep)
        forward_in_time()
        shrink(sweep)
        back_in_source()
        for start in range(0, groups, SPAN):
            rows_of_span = slice(start * sources, (start + SPAN) * sources)
            restored = back_in_time(rows_of_span)
            if sweep < ITERS - 1:
                for half in range(2):
                    traces[half, rows_of_span, :] = bfloat(restored[:, columns(half)])
                continue
            for group in range(0, SPAN, 2):
                pair = restored[group * sources : (group + 2) * sources]
                deliver((start + group) // windows, (start + group) % windows, pair)


def gathers_of_all_samples(shots, blended, delays, thresholds):
    receivers, own, samples = blended.shape
    blocks_of_time = lax.axis_size("tm")
    count = shots * blocks_of_time
    each = receivers // count
    blocks = samples // BLK
    windows = samples * blocks_of_time // WIN
    rows = blocks * own
    sent = blended.reshape(receivers, own, blocks, BLK).transpose(0, 2, 1, 3)
    sent = lax.optimization_barrier(sent.reshape(each, count, rows, BLK))

    def exchanged(array):
        return lax.all_to_all(array, ("shot", "tm"), split_axis=0, concat_axis=0, tiled=True)

    tables = [jnp.asarray(table) for table in half_spectrum_tables()]
    vmem = pl.BlockSpec(memory_space=pltpu.VMEM)
    held = SRC // shots
    filtered = pl.pallas_call(
        functools.partial(gather_kernel, shots),
        out_shape=jax.ShapeDtypeStruct((count, 1, blocks * held, BLK), jnp.bfloat16),
        in_specs=[pl.BlockSpec(memory_space=pltpu.SMEM)] + [vmem] * 7,
        out_specs=vmem,
        scratch_shapes=[
            pltpu.VMEM((1, shots, blocks_of_time * rows, BLK), jnp.float32),
            pltpu.VMEM((4 * SRC, (windows + 1) * HALF), jnp.bfloat16),
            pltpu.VMEM((4 * SRC, (windows + 1) * HALF), jnp.bfloat16),
            pltpu.VMEM((windows * SRC, WIN), jnp.bfloat16),
            pltpu.VMEM((windows * SRC, WIN), jnp.bfloat16),
            pltpu.VMEM((2, windows * SRC, BLK), jnp.float32),
        ],
        compiler_params=pltpu.CompilerParams(vmem_limit_bytes=24 * 1024 * 1024),
        cost_estimate=pl.CostEstimate(
            flops=2 * ITERS * windows * SRC * WIN * WIN * 9,
            bytes_accessed=2 * 1024 * 1024,
            transcendentals=ITERS * windows * SRC * HALF,
        ),
    )
    received = [exchanged(sent[half].astype(jnp.bfloat16)) for half in range(each)]
    restored = [
        exchanged(filtered(delays, thresholds, part[:, None], *tables)) for part in received
    ]
    final = jnp.concatenate(restored, axis=0)
    final = final.reshape(receivers, blocks, held, BLK).transpose(0, 2, 1, 3)
    return final.reshape(receivers, held, samples)


def shifted(array, axis, by):
    count = lax.axis_size(axis)
    pairs = [(i, i + by) for i in range(count) if 0 <= i + by < count]
    return lax.ppermute(array, axis, pairs)


def phase_table(length_first, length_second, period):
    first_index = jnp.arange(length_first, dtype=jnp.int32)[:, None]
    second_index = jnp.arange(length_second, dtype=jnp.int32)[None, :]
    return (first_index * second_index % period).astype(jnp.float32) * (2.0 * math.pi / period)


def make_tables():
    time_angle = phase_table(WIN, WIN, WIN)
    time_scale = 1.0 / math.sqrt(WIN)
    cos_forward = jnp.cos(time_angle).astype(jnp.bfloat16)
    sin_forward = -jnp.sin(time_angle).astype(jnp.bfloat16)
    cos_inverse = jnp.cos(time_angle) * time_scale
    sin_inverse = -jnp.sin(time_angle) * time_scale
    source_angle = phase_table(SRC, SRC, SRC)
    cos_source = jnp.cos(source_angle) / math.sqrt(SRC)
    sin_source = jnp.sin(source_angle) / math.sqrt(SRC)
    return (cos_forward, sin_forward, cos_inverse, sin_inverse, cos_source, sin_source)


def blend(estimate, own_delays):
    receivers, sources, samples = estimate.shape
    blocks = samples // BLK
    experiments = sources // SRC_EXP
    earlier = shifted(estimate[:, :, samples - BLK :], "tm", 1)
    upper = estimate.reshape(receivers, sources, blocks, BLK)
    shifts = own_delays.reshape(-1)
    row_index = jnp.arange(BLK, dtype=jnp.int32)[None, :, None]
    column_index = jnp.arange(BLK, dtype=jnp.int32)[None, None, :]
    select_same = (row_index == column_index - shifts[:, None, None]).astype(jnp.bfloat16)
    select_prior = (row_index == BLK + column_index - shifts[:, None, None]).astype(jnp.bfloat16)
    same = jnp.einsum("rsnb,sbi->rsni", upper, select_same, preferred_element_type=jnp.float32)
    onward = jnp.einsum("rsnb,sbi->rsni", upper, select_prior, preferred_element_type=jnp.float32)
    edge_part = jnp.einsum(
        "rsb,sbi->rsi", earlier, select_prior, preferred_element_type=jnp.float32
    )
    same = jnp.sum(same.reshape(receivers, experiments, SRC_EXP, blocks, BLK), axis=2)
    onward = jnp.sum(onward.reshape(receivers, experiments, SRC_EXP, blocks, BLK), axis=2)
    edge_part = jnp.sum(edge_part.reshape(receivers, experiments, SRC_EXP, BLK), axis=2)
    carried = jnp.concatenate([edge_part[:, :, None], onward[:, :, : blocks - 1]], axis=2)
    return (same + carried).reshape(receivers, experiments, samples)


def spread(residual, own_delays):
    receivers, experiments, samples = residual.shape
    blocks = samples // BLK
    later = shifted(residual[:, :, :BLK], "tm", -1)
    lower = residual.reshape(receivers, experiments, blocks, BLK)
    row_index = jnp.arange(BLK, dtype=jnp.int32)[None, None, :, None]
    column_index = jnp.arange(BLK, dtype=jnp.int32)[None, None, None, :]
    select_same = (row_index == column_index + own_delays[:, :, None, None]).astype(jnp.bfloat16)
    select_next = (row_index + BLK == column_index + own_delays[:, :, None, None]).astype(
        jnp.bfloat16
    )
    same = jnp.einsum("rena,ekai->rekni", lower, select_same, preferred_element_type=jnp.float32)
    backward = jnp.einsum(
        "rena,ekai->rekni", lower, select_next, preferred_element_type=jnp.float32
    )
    edge_part = jnp.einsum("rea,ekai->reki", later, select_next, preferred_element_type=jnp.float32)
    carried = jnp.concatenate([backward[:, :, :, 1:], edge_part[:, :, :, None]], axis=3)
    return (same + carried).reshape(receivers, experiments * SRC_EXP, samples)


def coherence(gathers, limits, tables):
    cos_forward, sin_forward, cos_inverse, sin_inverse, cos_source, sin_source = tables
    receivers, sources, samples = gathers.shape
    windows = samples // WIN
    careful = lax.Precision.HIGH
    scale = 1.0 / math.sqrt(WIN)
    signal = gathers.reshape(receivers * sources * windows, WIN)
    real_time = (jnp.dot(signal, cos_forward, preferred_element_type=jnp.float32) * scale).reshape(
        receivers, sources, samples
    )
    imag_time = (jnp.dot(signal, sin_forward, preferred_element_type=jnp.float32) * scale).reshape(
        receivers, sources, samples
    )

    def mixing(table, field):
        return jnp.einsum(
            "ps,rsx->rpx", table, field, precision=careful, preferred_element_type=jnp.float32
        )

    real_part = mixing(cos_source, real_time) + mixing(sin_source, imag_time)
    imag_part = mixing(cos_source, imag_time) - mixing(sin_source, real_time)
    magnitude = jnp.sqrt(real_part * real_part + imag_part * imag_part)
    bound = limits[None, :, None]
    factor = jnp.maximum(magnitude - bound, 0.0) / jnp.maximum(magnitude, bound)
    kept_real = real_part * factor
    kept_imag = imag_part * factor
    back_real = mixing(cos_source, kept_real) - mixing(sin_source, kept_imag)
    back_imag = mixing(cos_source, kept_imag) + mixing(sin_source, kept_real)
    restored = jnp.dot(
        back_real.reshape(-1, WIN),
        cos_inverse,
        precision=careful,
        preferred_element_type=jnp.float32,
    )
    restored = restored + jnp.dot(
        back_imag.reshape(-1, WIN),
        sin_inverse,
        precision=careful,
        preferred_element_type=jnp.float32,
    )
    return restored.reshape(receivers, sources, samples)


def gathers_of_own_samples(blended, delays, thresholds):
    tables = make_tables()
    local_count = blended.shape[1]
    own_delays = lax.dynamic_slice_in_dim(
        delays, lax.axis_index("shot") * local_count, local_count, 0
    )
    estimate = None
    for sweep in range(ITERS):
        if sweep == 0:
            residual = blended.astype(jnp.bfloat16)
            update = (RELAX * spread(residual, own_delays)).astype(jnp.bfloat16)
        else:
            residual = (blended - blend(estimate, own_delays)).astype(jnp.bfloat16)
            update = (estimate.astype(jnp.float32) + RELAX * spread(residual, own_delays)).astype(
                jnp.bfloat16
            )
        gathers = lax.all_to_all(update, "shot", split_axis=0, concat_axis=1, tiled=True)
        filtered = coherence(gathers, thresholds[sweep], tables).astype(jnp.bfloat16)
        estimate = lax.all_to_all(filtered, "shot", split_axis=1, concat_axis=0, tiled=True)
    return estimate


def whole_receivers_fit(shots, blocks_of_time, receivers, samples):
    held, windows = SRC // shots, samples // WIN
    return (
        receivers % (shots * blocks_of_time) == 0
        and held * 2 == SUB
        and windows % 2 == 0
        and windows * blocks_of_time == SUB
        and receivers // (shots * blocks_of_time) * SUB <= HALF
    )


def local(blended, delays, thresholds):
    shots, blocks_of_time = lax.axis_size("shot"), lax.axis_size("tm")
    if whole_receivers_fit(shots, blocks_of_time, blended.shape[0], blended.shape[2]):
        return gathers_of_all_samples(shots, blended, delays, thresholds)
    return gathers_of_own_samples(blended, delays, thresholds)


def solution(mesh):
    return jax.shard_map(
        local,
        mesh=mesh,
        in_specs=(P(None, "shot", "tm"), P(), P()),
        out_specs=P(None, "shot", "tm"),
        check_vma=False,
    )
```

```python
import functools
import math

import jax
import jax.numpy as jnp
import ml_dtypes
import numpy as np
from jax import lax
from jax.experimental import pallas as pl
from jax.experimental.pallas import tpu as pltpu
from jax.sharding import PartitionSpec as P

SRC = 64
SRC_EXP = 2
WIN = 256
BLK = 128
ITERS = 2


RELAX = 0.5
HALF = WIN // 2
SUB = 8
SPAN = 4
TILE = 256


def split_table(table):
    high = table.astype(ml_dtypes.bfloat16)
    low = (table - high.astype(np.float64)).astype(ml_dtypes.bfloat16)
    return high, low


def half_spectrum_tables():
    moment = np.arange(WIN)
    angle = (moment[:, None] * np.arange(HALF)[None, :] % WIN) * (2.0 * math.pi / WIN)
    nyquist = np.where(moment % 2 == 0, 1.0, -1.0)
    sine = -np.sin(angle)
    sine[:, 0] = nyquist
    forward = np.concatenate([np.cos(angle), sine], axis=1).astype(ml_dtypes.bfloat16)
    inverse = np.concatenate([np.cos(angle), sine], axis=1).T / math.sqrt(WIN)
    inverse[0] *= 0.5
    inverse[HALF] *= 0.5
    source = np.arange(SRC)
    turn = (source[:, None] * source[None, :] % SRC) * (2.0 * math.pi / SRC)
    cosine, sine = np.cos(turn) / math.sqrt(SRC), np.sin(turn) / math.sqrt(SRC)
    onward = np.block([[cosine, sine], [-sine, cosine]])
    pair = []
    for table in (onward / math.sqrt(WIN), onward.T):
        high, low = split_table(table)
        pair.append(np.block([[high, high], [low, low]]))
    return (forward, *split_table(inverse), *pair)


def rearranging(shape, axes):
    order = np.arange(math.prod(shape)).reshape(shape).transpose(axes).reshape(-1)
    return np.eye(order.size)[order].astype(ml_dtypes.bfloat16)


def order_tables(windows, own):
    shots, sources = TILE // (2 * windows * own), TILE // windows
    return (
        rearranging((shots, windows, 2, own), (0, 3, 2, 1)),
        rearranging((sources, windows), (1, 0)),
        rearranging((windows, sources), (1, 0)),
    )


def halves(value):
    high = value.astype(jnp.bfloat16)
    return high, (value - high.astype(jnp.float32)).astype(jnp.bfloat16)


def bfloat(value):
    return value.astype(jnp.bfloat16).astype(jnp.float32)


def product(left, right):
    return jnp.dot(left, right, preferred_element_type=jnp.float32)


def gather_kernel(
    shots,
    delays,
    limits,
    received,
    forward,
    inverse_high,
    inverse_low,
    onward,
    backward,
    order_arrived,
    order_windows,
    order_sources,
    out,
    records,
    field,
    mixed,
    back_high,
    back_low,
    estimates,
):
    count, receivers, rows, _ = received.shape
    blocks_of_time = count // shots
    experiments, sources = delays.shape[1], SRC
    windows = blocks_of_time * rows * shots // (2 * experiments)
    groups = receivers * windows
    parts = windows // blocks_of_time
    some = TILE // windows
    lane = lax.broadcasted_iota(jnp.int32, (windows, BLK), 1)
    row = lax.broadcasted_iota(jnp.int32, (windows, BLK), 0)
    lane_of_group = lax.broadcasted_iota(jnp.int32, (sources, HALF), 1)
    lane_of_some = lax.broadcasted_iota(jnp.int32, (some, HALF), 1)

    for chunk in range(sources // some):
        senders = slice(chunk * TILE // rows, (chunk + 1) * TILE // rows)
        arrived = [received[senders, r].reshape(TILE, BLK) for r in range(receivers)]
        records[chunk] = product(order_arrived[...], jnp.concatenate(arrived, axis=1))

    def advanced(even, odd, delay):
        by = (BLK - delay) & (BLK - 1)
        even, odd = pltpu.roll(even, by, 1), pltpu.roll(odd, by, 1)
        after = jnp.where(row < windows - 1, pltpu.roll(even, windows - 1, 0), 0.0)
        same = lane < BLK - delay
        return jnp.where(same, even, odd), jnp.where(same, odd, after)

    def delayed(even, odd, delay):
        even, odd = pltpu.roll(even, delay, 1), pltpu.roll(odd, delay, 1)
        before = jnp.where(row > 0, pltpu.roll(odd, 1, 0), 0.0)
        same = lane >= delay
        return jnp.where(same, even, before), jnp.where(same, odd, even)

    def columns(group, many=1):
        return slice(group * HALF, (group + many) * HALF)

    def update(sweep, r, chunk):
        if sweep > 0:
            before = [
                estimates[pl.ds((r * windows + w) * sources + chunk * some, some), :]
                for w in range(windows)
            ]
            before = product(order_sources[...], jnp.concatenate(before, axis=0))
        updated = []
        for at in range(0, some, SRC_EXP):
            experiment = (chunk * some + at) // SRC_EXP
            lags = [delays[k, experiment] for k in range(SRC_EXP)]
            even, odd = (
                records[chunk, pl.ds((at + half) * windows, windows), columns(r)]
                for half in range(2)
            )
            if sweep > 0:
                estimate = [
                    tuple(
                        before[(at + k) * windows : (at + k + 1) * windows, columns(half)]
                        for half in range(2)
                    )
                    for k in range(SRC_EXP)
                ]
                late = [delayed(*estimate[k], lags[k]) for k in range(SRC_EXP)]
                even = bfloat(even - sum(x[0] for x in late))
                odd = bfloat(odd - sum(x[1] for x in late))
            for k in range(SRC_EXP):
                values = [RELAX * x for x in advanced(even, odd, lags[k])]
                if sweep > 0:
                    values = [a + b for a, b in zip(estimate[k], values)]
                updated.append(jnp.concatenate(values, axis=1))
        return jnp.concatenate(updated, axis=0).astype(jnp.bfloat16)

    def update_and_forward_in_time(sweep):
        for chunk in range(sources // some):
            nyquist = jnp.zeros((some, HALF), jnp.float32)
            for r in range(receivers):
                signal = product(order_windows[...], update(sweep, r, chunk))
                spectra = product(signal.astype(jnp.bfloat16), forward[...])
                for w in range(windows):
                    group = r * windows + w
                    spectrum = spectra[w * some : (w + 1) * some]
                    real, imag = spectrum[:, :HALF], spectrum[:, HALF:]
                    moved = pltpu.roll(imag, group, 1) if group else imag
                    nyquist = jnp.where(lane_of_some == group, moved, nyquist)
                    imag = jnp.where(lane_of_some == 0, 0.0, imag)
                    put(field, columns(group), real, imag, chunk * some)
            put(field, columns(groups), nyquist, jnp.zeros_like(nyquist), chunk * some)

    def put(ref, where, real, imag, first=0):
        real_high, real_low = halves(real)
        imag_high, imag_low = halves(imag)
        for at, value in enumerate((real_high, imag_high, real_low, imag_low)):
            start = at * sources + first
            ref[start : start + value.shape[0], where] = value

    def chunks():
        yield columns(groups)
        for group in range(0, groups, 2):
            yield columns(group, 2)

    def mixing(table, ref, where):
        both = product(table[...], ref[:, where])
        total = both[: 2 * sources] + both[2 * sources :]
        return total[:sources], total[sources:]

    def shrink(sweep):
        limit = limits[sweep : sweep + 1, :]
        p = lax.broadcasted_iota(jnp.int32, (sources, sources), 0)
        q = lax.broadcasted_iota(jnp.int32, (sources, sources), 1)
        bound = jnp.sum(jnp.where(p == q, limit, 0.0), axis=1, keepdims=True)
        mirrored = (p + q == 0) | (p + q == sources)
        bound_mirrored = jnp.sum(jnp.where(mirrored, limit, 0.0), axis=1, keepdims=True)
        for where in chunks():
            real, imag = mixing(onward, field, where)
            inverse_size = lax.rsqrt(real * real + imag * imag)
            factor = jnp.maximum(1.0 - bound * inverse_size, 0.0) + jnp.maximum(
                1.0 - bound_mirrored * inverse_size, 0.0
            )
            put(mixed, where, real * factor, imag * factor)

    def back_in_source():
        nyquist = None
        group = 0
        for where in chunks():
            real, imag = mixing(backward, mixed, where)
            if nyquist is None:
                nyquist = real
                continue
            for part in range(2):
                own_real, own_imag = real[:, columns(part)], imag[:, columns(part)]
                moved = pltpu.roll(nyquist, HALF - group, 1) if group else nyquist
                own_imag = jnp.where(lane_of_group == 0, moved, own_imag)
                rows_of_group = slice(group * sources, (group + 1) * sources)
                for half, value in enumerate((own_real, own_imag)):
                    high, low = halves(value)
                    back_high[rows_of_group, columns(half)] = high
                    back_low[rows_of_group, columns(half)] = low
                group += 1

    def back_in_time(rows_of_span):
        high = back_high[rows_of_span, :]
        return (
            product(high, inverse_high[...])
            + product(back_low[rows_of_span, :], inverse_high[...])
            + product(high, inverse_low[...])
        )

    def swapped(value):
        return pltpu.roll(value, SUB // 2, 1)

    def deliver(r, w, restored):
        low = lax.broadcasted_iota(jnp.int32, (sources // SUB, SUB, BLK), 1) < SUB // 2
        pieces = []
        for part in range(2):
            window = restored[part * sources : (part + 1) * sources]
            even = window[:, :BLK].reshape(sources // SUB, SUB, BLK)
            odd = window[:, BLK:].reshape(sources // SUB, SUB, BLK)
            pieces.append(
                (jnp.where(low, even, swapped(odd)), jnp.where(low, swapped(even), odd))
            )
        block, inside = w // parts, w % parts
        for side in range(2):
            both = jnp.concatenate([pieces[0][side], pieces[1][side]], axis=1)
            both = both.astype(jnp.bfloat16)
            for k in range(sources // SUB):
                target = (2 * k + side) * blocks_of_time + block
                out[target, r, inside * SUB : (inside + 2) * SUB, :] = both[k]

    for sweep in range(ITERS):
        update_and_forward_in_time(sweep)
        shrink(sweep)
        back_in_source()
        for start in range(0, groups, SPAN):
            rows_of_span = slice(start * sources, (start + SPAN) * sources)
            restored = back_in_time(rows_of_span)
            if sweep < ITERS - 1:
                estimates[rows_of_span, :] = restored.astype(jnp.bfloat16)
                continue
            for group in range(0, SPAN, 2):
                pair = restored[group * sources : (group + 2) * sources]
                deliver((start + group) // windows, (start + group) % windows, pair)


def gathers_of_all_samples(shots, blended, delays, thresholds):
    receivers, own, samples = blended.shape
    blocks_of_time = lax.axis_size("tm")
    count = shots * blocks_of_time
    each = receivers // count
    blocks = samples // BLK
    windows = samples * blocks_of_time // WIN
    groups = each * windows
    rows = blocks * own
    sent = blended.reshape(receivers, own, blocks, BLK).transpose(0, 2, 1, 3)
    sent = lax.optimization_barrier(sent.reshape(count, each, rows, BLK)).astype(jnp.bfloat16)
    received = lax.all_to_all(sent, ("shot", "tm"), split_axis=0, concat_axis=0, tiled=True)
    tables = half_spectrum_tables() + order_tables(windows, own)
    tables = [jnp.asarray(table) for table in tables]
    vmem = pl.BlockSpec(memory_space=pltpu.VMEM)
    held = SRC // shots
    restored = pl.pallas_call(
        functools.partial(gather_kernel, shots),
        out_shape=jax.ShapeDtypeStruct((count, each, blocks * held, BLK), jnp.bfloat16),
        in_specs=[pl.BlockSpec(memory_space=pltpu.SMEM)] + [vmem] * (2 + len(tables)),
        out_specs=vmem,
        scratch_shapes=[
            pltpu.VMEM((SRC * windows // TILE, TILE, each * BLK), jnp.float32),
            pltpu.VMEM((4 * SRC, (groups + 1) * HALF), jnp.bfloat16),
            pltpu.VMEM((4 * SRC, (groups + 1) * HALF), jnp.bfloat16),
            pltpu.VMEM((groups * SRC, WIN), jnp.bfloat16),
            pltpu.VMEM((groups * SRC, WIN), jnp.bfloat16),
            pltpu.VMEM((groups * SRC, WIN), jnp.bfloat16),
        ],
        compiler_params=pltpu.CompilerParams(vmem_limit_bytes=40 * 1024 * 1024),
        cost_estimate=pl.CostEstimate(
            flops=2 * ITERS * groups * SRC * WIN * WIN * 9,
            bytes_accessed=2 * 1024 * 1024,
            transcendentals=ITERS * groups * SRC * HALF,
        ),
    )(delays.T, thresholds, received, *tables)
    final = lax.all_to_all(restored, ("shot", "tm"), split_axis=0, concat_axis=0, tiled=True)
    final = final.reshape(receivers, blocks, held, BLK).transpose(0, 2, 1, 3)
    return final.reshape(receivers, held, samples)


def shifted(array, axis, by):
    count = lax.axis_size(axis)
    pairs = [(i, i + by) for i in range(count) if 0 <= i + by < count]
    return lax.ppermute(array, axis, pairs)


def phase_table(length_first, length_second, period):
    first_index = jnp.arange(length_first, dtype=jnp.int32)[:, None]
    second_index = jnp.arange(length_second, dtype=jnp.int32)[None, :]
    return (first_index * second_index % period).astype(jnp.float32) * (2.0 * math.pi / period)


def make_tables():
    time_angle = phase_table(WIN, WIN, WIN)
    time_scale = 1.0 / math.sqrt(WIN)
    cos_forward = jnp.cos(time_angle).astype(jnp.bfloat16)
    sin_forward = -jnp.sin(time_angle).astype(jnp.bfloat16)
    cos_inverse = jnp.cos(time_angle) * time_scale
    sin_inverse = -jnp.sin(time_angle) * time_scale
    source_angle = phase_table(SRC, SRC, SRC)
    cos_source = jnp.cos(source_angle) / math.sqrt(SRC)
    sin_source = jnp.sin(source_angle) / math.sqrt(SRC)
    return (cos_forward, sin_forward, cos_inverse, sin_inverse, cos_source, sin_source)


def blend(estimate, own_delays):
    receivers, sources, samples = estimate.shape
    blocks = samples // BLK
    experiments = sources // SRC_EXP
    earlier = shifted(estimate[:, :, samples - BLK :], "tm", 1)
    upper = estimate.reshape(receivers, sources, blocks, BLK)
    shifts = own_delays.reshape(-1)
    row_index = jnp.arange(BLK, dtype=jnp.int32)[None, :, None]
    column_index = jnp.arange(BLK, dtype=jnp.int32)[None, None, :]
    select_same = (row_index == column_index - shifts[:, None, None]).astype(jnp.bfloat16)
    select_prior = (row_index == BLK + column_index - shifts[:, None, None]).astype(jnp.bfloat16)
    same = jnp.einsum("rsnb,sbi->rsni", upper, select_same, preferred_element_type=jnp.float32)
    onward = jnp.einsum("rsnb,sbi->rsni", upper, select_prior, preferred_element_type=jnp.float32)
    edge_part = jnp.einsum(
        "rsb,sbi->rsi", earlier, select_prior, preferred_element_type=jnp.float32
    )
    same = jnp.sum(same.reshape(receivers, experiments, SRC_EXP, blocks, BLK), axis=2)
    onward = jnp.sum(onward.reshape(receivers, experiments, SRC_EXP, blocks, BLK), axis=2)
    edge_part = jnp.sum(edge_part.reshape(receivers, experiments, SRC_EXP, BLK), axis=2)
    carried = jnp.concatenate([edge_part[:, :, None], onward[:, :, : blocks - 1]], axis=2)
    return (same + carried).reshape(receivers, experiments, samples)


def spread(residual, own_delays):
    receivers, experiments, samples = residual.shape
    blocks = samples // BLK
    later = shifted(residual[:, :, :BLK], "tm", -1)
    lower = residual.reshape(receivers, experiments, blocks, BLK)
    row_index = jnp.arange(BLK, dtype=jnp.int32)[None, None, :, None]
    column_index = jnp.arange(BLK, dtype=jnp.int32)[None, None, None, :]
    select_same = (row_index == column_index + own_delays[:, :, None, None]).astype(jnp.bfloat16)
    select_next = (row_index + BLK == column_index + own_delays[:, :, None, None]).astype(
        jnp.bfloat16
    )
    same = jnp.einsum("rena,ekai->rekni", lower, select_same, preferred_element_type=jnp.float32)
    backward = jnp.einsum(
        "rena,ekai->rekni", lower, select_next, preferred_element_type=jnp.float32
    )
    edge_part = jnp.einsum("rea,ekai->reki", later, select_next, preferred_element_type=jnp.float32)
    carried = jnp.concatenate([backward[:, :, :, 1:], edge_part[:, :, :, None]], axis=3)
    return (same + carried).reshape(receivers, experiments * SRC_EXP, samples)


def coherence(gathers, limits, tables):
    cos_forward, sin_forward, cos_inverse, sin_inverse, cos_source, sin_source = tables
    receivers, sources, samples = gathers.shape
    windows = samples // WIN
    careful = lax.Precision.HIGH
    scale = 1.0 / math.sqrt(WIN)
    signal = gathers.reshape(receivers * sources * windows, WIN)
    real_time = (jnp.dot(signal, cos_forward, preferred_element_type=jnp.float32) * scale).reshape(
        receivers, sources, samples
    )
    imag_time = (jnp.dot(signal, sin_forward, preferred_element_type=jnp.float32) * scale).reshape(
        receivers, sources, samples
    )

    def mixing(table, field):
        return jnp.einsum(
            "ps,rsx->rpx", table, field, precision=careful, preferred_element_type=jnp.float32
        )

    real_part = mixing(cos_source, real_time) + mixing(sin_source, imag_time)
    imag_part = mixing(cos_source, imag_time) - mixing(sin_source, real_time)
    magnitude = jnp.sqrt(real_part * real_part + imag_part * imag_part)
    bound = limits[None, :, None]
    factor = jnp.maximum(magnitude - bound, 0.0) / jnp.maximum(magnitude, bound)
    kept_real = real_part * factor
    kept_imag = imag_part * factor
    back_real = mixing(cos_source, kept_real) - mixing(sin_source, kept_imag)
    back_imag = mixing(cos_source, kept_imag) + mixing(sin_source, kept_real)
    restored = jnp.dot(
        back_real.reshape(-1, WIN),
        cos_inverse,
        precision=careful,
        preferred_element_type=jnp.float32,
    )
    restored = restored + jnp.dot(
        back_imag.reshape(-1, WIN),
        sin_inverse,
        precision=careful,
        preferred_element_type=jnp.float32,
    )
    return restored.reshape(receivers, sources, samples)


def gathers_of_own_samples(blended, delays, thresholds):
    tables = make_tables()
    local_count = blended.shape[1]
    own_delays = lax.dynamic_slice_in_dim(
        delays, lax.axis_index("shot") * local_count, local_count, 0
    )
    estimate = None
    for sweep in range(ITERS):
        if sweep == 0:
            residual = blended.astype(jnp.bfloat16)
            update = (RELAX * spread(residual, own_delays)).astype(jnp.bfloat16)
        else:
            residual = (blended - blend(estimate, own_delays)).astype(jnp.bfloat16)
            update = (estimate.astype(jnp.float32) + RELAX * spread(residual, own_delays)).astype(
                jnp.bfloat16
            )
        gathers = lax.all_to_all(update, "shot", split_axis=0, concat_axis=1, tiled=True)
        filtered = coherence(gathers, thresholds[sweep], tables).astype(jnp.bfloat16)
        estimate = lax.all_to_all(filtered, "shot", split_axis=1, concat_axis=0, tiled=True)
    return estimate


def whole_receivers_fit(shots, blocks_of_time, receivers, samples):
    held, windows = SRC // shots, samples // WIN
    return (
        receivers % (shots * blocks_of_time) == 0
        and held * 2 == SUB
        and windows % 2 == 0
        and windows * blocks_of_time == SUB
        and receivers // (shots * blocks_of_time) * SUB <= HALF
    )


def local(blended, delays, thresholds):
    shots, blocks_of_time = lax.axis_size("shot"), lax.axis_size("tm")
    if whole_receivers_fit(shots, blocks_of_time, blended.shape[0], blended.shape[2]):
        return gathers_of_all_samples(shots, blended, delays, thresholds)
    return gathers_of_own_samples(blended, delays, thresholds)


def solution(mesh):
    return jax.shard_map(
        local,
        mesh=mesh,
        in_specs=(P(None, "shot", "tm"), P(), P()),
        out_specs=P(None, "shot", "tm"),
        check_vma=False,
    )
```

```python
import functools
import math

import jax
import jax.numpy as jnp
import ml_dtypes
import numpy as np
from jax import lax
from jax.experimental import pallas as pl
from jax.experimental.pallas import tpu as pltpu
from jax.sharding import PartitionSpec as P

SRC = 64
SRC_EXP = 2
WIN = 256
BLK = 128
ITERS = 2


RELAX = 0.5
HALF = WIN // 2
SUB = 8
SPAN = 4
TILE = 256


def bfloat_scale(table):
    values = np.unique(np.abs(table).round(12))
    factors = 1.0 + np.arange(4096) / 4096.0
    scaled = factors[:, None] * values
    lost = scaled.astype(ml_dtypes.bfloat16).astype(np.float64) - scaled
    return factors[np.argmin(np.sum((lost / factors[:, None]) ** 2, axis=1))]


def half_spectrum_tables():
    moment = np.arange(WIN)
    angle = (moment[:, None] * np.arange(HALF)[None, :] % WIN) * (2.0 * math.pi / WIN)
    nyquist = np.where(moment % 2 == 0, 1.0, -1.0)
    sine = -np.sin(angle)
    sine[:, 0] = nyquist
    forward = np.concatenate([np.cos(angle), sine], axis=1).astype(ml_dtypes.bfloat16)
    inverse = np.concatenate([np.cos(angle), sine], axis=1).T / math.sqrt(WIN)
    inverse[0] *= 0.5
    inverse[HALF] *= 0.5
    source = np.arange(SRC)
    turn = (source[:, None] * source[None, :] % SRC) * (2.0 * math.pi / SRC)
    cosine, sine = np.cos(turn) / math.sqrt(SRC), np.sin(turn) / math.sqrt(SRC)
    onward = np.block([[cosine, sine], [-sine, cosine]])
    source_scale, time_scale = bfloat_scale(onward), bfloat_scale(inverse)
    onward = onward * source_scale
    tables = (
        forward,
        inverse * time_scale,
        np.concatenate([onward, onward], axis=1) / math.sqrt(WIN),
        np.concatenate([onward.T, onward.T], axis=1),
    )
    tables = tuple(table.astype(ml_dtypes.bfloat16) for table in tables)
    return tables, source_scale, 1.0 / (source_scale * source_scale * time_scale)


def rearranging(shape, axes):
    order = np.arange(math.prod(shape)).reshape(shape).transpose(axes).reshape(-1)
    return np.eye(order.size)[order].astype(ml_dtypes.bfloat16)


def order_tables(windows, own):
    shots, sources = TILE // (2 * windows * own), TILE // windows
    return (
        rearranging((shots, windows, 2, own), (0, 3, 2, 1)),
        rearranging((sources, windows), (1, 0)),
        rearranging((windows, sources), (1, 0)),
    )


def halves(value):
    high = value.astype(jnp.bfloat16)
    return high, (value - high.astype(jnp.float32)).astype(jnp.bfloat16)


def product(left, right):
    return jnp.dot(left, right, preferred_element_type=jnp.float32)


def gather_kernel(
    shots,
    limit_scale,
    kept_scale,
    delays_far,
    limits_far,
    received,
    forward,
    inverse,
    onward,
    backward,
    order_arrived,
    order_windows,
    order_sources,
    out,
    delays,
    limits,
    records,
    field,
    mixed,
    back,
    estimates,
    sems,
):
    copies = [
        pltpu.make_async_copy(delays_far, delays, sems.at[0]),
        pltpu.make_async_copy(limits_far, limits, sems.at[1]),
    ]
    for copy in copies:
        copy.start()
    count, receivers, rows, _ = received.shape
    blocks_of_time = count // shots
    experiments, sources = delays.shape[1], SRC
    windows = blocks_of_time * rows * shots // (2 * experiments)
    groups = receivers * windows
    parts = windows // blocks_of_time
    some = TILE // windows
    lane = lax.broadcasted_iota(jnp.int32, (windows, BLK), 1)
    row = lax.broadcasted_iota(jnp.int32, (windows, BLK), 0)
    lane_of_group = lax.broadcasted_iota(jnp.int32, (sources, HALF), 1)
    lane_of_some = lax.broadcasted_iota(jnp.int32, (some, HALF), 1)

    for chunk in range(sources // some):
        senders = slice(chunk * TILE // rows, (chunk + 1) * TILE // rows)
        arrived = [received[senders, r].reshape(TILE, BLK) for r in range(receivers)]
        records[chunk] = product(order_arrived[...], jnp.concatenate(arrived, axis=1))

    for copy in copies:
        copy.wait()

    def advanced(even, odd, delay):
        by = (BLK - delay) & (BLK - 1)
        even, odd = pltpu.roll(even, by, 1), pltpu.roll(odd, by, 1)
        after = jnp.where(row < windows - 1, pltpu.roll(even, windows - 1, 0), 0.0)
        same = lane < BLK - delay
        return jnp.where(same, even, odd), jnp.where(same, odd, after)

    def delayed(even, odd, delay):
        even, odd = pltpu.roll(even, delay, 1), pltpu.roll(odd, delay, 1)
        before = jnp.where(row > 0, pltpu.roll(odd, 1, 0), 0.0)
        same = lane >= delay
        return jnp.where(same, even, before), jnp.where(same, odd, even)

    def columns(group, many=1):
        return slice(group * HALF, (group + many) * HALF)

    def update(sweep, r, chunk):
        if sweep > 0:
            before = [
                estimates[pl.ds((r * windows + w) * sources + chunk * some, some), :]
                for w in range(windows)
            ]
            before = product(order_sources[...], jnp.concatenate(before, axis=0))
        updated = []
        for at in range(0, some, SRC_EXP):
            experiment = (chunk * some + at) // SRC_EXP
            lags = [delays[k, experiment] for k in range(SRC_EXP)]
            even, odd = (
                records[chunk, pl.ds((at + half) * windows, windows), columns(r)]
                for half in range(2)
            )
            if sweep > 0:
                estimate = [
                    tuple(
                        before[(at + k) * windows : (at + k + 1) * windows, columns(half)]
                        for half in range(2)
                    )
                    for k in range(SRC_EXP)
                ]
                late = [delayed(*estimate[k], lags[k]) for k in range(SRC_EXP)]
                even = even - sum(x[0] for x in late)
                odd = odd - sum(x[1] for x in late)
            for k in range(SRC_EXP):
                values = [RELAX * x for x in advanced(even, odd, lags[k])]
                if sweep > 0:
                    values = [a + b for a, b in zip(estimate[k], values)]
                updated.append(jnp.concatenate(values, axis=1))
        return jnp.concatenate(updated, axis=0).astype(jnp.bfloat16)

    def update_and_forward_in_time(sweep):
        nyquists = [jnp.zeros((some, HALF), jnp.float32) for _ in range(sources // some)]
        for r in range(receivers):
            for chunk in range(sources // some):
                signal = product(order_windows[...], update(sweep, r, chunk))
                spectra = product(signal.astype(jnp.bfloat16), forward[...])
                for w in range(windows):
                    group = r * windows + w
                    spectrum = spectra[w * some : (w + 1) * some]
                    real, imag = spectrum[:, :HALF], spectrum[:, HALF:]
                    moved = pltpu.roll(imag, group, 1) if group else imag
                    nyquists[chunk] = jnp.where(lane_of_some == group, moved, nyquists[chunk])
                    imag = jnp.where(lane_of_some == 0, 0.0, imag)
                    put(field, columns(group), real, imag, chunk * some)
        for chunk, nyquist in enumerate(nyquists):
            put(field, columns(groups), nyquist, jnp.zeros_like(nyquist), chunk * some)

    def put(ref, where, real, imag, first=0):
        real_high, real_low = halves(real)
        imag_high, imag_low = halves(imag)
        for at, value in enumerate((real_high, imag_high, real_low, imag_low)):
            start = at * sources + first
            ref[start : start + value.shape[0], where] = value

    def chunks():
        yield columns(groups)
        for group in range(0, groups, 2):
            yield columns(group, 2)

    def mixing(table, ref, where):
        total = product(table[...], ref[:, where])
        return total[:sources], total[sources:]

    def shrink(sweep):
        limit = limits[sweep : sweep + 1, :] * (limit_scale * kept_scale)
        p = lax.broadcasted_iota(jnp.int32, (sources, sources), 0)
        q = lax.broadcasted_iota(jnp.int32, (sources, sources), 1)
        bound = jnp.sum(jnp.where(p == q, limit, 0.0), axis=1, keepdims=True)
        mirrored = (p + q == 0) | (p + q == sources)
        bound_mirrored = jnp.sum(jnp.where(mirrored, limit, 0.0), axis=1, keepdims=True)
        for where in chunks():
            real, imag = mixing(onward, field, where)
            inverse_size = lax.rsqrt(real * real + imag * imag)
            factor = jnp.maximum(kept_scale - bound * inverse_size, 0.0) + jnp.maximum(
                kept_scale - bound_mirrored * inverse_size, 0.0
            )
            put(mixed, where, real * factor, imag * factor)

    def back_in_source():
        nyquist = None
        group = 0
        for where in chunks():
            real, imag = mixing(backward, mixed, where)
            if nyquist is None:
                nyquist = real
                continue
            for part in range(2):
                own_real, own_imag = real[:, columns(part)], imag[:, columns(part)]
                moved = pltpu.roll(nyquist, HALF - group, 1) if group else nyquist
                own_imag = jnp.where(lane_of_group == 0, moved, own_imag)
                rows_of_group = slice(group * sources, (group + 1) * sources)
                for half, value in enumerate((own_real, own_imag)):
                    back[rows_of_group, columns(half)] = value.astype(jnp.bfloat16)
                group += 1

    def swapped(value):
        return pltpu.roll(value, SUB // 2, 1)

    def deliver(r, w, restored):
        low = lax.broadcasted_iota(jnp.int32, (sources // SUB, SUB, BLK), 1) < SUB // 2
        pieces = []
        for part in range(2):
            window = restored[part * sources : (part + 1) * sources]
            even = window[:, :BLK].reshape(sources // SUB, SUB, BLK)
            odd = window[:, BLK:].reshape(sources // SUB, SUB, BLK)
            pieces.append(
                (jnp.where(low, even, swapped(odd)), jnp.where(low, swapped(even), odd))
            )
        block, inside = w // parts, w % parts
        for side in range(2):
            both = jnp.concatenate([pieces[0][side], pieces[1][side]], axis=1)
            both = both.astype(jnp.bfloat16)
            for k in range(sources // SUB):
                target = (2 * k + side) * blocks_of_time + block
                out[target, r, inside * SUB : (inside + 2) * SUB, :] = both[k]

    for sweep in range(ITERS):
        update_and_forward_in_time(sweep)
        shrink(sweep)
        back_in_source()
        for start in range(0, groups, SPAN):
            rows_of_span = slice(start * sources, (start + SPAN) * sources)
            restored = product(back[rows_of_span, :], inverse[...])
            if sweep < ITERS - 1:
                estimates[rows_of_span, :] = restored.astype(jnp.bfloat16)
                continue
            for group in range(0, SPAN, 2):
                pair = restored[group * sources : (group + 2) * sources]
                deliver((start + group) // windows, (start + group) % windows, pair)


def gathers_of_all_samples(shots, blended, delays, thresholds):
    receivers, own, samples = blended.shape
    blocks_of_time = lax.axis_size("tm")
    count = shots * blocks_of_time
    each = receivers // count
    blocks = samples // BLK
    windows = samples * blocks_of_time // WIN
    groups = each * windows
    rows = blocks * own
    sent = blended.reshape(receivers, own, blocks, BLK).transpose(0, 2, 1, 3)
    sent = lax.optimization_barrier(sent.reshape(count, each, rows, BLK)).astype(jnp.bfloat16)
    received = lax.all_to_all(sent, ("shot", "tm"), split_axis=0, concat_axis=0, tiled=True)
    tables, limit_scale, kept_scale = half_spectrum_tables()
    tables = [jnp.asarray(table) for table in tables + order_tables(windows, own)]
    vmem, far = pl.BlockSpec(memory_space=pltpu.VMEM), pl.BlockSpec(memory_space=pltpu.HBM)
    held = SRC // shots
    restored = pl.pallas_call(
        functools.partial(gather_kernel, shots, float(limit_scale), float(kept_scale)),
        out_shape=jax.ShapeDtypeStruct((count, each, blocks * held, BLK), jnp.bfloat16),
        in_specs=[far] * 2 + [vmem] * (1 + len(tables)),
        out_specs=vmem,
        scratch_shapes=[
            pltpu.SMEM(delays.T.shape, jnp.int32),
            pltpu.VMEM(thresholds.shape, jnp.float32),
            pltpu.VMEM((SRC * windows // TILE, TILE, each * BLK), jnp.float32),
            pltpu.VMEM((4 * SRC, (groups + 1) * HALF), jnp.bfloat16),
            pltpu.VMEM((4 * SRC, (groups + 1) * HALF), jnp.bfloat16),
            pltpu.VMEM((groups * SRC, WIN), jnp.bfloat16),
            pltpu.VMEM((groups * SRC, WIN), jnp.bfloat16),
            pltpu.SemaphoreType.DMA((2,)),
        ],
        compiler_params=pltpu.CompilerParams(vmem_limit_bytes=40 * 1024 * 1024),
        cost_estimate=pl.CostEstimate(
            flops=2 * ITERS * groups * SRC * WIN * WIN * 5,
            bytes_accessed=2 * 1024 * 1024,
            transcendentals=ITERS * groups * SRC * HALF,
        ),
    )(delays.T, thresholds, received, *tables)
    final = lax.all_to_all(restored, ("shot", "tm"), split_axis=0, concat_axis=0, tiled=True)
    final = final.reshape(receivers, blocks, held, BLK).transpose(0, 2, 1, 3)
    return final.reshape(receivers, held, samples)


def shifted(array, axis, by):
    count = lax.axis_size(axis)
    pairs = [(i, i + by) for i in range(count) if 0 <= i + by < count]
    return lax.ppermute(array, axis, pairs)


def phase_table(length_first, length_second, period):
    first_index = jnp.arange(length_first, dtype=jnp.int32)[:, None]
    second_index = jnp.arange(length_second, dtype=jnp.int32)[None, :]
    return (first_index * second_index % period).astype(jnp.float32) * (2.0 * math.pi / period)


def make_tables():
    time_angle = phase_table(WIN, WIN, WIN)
    time_scale = 1.0 / math.sqrt(WIN)
    cos_forward = jnp.cos(time_angle).astype(jnp.bfloat16)
    sin_forward = -jnp.sin(time_angle).astype(jnp.bfloat16)
    cos_inverse = jnp.cos(time_angle) * time_scale
    sin_inverse = -jnp.sin(time_angle) * time_scale
    source_angle = phase_table(SRC, SRC, SRC)
    cos_source = jnp.cos(source_angle) / math.sqrt(SRC)
    sin_source = jnp.sin(source_angle) / math.sqrt(SRC)
    return (cos_forward, sin_forward, cos_inverse, sin_inverse, cos_source, sin_source)


def blend(estimate, own_delays):
    receivers, sources, samples = estimate.shape
    blocks = samples // BLK
    experiments = sources // SRC_EXP
    earlier = shifted(estimate[:, :, samples - BLK :], "tm", 1)
    upper = estimate.reshape(receivers, sources, blocks, BLK)
    shifts = own_delays.reshape(-1)
    row_index = jnp.arange(BLK, dtype=jnp.int32)[None, :, None]
    column_index = jnp.arange(BLK, dtype=jnp.int32)[None, None, :]
    select_same = (row_index == column_index - shifts[:, None, None]).astype(jnp.bfloat16)
    select_prior = (row_index == BLK + column_index - shifts[:, None, None]).astype(jnp.bfloat16)
    same = jnp.einsum("rsnb,sbi->rsni", upper, select_same, preferred_element_type=jnp.float32)
    onward = jnp.einsum("rsnb,sbi->rsni", upper, select_prior, preferred_element_type=jnp.float32)
    edge_part = jnp.einsum(
        "rsb,sbi->rsi", earlier, select_prior, preferred_element_type=jnp.float32
    )
    same = jnp.sum(same.reshape(receivers, experiments, SRC_EXP, blocks, BLK), axis=2)
    onward = jnp.sum(onward.reshape(receivers, experiments, SRC_EXP, blocks, BLK), axis=2)
    edge_part = jnp.sum(edge_part.reshape(receivers, experiments, SRC_EXP, BLK), axis=2)
    carried = jnp.concatenate([edge_part[:, :, None], onward[:, :, : blocks - 1]], axis=2)
    return (same + carried).reshape(receivers, experiments, samples)


def spread(residual, own_delays):
    receivers, experiments, samples = residual.shape
    blocks = samples // BLK
    later = shifted(residual[:, :, :BLK], "tm", -1)
    lower = residual.reshape(receivers, experiments, blocks, BLK)
    row_index = jnp.arange(BLK, dtype=jnp.int32)[None, None, :, None]
    column_index = jnp.arange(BLK, dtype=jnp.int32)[None, None, None, :]
    select_same = (row_index == column_index + own_delays[:, :, None, None]).astype(jnp.bfloat16)
    select_next = (row_index + BLK == column_index + own_delays[:, :, None, None]).astype(
        jnp.bfloat16
    )
    same = jnp.einsum("rena,ekai->rekni", lower, select_same, preferred_element_type=jnp.float32)
    backward = jnp.einsum(
        "rena,ekai->rekni", lower, select_next, preferred_element_type=jnp.float32
    )
    edge_part = jnp.einsum("rea,ekai->reki", later, select_next, preferred_element_type=jnp.float32)
    carried = jnp.concatenate([backward[:, :, :, 1:], edge_part[:, :, :, None]], axis=3)
    return (same + carried).reshape(receivers, experiments * SRC_EXP, samples)


def coherence(gathers, limits, tables):
    cos_forward, sin_forward, cos_inverse, sin_inverse, cos_source, sin_source = tables
    receivers, sources, samples = gathers.shape
    windows = samples // WIN
    careful = lax.Precision.HIGH
    scale = 1.0 / math.sqrt(WIN)
    signal = gathers.reshape(receivers * sources * windows, WIN)
    real_time = (jnp.dot(signal, cos_forward, preferred_element_type=jnp.float32) * scale).reshape(
        receivers, sources, samples
    )
    imag_time = (jnp.dot(signal, sin_forward, preferred_element_type=jnp.float32) * scale).reshape(
        receivers, sources, samples
    )

    def mixing(table, field):
        return jnp.einsum(
            "ps,rsx->rpx", table, field, precision=careful, preferred_element_type=jnp.float32
        )

    real_part = mixing(cos_source, real_time) + mixing(sin_source, imag_time)
    imag_part = mixing(cos_source, imag_time) - mixing(sin_source, real_time)
    magnitude = jnp.sqrt(real_part * real_part + imag_part * imag_part)
    bound = limits[None, :, None]
    factor = jnp.maximum(magnitude - bound, 0.0) / jnp.maximum(magnitude, bound)
    kept_real = real_part * factor
    kept_imag = imag_part * factor
    back_real = mixing(cos_source, kept_real) - mixing(sin_source, kept_imag)
    back_imag = mixing(cos_source, kept_imag) + mixing(sin_source, kept_real)
    restored = jnp.dot(
        back_real.reshape(-1, WIN),
        cos_inverse,
        precision=careful,
        preferred_element_type=jnp.float32,
    )
    restored = restored + jnp.dot(
        back_imag.reshape(-1, WIN),
        sin_inverse,
        precision=careful,
        preferred_element_type=jnp.float32,
    )
    return restored.reshape(receivers, sources, samples)


def gathers_of_own_samples(blended, delays, thresholds):
    tables = make_tables()
    local_count = blended.shape[1]
    own_delays = lax.dynamic_slice_in_dim(
        delays, lax.axis_index("shot") * local_count, local_count, 0
    )
    estimate = None
    for sweep in range(ITERS):
        if sweep == 0:
            residual = blended.astype(jnp.bfloat16)
            update = (RELAX * spread(residual, own_delays)).astype(jnp.bfloat16)
        else:
            residual = (blended - blend(estimate, own_delays)).astype(jnp.bfloat16)
            update = (estimate.astype(jnp.float32) + RELAX * spread(residual, own_delays)).astype(
                jnp.bfloat16
            )
        gathers = lax.all_to_all(update, "shot", split_axis=0, concat_axis=1, tiled=True)
        filtered = coherence(gathers, thresholds[sweep], tables).astype(jnp.bfloat16)
        estimate = lax.all_to_all(filtered, "shot", split_axis=1, concat_axis=0, tiled=True)
    return estimate


def whole_receivers_fit(shots, blocks_of_time, receivers, samples):
    held, windows = SRC // shots, samples // WIN
    return (
        receivers % (shots * blocks_of_time) == 0
        and held * 2 == SUB
        and windows % 2 == 0
        and windows * blocks_of_time == SUB
        and receivers // (shots * blocks_of_time) * SUB <= HALF
    )


def local(blended, delays, thresholds):
    shots, blocks_of_time = lax.axis_size("shot"), lax.axis_size("tm")
    if whole_receivers_fit(shots, blocks_of_time, blended.shape[0], blended.shape[2]):
        return gathers_of_all_samples(shots, blended, delays, thresholds)
    return gathers_of_own_samples(blended, delays, thresholds)


def solution(mesh):
    return jax.shard_map(
        local,
        mesh=mesh,
        in_specs=(P(None, "shot", "tm"), P(), P()),
        out_specs=P(None, "shot", "tm"),
        check_vma=False,
    )
```

```python
import functools
import math

import jax
import jax.numpy as jnp
import ml_dtypes
import numpy as np
from jax import lax
from jax.experimental import pallas as pl
from jax.experimental.pallas import tpu as pltpu
from jax.sharding import PartitionSpec as P

SRC = 64
SRC_EXP = 2
WIN = 256
BLK = 128
ITERS = 2


RELAX = 0.5
HALF = WIN // 2
SUB = 8
SPAN = 4
TILE = 256


def bfloat_scale(table):
    values = np.unique(np.abs(table).round(12))
    factors = 1.0 + np.arange(4096) / 4096.0
    scaled = factors[:, None] * values
    lost = scaled.astype(ml_dtypes.bfloat16).astype(np.float64) - scaled
    return factors[np.argmin(np.sum((lost / factors[:, None]) ** 2, axis=1))]


def half_spectrum_tables():
    moment = np.arange(WIN)
    angle = (moment[:, None] * np.arange(HALF)[None, :] % WIN) * (2.0 * math.pi / WIN)
    nyquist = np.where(moment % 2 == 0, 1.0, -1.0)
    sine = -np.sin(angle)
    sine[:, 0] = nyquist
    forward = np.concatenate([np.cos(angle), sine], axis=1).astype(ml_dtypes.bfloat16)
    inverse = np.concatenate([np.cos(angle), sine], axis=1).T / math.sqrt(WIN)
    inverse[0] *= 0.5
    inverse[HALF] *= 0.5
    source = np.arange(SRC)
    turn = (source[:, None] * source[None, :] % SRC) * (2.0 * math.pi / SRC)
    cosine, sine = np.cos(turn) / math.sqrt(SRC), np.sin(turn) / math.sqrt(SRC)
    onward = np.block([[cosine, sine], [-sine, cosine]])
    source_scale, time_scale = bfloat_scale(onward), bfloat_scale(inverse)
    onward = onward * source_scale
    tables = (
        forward,
        inverse * time_scale,
        np.concatenate([onward, onward], axis=1) / math.sqrt(WIN),
        np.concatenate([onward.T, onward.T], axis=1),
    )
    tables = tuple(table.astype(ml_dtypes.bfloat16) for table in tables)
    return tables, source_scale, 1.0 / (source_scale * source_scale * time_scale)


def rearranging(shape, axes):
    order = np.arange(math.prod(shape)).reshape(shape).transpose(axes).reshape(-1)
    return np.eye(order.size)[order].astype(ml_dtypes.bfloat16)


def order_tables(windows, own):
    shots, sources = TILE // (2 * windows * own), TILE // windows
    return (
        rearranging((shots, windows, 2, own), (0, 3, 2, 1)),
        rearranging((sources, windows), (1, 0)),
        rearranging((windows, sources), (1, 0)),
    )


def halves(value):
    high = value.astype(jnp.bfloat16)
    return high, (value - high.astype(jnp.float32)).astype(jnp.bfloat16)


def product(left, right):
    return jnp.dot(left, right, preferred_element_type=jnp.float32)


def gather_kernel(
    shots,
    limit_scale,
    kept_scale,
    delays_far,
    limits,
    received,
    tables,
    out,
    delays,
    records,
    field,
    mixed,
    back,
    firsts,
    estimates,
    sem,
):
    copy = pltpu.make_async_copy(delays_far, delays, sem)
    copy.start()
    forward, inverse, order_arrived, order_windows, order_sources = (
        tables.at[pl.ds(at * TILE, TILE)] for at in range(5)
    )
    onward, backward = (
        tables.at[pl.ds(5 * TILE + at * 2 * SRC, 2 * SRC)] for at in range(2)
    )
    count, receivers, rows, _ = received.shape
    blocks_of_time = count // shots
    experiments, sources = delays.shape[1], SRC
    windows = blocks_of_time * rows * shots // (2 * experiments)
    groups = receivers * windows
    parts = windows // blocks_of_time
    some = TILE // windows
    lane = lax.broadcasted_iota(jnp.int32, (windows, BLK), 1)
    row = lax.broadcasted_iota(jnp.int32, (windows, BLK), 0)
    lane_of_group = lax.broadcasted_iota(jnp.int32, (sources, HALF), 1)
    lane_of_some = lax.broadcasted_iota(jnp.int32, (some, HALF), 1)

    for chunk in range(sources // some):
        senders = slice(chunk * TILE // rows, (chunk + 1) * TILE // rows)
        arrived = [received[senders, r].reshape(TILE, BLK) for r in range(receivers)]
        records[chunk] = product(order_arrived[...], jnp.concatenate(arrived, axis=1))

    copy.wait()

    def advanced(even, odd, delay):
        by = (BLK - delay) & (BLK - 1)
        even, odd = pltpu.roll(even, by, 1), pltpu.roll(odd, by, 1)
        after = jnp.where(row < windows - 1, pltpu.roll(even, windows - 1, 0), 0.0)
        same = lane < BLK - delay
        return jnp.where(same, even, odd), jnp.where(same, odd, after)

    def moved_by(even, odd, ahead_by):
        ahead = ahead_by >= 0
        by = (BLK - ahead_by) & (BLK - 1)
        even, odd = pltpu.roll(even, by, 1), pltpu.roll(odd, by, 1)
        other = pltpu.roll(jnp.where(ahead, even, odd), jnp.where(ahead, windows - 1, 1), 0)
        other = jnp.where(row != jnp.where(ahead, windows - 1, 0), other, 0.0)
        same = ((lane + ahead_by) & -BLK) == 0
        return (
            jnp.where(same, even, jnp.where(ahead, odd, other)),
            jnp.where(same, odd, jnp.where(ahead, other, even)),
        )

    def columns(group, many=1):
        return slice(group * HALF, (group + many) * HALF)

    def first_update(r, chunk):
        updated = []
        for at in range(0, some, SRC_EXP):
            even, odd = (
                records[chunk, pl.ds((at + half) * windows, windows), columns(r)]
                for half in range(2)
            )
            for k in range(SRC_EXP):
                early = advanced(even, odd, delays[k, (chunk * some + at) // SRC_EXP])
                updated.append(jnp.concatenate([RELAX * x for x in early], axis=1))
        updated = jnp.concatenate(updated, axis=0).astype(jnp.bfloat16)
        firsts[pl.ds((r * sources + chunk * some) * windows, TILE), :] = updated
        return updated

    def later_update(r, chunk):
        before = [
            estimates[pl.ds((r * windows + w) * sources + chunk * some, some), :]
            for w in range(windows)
        ]
        before = product(order_sources[...], jnp.concatenate(before, axis=0))
        first = (r * sources + chunk * some) * windows
        updated = []
        for at in range(0, some, SRC_EXP):
            lags = [delays[k, (chunk * some + at) // SRC_EXP] for k in range(SRC_EXP)]
            spread = firsts[pl.ds(first + at * windows, SRC_EXP * windows), :]
            spread = spread.astype(jnp.float32)
            estimate = [
                tuple(
                    before[(at + k) * windows : (at + k + 1) * windows, columns(half)]
                    for half in range(2)
                )
                for k in range(SRC_EXP)
            ]
            for k in range(SRC_EXP):
                even, odd = estimate[k]
                other = moved_by(*estimate[1 - k], lags[k] - lags[1 - k])
                stays = (row < windows - 1) | (lane < BLK - lags[k])
                even = RELAX * (even - other[0])
                odd = jnp.where(stays, RELAX * (odd - other[1]), odd)
                step = spread[k * windows : (k + 1) * windows]
                updated.append(jnp.concatenate([even, odd], axis=1) + step)
        return jnp.concatenate(updated, axis=0).astype(jnp.bfloat16)

    def update_and_forward_in_time(sweep):
        nyquists = [jnp.zeros((some, HALF), jnp.float32) for _ in range(sources // some)]
        for r in range(receivers):
            for chunk in range(sources // some):
                update = later_update if sweep else first_update
                signal = product(order_windows[...], update(r, chunk))
                spectra = product(signal.astype(jnp.bfloat16), forward[...])
                for w in range(windows):
                    group = r * windows + w
                    spectrum = spectra[w * some : (w + 1) * some]
                    real, imag = spectrum[:, :HALF], spectrum[:, HALF:]
                    moved = pltpu.roll(imag, group, 1) if group else imag
                    nyquists[chunk] = jnp.where(lane_of_some == group, moved, nyquists[chunk])
                    imag = jnp.where(lane_of_some == 0, 0.0, imag)
                    put(field, columns(group), real, imag, chunk * some)
        for chunk, nyquist in enumerate(nyquists):
            put(field, columns(groups), nyquist, jnp.zeros_like(nyquist), chunk * some)

    def put(ref, where, real, imag, first=0):
        real_high, real_low = halves(real)
        imag_high, imag_low = halves(imag)
        for at, value in enumerate((real_high, imag_high, real_low, imag_low)):
            start = at * sources + first
            ref[start : start + value.shape[0], where] = value

    def chunks():
        yield columns(groups)
        for group in range(0, groups, 2):
            yield columns(group, 2)

    def mixing(table, ref, where):
        total = product(table[...], ref[:, where])
        return total[:sources], total[sources:]

    def shrink(sweep):
        limit = limits[sweep : sweep + 1, :] * (limit_scale * kept_scale)
        p = lax.broadcasted_iota(jnp.int32, (sources, sources), 0)
        q = lax.broadcasted_iota(jnp.int32, (sources, sources), 1)
        bound = jnp.sum(jnp.where(p == q, limit, 0.0), axis=1, keepdims=True)
        mirrored = (p + q == 0) | (p + q == sources)
        bound_mirrored = jnp.sum(jnp.where(mirrored, limit, 0.0), axis=1, keepdims=True)
        for where in chunks():
            real, imag = mixing(onward, field, where)
            inverse_size = lax.rsqrt(real * real + imag * imag)
            factor = jnp.maximum(kept_scale - bound * inverse_size, 0.0) + jnp.maximum(
                kept_scale - bound_mirrored * inverse_size, 0.0
            )
            put(mixed, where, real * factor, imag * factor)

    def back_in_source():
        nyquist = None
        group = 0
        for where in chunks():
            real, imag = mixing(backward, mixed, where)
            if nyquist is None:
                nyquist = real
                continue
            for part in range(2):
                own_real, own_imag = real[:, columns(part)], imag[:, columns(part)]
                moved = pltpu.roll(nyquist, HALF - group, 1) if group else nyquist
                own_imag = jnp.where(lane_of_group == 0, moved, own_imag)
                rows_of_group = slice(group * sources, (group + 1) * sources)
                for half, value in enumerate((own_real, own_imag)):
                    back[rows_of_group, columns(half)] = value.astype(jnp.bfloat16)
                group += 1

    def swapped(value):
        return pltpu.roll(value, SUB // 2, 1)

    def deliver(r, w, restored):
        low = lax.broadcasted_iota(jnp.int32, (sources // SUB, SUB, BLK), 1) < SUB // 2
        pieces = []
        for part in range(2):
            window = restored[part * sources : (part + 1) * sources]
            even = window[:, :BLK].reshape(sources // SUB, SUB, BLK)
            odd = window[:, BLK:].reshape(sources // SUB, SUB, BLK)
            pieces.append(
                (jnp.where(low, even, swapped(odd)), jnp.where(low, swapped(even), odd))
            )
        block, inside = w // parts, w % parts
        for side in range(2):
            both = jnp.concatenate([pieces[0][side], pieces[1][side]], axis=1)
            both = both.astype(jnp.bfloat16)
            for k in range(sources // SUB):
                target = (2 * k + side) * blocks_of_time + block
                out[target, r, inside * SUB : (inside + 2) * SUB, :] = both[k]

    for sweep in range(ITERS):
        update_and_forward_in_time(sweep)
        shrink(sweep)
        back_in_source()
        for start in range(0, groups, SPAN):
            rows_of_span = slice(start * sources, (start + SPAN) * sources)
            restored = product(back[rows_of_span, :], inverse[...])
            if sweep < ITERS - 1:
                estimates[rows_of_span, :] = restored.astype(jnp.bfloat16)
                continue
            for group in range(0, SPAN, 2):
                pair = restored[group * sources : (group + 2) * sources]
                deliver((start + group) // windows, (start + group) % windows, pair)


def cast_kernel(blended, delays, limits, sent, delays_near, limits_near):
    sent[...] = blended[...].astype(jnp.bfloat16)
    delays_near[...] = delays[...]
    limits_near[...] = limits[...]


def gathers_of_all_samples(shots, blended, delays, thresholds):
    receivers, own, samples = blended.shape
    blocks_of_time = lax.axis_size("tm")
    count = shots * blocks_of_time
    each = receivers // count
    blocks = samples // BLK
    windows = samples * blocks_of_time // WIN
    groups = each * windows
    rows = blocks * own
    sent = blended.reshape(receivers, own, blocks, BLK).transpose(0, 2, 1, 3)
    sent = sent.reshape(count, each, rows, BLK)
    vmem = pl.BlockSpec(memory_space=pltpu.VMEM)
    sent, delays, thresholds = pl.pallas_call(
        cast_kernel,
        out_shape=(
            jax.ShapeDtypeStruct(sent.shape, jnp.bfloat16),
            jax.ShapeDtypeStruct(delays.T.shape, delays.dtype),
            jax.ShapeDtypeStruct(thresholds.shape, thresholds.dtype),
        ),
        in_specs=[vmem] * 3,
        out_specs=[vmem] * 3,
        compiler_params=pltpu.CompilerParams(vmem_limit_bytes=8 * 1024 * 1024),
    )(sent, delays.T, thresholds)
    received = lax.all_to_all(sent, ("shot", "tm"), split_axis=0, concat_axis=0, tiled=True)
    tables, limit_scale, kept_scale = half_spectrum_tables()
    tables = np.concatenate(tables[:2] + order_tables(windows, own) + tables[2:], axis=0)
    held = SRC // shots
    restored = pl.pallas_call(
        functools.partial(gather_kernel, shots, float(limit_scale), float(kept_scale)),
        out_shape=jax.ShapeDtypeStruct((count, each, blocks * held, BLK), jnp.bfloat16),
        in_specs=[pl.BlockSpec(memory_space=pl.ANY)] + [vmem] * 3,
        out_specs=vmem,
        scratch_shapes=[
            pltpu.SMEM(delays.shape, jnp.int32),
            pltpu.VMEM((SRC * windows // TILE, TILE, each * BLK), jnp.float32),
            pltpu.VMEM((4 * SRC, (groups + 1) * HALF), jnp.bfloat16),
            pltpu.VMEM((4 * SRC, (groups + 1) * HALF), jnp.bfloat16),
            pltpu.VMEM((groups * SRC, WIN), jnp.bfloat16),
            pltpu.VMEM((groups * SRC, WIN), jnp.bfloat16),
            pltpu.VMEM((groups * SRC, WIN), jnp.bfloat16),
            pltpu.SemaphoreType.DMA(()),
        ],
        compiler_params=pltpu.CompilerParams(vmem_limit_bytes=40 * 1024 * 1024),
        cost_estimate=pl.CostEstimate(
            flops=2 * ITERS * groups * SRC * WIN * WIN * 5,
            bytes_accessed=2 * 1024 * 1024,
            transcendentals=ITERS * groups * SRC * HALF,
        ),
    )(delays, thresholds, received, jnp.asarray(tables))
    final = lax.all_to_all(restored, ("shot", "tm"), split_axis=0, concat_axis=0, tiled=True)
    final = final.reshape(receivers, blocks, held, BLK).transpose(0, 2, 1, 3)
    return final.reshape(receivers, held, samples)


def shifted(array, axis, by):
    count = lax.axis_size(axis)
    pairs = [(i, i + by) for i in range(count) if 0 <= i + by < count]
    return lax.ppermute(array, axis, pairs)


def phase_table(length_first, length_second, period):
    first_index = jnp.arange(length_first, dtype=jnp.int32)[:, None]
    second_index = jnp.arange(length_second, dtype=jnp.int32)[None, :]
    return (first_index * second_index % period).astype(jnp.float32) * (2.0 * math.pi / period)


def make_tables():
    time_angle = phase_table(WIN, WIN, WIN)
    time_scale = 1.0 / math.sqrt(WIN)
    cos_forward = jnp.cos(time_angle).astype(jnp.bfloat16)
    sin_forward = -jnp.sin(time_angle).astype(jnp.bfloat16)
    cos_inverse = jnp.cos(time_angle) * time_scale
    sin_inverse = -jnp.sin(time_angle) * time_scale
    source_angle = phase_table(SRC, SRC, SRC)
    cos_source = jnp.cos(source_angle) / math.sqrt(SRC)
    sin_source = jnp.sin(source_angle) / math.sqrt(SRC)
    return (cos_forward, sin_forward, cos_inverse, sin_inverse, cos_source, sin_source)


def blend(estimate, own_delays):
    receivers, sources, samples = estimate.shape
    blocks = samples // BLK
    experiments = sources // SRC_EXP
    earlier = shifted(estimate[:, :, samples - BLK :], "tm", 1)
    upper = estimate.reshape(receivers, sources, blocks, BLK)
    shifts = own_delays.reshape(-1)
    row_index = jnp.arange(BLK, dtype=jnp.int32)[None, :, None]
    column_index = jnp.arange(BLK, dtype=jnp.int32)[None, None, :]
    select_same = (row_index == column_index - shifts[:, None, None]).astype(jnp.bfloat16)
    select_prior = (row_index == BLK + column_index - shifts[:, None, None]).astype(jnp.bfloat16)
    same = jnp.einsum("rsnb,sbi->rsni", upper, select_same, preferred_element_type=jnp.float32)
    onward = jnp.einsum("rsnb,sbi->rsni", upper, select_prior, preferred_element_type=jnp.float32)
    edge_part = jnp.einsum(
        "rsb,sbi->rsi", earlier, select_prior, preferred_element_type=jnp.float32
    )
    same = jnp.sum(same.reshape(receivers, experiments, SRC_EXP, blocks, BLK), axis=2)
    onward = jnp.sum(onward.reshape(receivers, experiments, SRC_EXP, blocks, BLK), axis=2)
    edge_part = jnp.sum(edge_part.reshape(receivers, experiments, SRC_EXP, BLK), axis=2)
    carried = jnp.concatenate([edge_part[:, :, None], onward[:, :, : blocks - 1]], axis=2)
    return (same + carried).reshape(receivers, experiments, samples)


def spread(residual, own_delays):
    receivers, experiments, samples = residual.shape
    blocks = samples // BLK
    later = shifted(residual[:, :, :BLK], "tm", -1)
    lower = residual.reshape(receivers, experiments, blocks, BLK)
    row_index = jnp.arange(BLK, dtype=jnp.int32)[None, None, :, None]
    column_index = jnp.arange(BLK, dtype=jnp.int32)[None, None, None, :]
    select_same = (row_index == column_index + own_delays[:, :, None, None]).astype(jnp.bfloat16)
    select_next = (row_index + BLK == column_index + own_delays[:, :, None, None]).astype(
        jnp.bfloat16
    )
    same = jnp.einsum("rena,ekai->rekni", lower, select_same, preferred_element_type=jnp.float32)
    backward = jnp.einsum(
        "rena,ekai->rekni", lower, select_next, preferred_element_type=jnp.float32
    )
    edge_part = jnp.einsum("rea,ekai->reki", later, select_next, preferred_element_type=jnp.float32)
    carried = jnp.concatenate([backward[:, :, :, 1:], edge_part[:, :, :, None]], axis=3)
    return (same + carried).reshape(receivers, experiments * SRC_EXP, samples)


def coherence(gathers, limits, tables):
    cos_forward, sin_forward, cos_inverse, sin_inverse, cos_source, sin_source = tables
    receivers, sources, samples = gathers.shape
    windows = samples // WIN
    careful = lax.Precision.HIGH
    scale = 1.0 / math.sqrt(WIN)
    signal = gathers.reshape(receivers * sources * windows, WIN)
    real_time = (jnp.dot(signal, cos_forward, preferred_element_type=jnp.float32) * scale).reshape(
        receivers, sources, samples
    )
    imag_time = (jnp.dot(signal, sin_forward, preferred_element_type=jnp.float32) * scale).reshape(
        receivers, sources, samples
    )

    def mixing(table, field):
        return jnp.einsum(
            "ps,rsx->rpx", table, field, precision=careful, preferred_element_type=jnp.float32
        )

    real_part = mixing(cos_source, real_time) + mixing(sin_source, imag_time)
    imag_part = mixing(cos_source, imag_time) - mixing(sin_source, real_time)
    magnitude = jnp.sqrt(real_part * real_part + imag_part * imag_part)
    bound = limits[None, :, None]
    factor = jnp.maximum(magnitude - bound, 0.0) / jnp.maximum(magnitude, bound)
    kept_real = real_part * factor
    kept_imag = imag_part * factor
    back_real = mixing(cos_source, kept_real) - mixing(sin_source, kept_imag)
    back_imag = mixing(cos_source, kept_imag) + mixing(sin_source, kept_real)
    restored = jnp.dot(
        back_real.reshape(-1, WIN),
        cos_inverse,
        precision=careful,
        preferred_element_type=jnp.float32,
    )
    restored = restored + jnp.dot(
        back_imag.reshape(-1, WIN),
        sin_inverse,
        precision=careful,
        preferred_element_type=jnp.float32,
    )
    return restored.reshape(receivers, sources, samples)


def gathers_of_own_samples(blended, delays, thresholds):
    tables = make_tables()
    local_count = blended.shape[1]
    own_delays = lax.dynamic_slice_in_dim(
        delays, lax.axis_index("shot") * local_count, local_count, 0
    )
    estimate = None
    for sweep in range(ITERS):
        if sweep == 0:
            residual = blended.astype(jnp.bfloat16)
            update = (RELAX * spread(residual, own_delays)).astype(jnp.bfloat16)
        else:
            residual = (blended - blend(estimate, own_delays)).astype(jnp.bfloat16)
            update = (estimate.astype(jnp.float32) + RELAX * spread(residual, own_delays)).astype(
                jnp.bfloat16
            )
        gathers = lax.all_to_all(update, "shot", split_axis=0, concat_axis=1, tiled=True)
        filtered = coherence(gathers, thresholds[sweep], tables).astype(jnp.bfloat16)
        estimate = lax.all_to_all(filtered, "shot", split_axis=1, concat_axis=0, tiled=True)
    return estimate


def whole_receivers_fit(shots, blocks_of_time, receivers, samples):
    held, windows = SRC // shots, samples // WIN
    return (
        receivers % (shots * blocks_of_time) == 0
        and held * 2 == SUB
        and windows % 2 == 0
        and windows * blocks_of_time == SUB
        and receivers // (shots * blocks_of_time) * SUB <= HALF
    )


def local(blended, delays, thresholds):
    shots, blocks_of_time = lax.axis_size("shot"), lax.axis_size("tm")
    if whole_receivers_fit(shots, blocks_of_time, blended.shape[0], blended.shape[2]):
        return gathers_of_all_samples(shots, blended, delays, thresholds)
    return gathers_of_own_samples(blended, delays, thresholds)


def solution(mesh):
    return jax.shard_map(
        local,
        mesh=mesh,
        in_specs=(P(None, "shot", "tm"), P(), P()),
        out_specs=P(None, "shot", "tm"),
        check_vma=False,
    )
```

```python
import functools
import math

import jax
import jax.numpy as jnp
import ml_dtypes
import numpy as np
from jax import lax
from jax.experimental import pallas as pl
from jax.experimental.pallas import tpu as pltpu
from jax.sharding import PartitionSpec as P

SRC = 64
SRC_EXP = 2
WIN = 256
BLK = 128
ITERS = 2


RELAX = 0.5
HALF = WIN // 2
SUB = 8
SPAN = 4
TILE = 256


def bfloat_scale(table):
    values = np.unique(np.abs(table).round(12))
    factors = 1.0 + np.arange(4096) / 4096.0
    scaled = factors[:, None] * values
    lost = scaled.astype(ml_dtypes.bfloat16).astype(np.float64) - scaled
    return factors[np.argmin(np.sum((lost / factors[:, None]) ** 2, axis=1))]


def half_spectrum_tables():
    moment = np.arange(WIN)
    angle = (moment[:, None] * np.arange(HALF)[None, :] % WIN) * (2.0 * math.pi / WIN)
    nyquist = np.where(moment % 2 == 0, 1.0, -1.0)
    sine = -np.sin(angle)
    sine[:, 0] = nyquist
    forward = np.concatenate([np.cos(angle), sine], axis=1).astype(ml_dtypes.bfloat16)
    inverse = np.concatenate([np.cos(angle), sine], axis=1).T / math.sqrt(WIN)
    inverse[0] *= 0.5
    inverse[HALF] *= 0.5
    source = np.arange(SRC)
    turn = (source[:, None] * source[None, :] % SRC) * (2.0 * math.pi / SRC)
    cosine, sine = np.cos(turn) / math.sqrt(SRC), np.sin(turn) / math.sqrt(SRC)
    onward = np.block([[cosine, sine], [-sine, cosine]])
    source_scale, time_scale = bfloat_scale(onward), bfloat_scale(inverse)
    onward = onward * source_scale
    tables = (
        forward,
        inverse * time_scale,
        np.concatenate([onward, onward], axis=1) / math.sqrt(WIN),
        np.concatenate([onward.T, onward.T], axis=1),
    )
    tables = tuple(table.astype(ml_dtypes.bfloat16) for table in tables)
    return tables, source_scale, 1.0 / (source_scale * source_scale * time_scale)


def rearranging(shape, axes):
    order = np.arange(math.prod(shape)).reshape(shape).transpose(axes).reshape(-1)
    return np.eye(order.size)[order].astype(ml_dtypes.bfloat16)


def order_tables(windows, own):
    shots, sources = TILE // (2 * windows * own), TILE // windows
    return (
        rearranging((shots, windows, 2, own), (0, 3, 2, 1)),
        rearranging((sources, windows), (1, 0)),
        rearranging((windows, sources), (1, 0)),
    )


def halves(value):
    high = value.astype(jnp.bfloat16)
    return high, (value - high.astype(jnp.float32)).astype(jnp.bfloat16)


def product(left, right):
    return jnp.dot(left, right, preferred_element_type=jnp.float32)


def interleaved(*steps):
    steps = list(steps)
    while steps:
        steps = [step for step in steps if next(step, step) is not step]


def gather_kernel(
    shots,
    limit_scale,
    kept_scale,
    delays_far,
    limits_far,
    received,
    tables,
    out,
    delays,
    limits,
    records,
    field,
    firsts,
    estimates,
    sems,
):
    copies = [
        pltpu.make_async_copy(delays_far, delays, sems.at[0]),
        pltpu.make_async_copy(limits_far, limits, sems.at[1]),
    ]
    for copy in copies:
        copy.start()
    forward, inverse, order_arrived, order_windows, order_sources = (
        tables.at[pl.ds(at * TILE, TILE)] for at in range(5)
    )
    onward, backward = (
        tables.at[pl.ds(5 * TILE + at * 2 * SRC, 2 * SRC)] for at in range(2)
    )
    count, receivers, rows, _ = received.shape
    blocks_of_time = count // shots
    experiments, sources = delays.shape[1], SRC
    windows = blocks_of_time * rows * shots // (2 * experiments)
    groups = receivers * windows
    parts = windows // blocks_of_time
    some = TILE // windows
    lane = lax.broadcasted_iota(jnp.int32, (windows, BLK), 1)
    row = lax.broadcasted_iota(jnp.int32, (windows, BLK), 0)
    lane_of_group = lax.broadcasted_iota(jnp.int32, (sources, HALF), 1)
    lane_of_some = lax.broadcasted_iota(jnp.int32, (some, HALF), 1)

    for chunk in range(sources // some):
        senders = slice(chunk * TILE // rows, (chunk + 1) * TILE // rows)
        arrived = [received[senders, r].reshape(TILE, BLK) for r in range(receivers)]
        records[chunk] = product(order_arrived[...], jnp.concatenate(arrived, axis=1))

    for copy in copies:
        copy.wait()

    def advanced(even, odd, delay):
        by = (BLK - delay) & (BLK - 1)
        even, odd = pltpu.roll(even, by, 1), pltpu.roll(odd, by, 1)
        after = jnp.where(row < windows - 1, pltpu.roll(even, windows - 1, 0), 0.0)
        same = lane < BLK - delay
        return jnp.where(same, even, odd), jnp.where(same, odd, after)

    def moved_by(even, odd, ahead_by):
        ahead = ahead_by >= 0
        by = (BLK - ahead_by) & (BLK - 1)
        even, odd = pltpu.roll(even, by, 1), pltpu.roll(odd, by, 1)
        other = pltpu.roll(jnp.where(ahead, even, odd), jnp.where(ahead, windows - 1, 1), 0)
        other = jnp.where(row != jnp.where(ahead, windows - 1, 0), other, 0.0)
        same = ((lane + ahead_by) & -BLK) == 0
        return (
            jnp.where(same, even, jnp.where(ahead, odd, other)),
            jnp.where(same, odd, jnp.where(ahead, other, even)),
        )

    def columns(group, many=1):
        return slice(group * HALF, (group + many) * HALF)

    def first_update(r, chunk):
        updated = []
        for at in range(0, some, SRC_EXP):
            even, odd = (
                records[chunk, pl.ds((at + half) * windows, windows), columns(r)]
                for half in range(2)
            )
            for k in range(SRC_EXP):
                early = advanced(even, odd, delays[k, (chunk * some + at) // SRC_EXP])
                updated.append(jnp.concatenate([RELAX * x for x in early], axis=1))
        updated = jnp.concatenate(updated, axis=0).astype(jnp.bfloat16)
        firsts[pl.ds((r * sources + chunk * some) * windows, TILE), :] = updated
        return updated

    def later_update(r, chunk):
        before = [
            estimates[pl.ds((r * windows + w) * sources + chunk * some, some), :]
            for w in range(windows)
        ]
        before = product(order_sources[...], jnp.concatenate(before, axis=0))
        first = (r * sources + chunk * some) * windows
        updated = []
        for at in range(0, some, SRC_EXP):
            lags = [delays[k, (chunk * some + at) // SRC_EXP] for k in range(SRC_EXP)]
            spread = firsts[pl.ds(first + at * windows, SRC_EXP * windows), :]
            spread = spread.astype(jnp.float32)
            estimate = [
                tuple(
                    before[(at + k) * windows : (at + k + 1) * windows, columns(half)]
                    for half in range(2)
                )
                for k in range(SRC_EXP)
            ]
            for k in range(SRC_EXP):
                even, odd = estimate[k]
                other = moved_by(*estimate[1 - k], lags[k] - lags[1 - k])
                stays = (row < windows - 1) | (lane < BLK - lags[k])
                even = RELAX * (even - other[0])
                odd = jnp.where(stays, RELAX * (odd - other[1]), odd)
                step = spread[k * windows : (k + 1) * windows]
                updated.append(jnp.concatenate([even, odd], axis=1) + step)
        return jnp.concatenate(updated, axis=0).astype(jnp.bfloat16)

    def parts_of(real, imag):
        real_high, real_low = halves(real)
        imag_high, imag_low = halves(imag)
        return real_high, imag_high, real_low, imag_low

    def put(r, where, real, imag, first):
        for at, value in enumerate(parts_of(real, imag)):
            start = at * sources + first
            field[r, start : start + value.shape[0], where] = value

    def onward_steps(sweep, r):
        update = later_update if sweep else first_update
        for chunk in range(sources // some):
            updated = update(r, chunk)
            yield
            signal = product(order_windows[...], updated).astype(jnp.bfloat16)
            yield
            spectra = product(signal, forward[...])
            yield
            nyquist = jnp.zeros((some, HALF), jnp.float32)
            for w in range(windows):
                spectrum = spectra[w * some : (w + 1) * some]
                real, imag = spectrum[:, :HALF], spectrum[:, HALF:]
                moved = pltpu.roll(imag, w, 1) if w else imag
                nyquist = jnp.where(lane_of_some == w, moved, nyquist)
                imag = jnp.where(lane_of_some == 0, 0.0, imag)
                put(r, columns(w), real, imag, chunk * some)
            put(r, columns(windows), nyquist, jnp.zeros_like(nyquist), chunk * some)
            yield

    def bounds_of(sweep):
        limit = limits[sweep : sweep + 1, :] * (limit_scale * kept_scale)
        p = lax.broadcasted_iota(jnp.int32, (sources, sources), 0)
        q = lax.broadcasted_iota(jnp.int32, (sources, sources), 1)
        mirrored = (p + q == 0) | (p + q == sources)
        return [
            jnp.sum(jnp.where(at, limit, 0.0), axis=1, keepdims=True) for at in (p == q, mirrored)
        ]

    def shrunk(bounds, real, imag):
        inverse_size = lax.rsqrt(real * real + imag * imag)
        factor = sum(jnp.maximum(kept_scale - bound * inverse_size, 0.0) for bound in bounds)
        return jnp.concatenate(parts_of(real * factor, imag * factor), axis=0)

    def backward_steps(sweep, r):
        nyquist = None
        for first in (windows, *range(0, windows, 2)):
            coefficients = product(onward[...], field[r, :, columns(first, min(2, windows + 1 - first))])
            yield
            kept = shrunk(bounds[sweep], coefficients[:sources], coefficients[sources:])
            yield
            mixed = product(backward[...], kept)
            yield
            if nyquist is None:
                nyquist = mixed[:sources]
                continue
            pieces = []
            for w in (first, first + 1):
                real, imag = (
                    mixed[part * sources : (part + 1) * sources, columns(w - first)]
                    for part in range(2)
                )
                moved = pltpu.roll(nyquist, HALF - w, 1) if w else nyquist
                imag = jnp.where(lane_of_group == 0, moved, imag)
                pieces.append(jnp.concatenate([real, imag], axis=1).astype(jnp.bfloat16))
            restored = product(jnp.concatenate(pieces, axis=0), inverse[...])
            yield
            if sweep < ITERS - 1:
                start = (r * windows + first) * sources
                estimates[start : start + 2 * sources, :] = restored.astype(jnp.bfloat16)
            else:
                deliver(r, first, restored)
            yield

    def swapped(value):
        return pltpu.roll(value, SUB // 2, 1)

    def deliver(r, w, restored):
        low = lax.broadcasted_iota(jnp.int32, (sources // SUB, SUB, BLK), 1) < SUB // 2
        pieces = []
        for part in range(2):
            window = restored[part * sources : (part + 1) * sources]
            even = window[:, :BLK].reshape(sources // SUB, SUB, BLK)
            odd = window[:, BLK:].reshape(sources // SUB, SUB, BLK)
            pieces.append(
                (jnp.where(low, even, swapped(odd)), jnp.where(low, swapped(even), odd))
            )
        block, inside = w // parts, w % parts
        for side in range(2):
            both = jnp.concatenate([pieces[0][side], pieces[1][side]], axis=1)
            both = both.astype(jnp.bfloat16)
            for k in range(sources // SUB):
                target = (2 * k + side) * blocks_of_time + block
                out[target, r, inside * SUB : (inside + 2) * SUB, :] = both[k]

    bounds = [bounds_of(sweep) for sweep in range(ITERS)]
    turns = [(sweep, r) for sweep in range(ITERS) for r in range(receivers)]
    interleaved(onward_steps(*turns[0]))
    for before, after in zip(turns, turns[1:]):
        if receivers > 1:
            interleaved(onward_steps(*after), backward_steps(*before))
        else:
            interleaved(backward_steps(*before))
            interleaved(onward_steps(*after))
    interleaved(backward_steps(*turns[-1]))


def cast_kernel(blended, sent, held, sems):
    pieces = sems.shape[0]
    count = blended.shape[0] // pieces
    spans = [pl.ds(at * count, count) for at in range(pieces)]
    copies = [
        pltpu.make_async_copy(blended.at[span], held.at[span], sems.at[at])
        for at, span in enumerate(spans)
    ]
    for copy in copies:
        copy.start()
    for copy, span in zip(copies, spans):
        copy.wait()
        sent[span] = held[span].astype(jnp.bfloat16)


def gathers_of_all_samples(shots, blended, delays, thresholds):
    receivers, own, samples = blended.shape
    blocks_of_time = lax.axis_size("tm")
    count = shots * blocks_of_time
    each = receivers // count
    blocks = samples // BLK
    windows = samples * blocks_of_time // WIN
    groups = each * windows
    rows = blocks * own
    sent = blended.reshape(receivers, own, blocks, BLK).transpose(0, 2, 1, 3)
    sent = sent.reshape(count, each, rows, BLK)
    vmem, far = pl.BlockSpec(memory_space=pltpu.VMEM), pl.BlockSpec(memory_space=pl.ANY)

    def kept_far(array):
        return pltpu.with_memory_space_constraint(array, pltpu.HBM)

    sent = pl.pallas_call(
        cast_kernel,
        out_shape=jax.ShapeDtypeStruct(sent.shape, jnp.bfloat16),
        in_specs=[far],
        out_specs=vmem,
        scratch_shapes=[pltpu.VMEM(sent.shape, jnp.float32), pltpu.SemaphoreType.DMA((4,))],
        compiler_params=pltpu.CompilerParams(vmem_limit_bytes=8 * 1024 * 1024),
    )(kept_far(sent))
    received = lax.all_to_all(sent, ("shot", "tm"), split_axis=0, concat_axis=0, tiled=True)
    tables, limit_scale, kept_scale = half_spectrum_tables()
    tables = np.concatenate(tables[:2] + order_tables(windows, own) + tables[2:], axis=0)
    held = SRC // shots
    restored = pl.pallas_call(
        functools.partial(gather_kernel, shots, float(limit_scale), float(kept_scale)),
        out_shape=jax.ShapeDtypeStruct((count, each, blocks * held, BLK), jnp.bfloat16),
        in_specs=[far] * 2 + [vmem] * 2,
        out_specs=vmem,
        scratch_shapes=[
            pltpu.SMEM(delays.T.shape, jnp.int32),
            pltpu.VMEM(thresholds.shape, jnp.float32),
            pltpu.VMEM((SRC * windows // TILE, TILE, each * BLK), jnp.float32),
            pltpu.VMEM((each, 4 * SRC, (windows + 1) * HALF), jnp.bfloat16),
            pltpu.VMEM((groups * SRC, WIN), jnp.bfloat16),
            pltpu.VMEM((groups * SRC, WIN), jnp.bfloat16),
            pltpu.SemaphoreType.DMA((2,)),
        ],
        compiler_params=pltpu.CompilerParams(vmem_limit_bytes=40 * 1024 * 1024),
        cost_estimate=pl.CostEstimate(
            flops=2 * ITERS * groups * SRC * WIN * WIN * 5,
            bytes_accessed=2 * 1024 * 1024,
            transcendentals=ITERS * groups * SRC * HALF,
        ),
    )(kept_far(delays.T), kept_far(thresholds), received, jnp.asarray(tables))
    final = lax.all_to_all(restored, ("shot", "tm"), split_axis=0, concat_axis=0, tiled=True)
    final = final.reshape(receivers, blocks, held, BLK).transpose(0, 2, 1, 3)
    return final.reshape(receivers, held, samples)


def shifted(array, axis, by):
    count = lax.axis_size(axis)
    pairs = [(i, i + by) for i in range(count) if 0 <= i + by < count]
    return lax.ppermute(array, axis, pairs)


def phase_table(length_first, length_second, period):
    first_index = jnp.arange(length_first, dtype=jnp.int32)[:, None]
    second_index = jnp.arange(length_second, dtype=jnp.int32)[None, :]
    return (first_index * second_index % period).astype(jnp.float32) * (2.0 * math.pi / period)


def make_tables():
    time_angle = phase_table(WIN, WIN, WIN)
    time_scale = 1.0 / math.sqrt(WIN)
    cos_forward = jnp.cos(time_angle).astype(jnp.bfloat16)
    sin_forward = -jnp.sin(time_angle).astype(jnp.bfloat16)
    cos_inverse = jnp.cos(time_angle) * time_scale
    sin_inverse = -jnp.sin(time_angle) * time_scale
    source_angle = phase_table(SRC, SRC, SRC)
    cos_source = jnp.cos(source_angle) / math.sqrt(SRC)
    sin_source = jnp.sin(source_angle) / math.sqrt(SRC)
    return (cos_forward, sin_forward, cos_inverse, sin_inverse, cos_source, sin_source)


def blend(estimate, own_delays):
    receivers, sources, samples = estimate.shape
    blocks = samples // BLK
    experiments = sources // SRC_EXP
    earlier = shifted(estimate[:, :, samples - BLK :], "tm", 1)
    upper = estimate.reshape(receivers, sources, blocks, BLK)
    shifts = own_delays.reshape(-1)
    row_index = jnp.arange(BLK, dtype=jnp.int32)[None, :, None]
    column_index = jnp.arange(BLK, dtype=jnp.int32)[None, None, :]
    select_same = (row_index == column_index - shifts[:, None, None]).astype(jnp.bfloat16)
    select_prior = (row_index == BLK + column_index - shifts[:, None, None]).astype(jnp.bfloat16)
    same = jnp.einsum("rsnb,sbi->rsni", upper, select_same, preferred_element_type=jnp.float32)
    onward = jnp.einsum("rsnb,sbi->rsni", upper, select_prior, preferred_element_type=jnp.float32)
    edge_part = jnp.einsum(
        "rsb,sbi->rsi", earlier, select_prior, preferred_element_type=jnp.float32
    )
    same = jnp.sum(same.reshape(receivers, experiments, SRC_EXP, blocks, BLK), axis=2)
    onward = jnp.sum(onward.reshape(receivers, experiments, SRC_EXP, blocks, BLK), axis=2)
    edge_part = jnp.sum(edge_part.reshape(receivers, experiments, SRC_EXP, BLK), axis=2)
    carried = jnp.concatenate([edge_part[:, :, None], onward[:, :, : blocks - 1]], axis=2)
    return (same + carried).reshape(receivers, experiments, samples)


def spread(residual, own_delays):
    receivers, experiments, samples = residual.shape
    blocks = samples // BLK
    later = shifted(residual[:, :, :BLK], "tm", -1)
    lower = residual.reshape(receivers, experiments, blocks, BLK)
    row_index = jnp.arange(BLK, dtype=jnp.int32)[None, None, :, None]
    column_index = jnp.arange(BLK, dtype=jnp.int32)[None, None, None, :]
    select_same = (row_index == column_index + own_delays[:, :, None, None]).astype(jnp.bfloat16)
    select_next = (row_index + BLK == column_index + own_delays[:, :, None, None]).astype(
        jnp.bfloat16
    )
    same = jnp.einsum("rena,ekai->rekni", lower, select_same, preferred_element_type=jnp.float32)
    backward = jnp.einsum(
        "rena,ekai->rekni", lower, select_next, preferred_element_type=jnp.float32
    )
    edge_part = jnp.einsum("rea,ekai->reki", later, select_next, preferred_element_type=jnp.float32)
    carried = jnp.concatenate([backward[:, :, :, 1:], edge_part[:, :, :, None]], axis=3)
    return (same + carried).reshape(receivers, experiments * SRC_EXP, samples)


def coherence(gathers, limits, tables):
    cos_forward, sin_forward, cos_inverse, sin_inverse, cos_source, sin_source = tables
    receivers, sources, samples = gathers.shape
    windows = samples // WIN
    careful = lax.Precision.HIGH
    scale = 1.0 / math.sqrt(WIN)
    signal = gathers.reshape(receivers * sources * windows, WIN)
    real_time = (jnp.dot(signal, cos_forward, preferred_element_type=jnp.float32) * scale).reshape(
        receivers, sources, samples
    )
    imag_time = (jnp.dot(signal, sin_forward, preferred_element_type=jnp.float32) * scale).reshape(
        receivers, sources, samples
    )

    def mixing(table, field):
        return jnp.einsum(
            "ps,rsx->rpx", table, field, precision=careful, preferred_element_type=jnp.float32
        )

    real_part = mixing(cos_source, real_time) + mixing(sin_source, imag_time)
    imag_part = mixing(cos_source, imag_time) - mixing(sin_source, real_time)
    magnitude = jnp.sqrt(real_part * real_part + imag_part * imag_part)
    bound = limits[None, :, None]
    factor = jnp.maximum(magnitude - bound, 0.0) / jnp.maximum(magnitude, bound)
    kept_real = real_part * factor
    kept_imag = imag_part * factor
    back_real = mixing(cos_source, kept_real) - mixing(sin_source, kept_imag)
    back_imag = mixing(cos_source, kept_imag) + mixing(sin_source, kept_real)
    restored = jnp.dot(
        back_real.reshape(-1, WIN),
        cos_inverse,
        precision=careful,
        preferred_element_type=jnp.float32,
    )
    restored = restored + jnp.dot(
        back_imag.reshape(-1, WIN),
        sin_inverse,
        precision=careful,
        preferred_element_type=jnp.float32,
    )
    return restored.reshape(receivers, sources, samples)


def gathers_of_own_samples(blended, delays, thresholds):
    tables = make_tables()
    local_count = blended.shape[1]
    own_delays = lax.dynamic_slice_in_dim(
        delays, lax.axis_index("shot") * local_count, local_count, 0
    )
    estimate = None
    for sweep in range(ITERS):
        if sweep == 0:
            residual = blended.astype(jnp.bfloat16)
            update = (RELAX * spread(residual, own_delays)).astype(jnp.bfloat16)
        else:
            residual = (blended - blend(estimate, own_delays)).astype(jnp.bfloat16)
            update = (estimate.astype(jnp.float32) + RELAX * spread(residual, own_delays)).astype(
                jnp.bfloat16
            )
        gathers = lax.all_to_all(update, "shot", split_axis=0, concat_axis=1, tiled=True)
        filtered = coherence(gathers, thresholds[sweep], tables).astype(jnp.bfloat16)
        estimate = lax.all_to_all(filtered, "shot", split_axis=1, concat_axis=0, tiled=True)
    return estimate


def whole_receivers_fit(shots, blocks_of_time, receivers, samples):
    held, windows = SRC // shots, samples // WIN
    return (
        receivers % (shots * blocks_of_time) == 0
        and held * 2 == SUB
        and windows % 2 == 0
        and windows * blocks_of_time == SUB
        and receivers // (shots * blocks_of_time) * SUB <= HALF
    )


def local(blended, delays, thresholds):
    shots, blocks_of_time = lax.axis_size("shot"), lax.axis_size("tm")
    if whole_receivers_fit(shots, blocks_of_time, blended.shape[0], blended.shape[2]):
        return gathers_of_all_samples(shots, blended, delays, thresholds)
    return gathers_of_own_samples(blended, delays, thresholds)


def solution(mesh):
    return jax.shard_map(
        local,
        mesh=mesh,
        in_specs=(P(None, "shot", "tm"), P(), P()),
        out_specs=P(None, "shot", "tm"),
        check_vma=False,
    )
```

```python
import functools
import math

import jax
import jax.numpy as jnp
import ml_dtypes
import numpy as np
from jax import lax
from jax.experimental import pallas as pl
from jax.experimental.pallas import tpu as pltpu
from jax.sharding import PartitionSpec as P

SRC = 64
SRC_EXP = 2
WIN = 256
BLK = 128
ITERS = 2


RELAX = 0.5
HALF = WIN // 2
SUB = 8
TILE = 256


def bfloat_scale(table):
    values = np.unique(np.abs(table).round(12))
    factors = 1.0 + np.arange(4096) / 4096.0
    scaled = factors[:, None] * values
    lost = scaled.astype(ml_dtypes.bfloat16).astype(np.float64) - scaled
    return factors[np.argmin(np.sum((lost / factors[:, None]) ** 2, axis=1))]


def half_spectrum_tables():
    moment = np.arange(WIN)
    angle = (moment[:, None] * np.arange(HALF)[None, :] % WIN) * (2.0 * math.pi / WIN)
    nyquist = np.where(moment % 2 == 0, 1.0, -1.0)
    sine = -np.sin(angle)
    sine[:, 0] = nyquist
    forward = np.concatenate([np.cos(angle), sine], axis=1).astype(ml_dtypes.bfloat16)
    inverse = np.concatenate([np.cos(angle), sine], axis=1).T / math.sqrt(WIN)
    inverse[0] *= 0.5
    inverse[HALF] *= 0.5
    source = np.arange(SRC)
    turn = (source[:, None] * source[None, :] % SRC) * (2.0 * math.pi / SRC)
    cosine, sine = np.cos(turn) / math.sqrt(SRC), np.sin(turn) / math.sqrt(SRC)
    onward = np.block([[cosine, sine], [-sine, cosine]])
    source_scale, time_scale = bfloat_scale(onward), bfloat_scale(inverse)
    onward = onward * source_scale
    tables = (
        forward,
        inverse * time_scale,
        np.concatenate([onward, onward], axis=1) / math.sqrt(WIN),
        np.concatenate([onward.T, onward.T], axis=1),
    )
    tables = tuple(table.astype(ml_dtypes.bfloat16) for table in tables)
    return tables, source_scale, 1.0 / (source_scale * source_scale * time_scale)


def rearranging(shape, axes):
    order = np.arange(math.prod(shape)).reshape(shape).transpose(axes).reshape(-1)
    return np.eye(order.size)[order].astype(ml_dtypes.bfloat16)


def order_tables(windows, own):
    shots, sources = TILE // (2 * windows * own), TILE // windows
    return (
        rearranging((shots, windows, 2, own), (0, 3, 2, 1)),
        rearranging((sources, windows), (1, 0)),
        rearranging((windows, sources), (1, 0)),
    )


def halves(value):
    high = value.astype(jnp.bfloat16)
    return high, (value - high.astype(jnp.float32)).astype(jnp.bfloat16)


def product(left, right):
    return jnp.dot(left, right, preferred_element_type=jnp.float32)


def gather_kernel(
    shots,
    limit_scale,
    kept_scale,
    delays_far,
    limits,
    received,
    tables,
    out,
    delays,
    records,
    field,
    mixed,
    back,
    firsts,
    estimates,
    sem,
):
    copy = pltpu.make_async_copy(delays_far, delays, sem)
    copy.start()
    forward, inverse, order_arrived, order_windows, order_sources = (
        tables.at[pl.ds(at * TILE, TILE)] for at in range(5)
    )
    onward, backward = (
        tables.at[pl.ds(5 * TILE + at * 2 * SRC, 2 * SRC)] for at in range(2)
    )
    count, receivers, rows, _ = received.shape
    blocks_of_time = count // shots
    experiments, sources = delays.shape[1], SRC
    windows = blocks_of_time * rows * shots // (2 * experiments)
    groups = receivers * windows
    parts = windows // blocks_of_time
    some = TILE // windows
    lane = lax.broadcasted_iota(jnp.int32, (windows, BLK), 1)
    row = lax.broadcasted_iota(jnp.int32, (windows, BLK), 0)
    lane_of_group = lax.broadcasted_iota(jnp.int32, (sources, HALF), 1)
    lane_of_some = lax.broadcasted_iota(jnp.int32, (some, HALF), 1)

    arrived = [
        received[slice(chunk * TILE // rows, (chunk + 1) * TILE // rows), r].reshape(TILE, BLK)
        for chunk in range(sources // some)
        for r in range(receivers)
    ]
    records[...] = product(order_arrived[...], jnp.concatenate(arrived, axis=1))

    copy.wait()

    def advanced(even, odd, delay):
        by = (BLK - delay) & (BLK - 1)
        even, odd = pltpu.roll(even, by, 1), pltpu.roll(odd, by, 1)
        after = jnp.where(row < windows - 1, pltpu.roll(even, windows - 1, 0), 0.0)
        same = lane < BLK - delay
        return jnp.where(same, even, odd), jnp.where(same, odd, after)

    def moved_by(even, odd, ahead_by):
        ahead = ahead_by >= 0
        by = (BLK - ahead_by) & (BLK - 1)
        even, odd = pltpu.roll(even, by, 1), pltpu.roll(odd, by, 1)
        other = pltpu.roll(jnp.where(ahead, even, odd), jnp.where(ahead, windows - 1, 1), 0)
        other = jnp.where(row != jnp.where(ahead, windows - 1, 0), other, 0.0)
        same = ((lane + ahead_by) & -BLK) == 0
        return (
            jnp.where(same, even, jnp.where(ahead, odd, other)),
            jnp.where(same, odd, jnp.where(ahead, other, even)),
        )

    def columns(group):
        return slice(group * HALF, (group + 1) * HALF)

    def first_update(r, chunk):
        updated = []
        for at in range(0, some, SRC_EXP):
            even, odd = (
                records[pl.ds((at + half) * windows, windows), columns(chunk * receivers + r)]
                for half in range(2)
            )
            for k in range(SRC_EXP):
                early = advanced(even, odd, delays[k, (chunk * some + at) // SRC_EXP])
                updated.append(jnp.concatenate([RELAX * x for x in early], axis=1))
        updated = jnp.concatenate(updated, axis=0).astype(jnp.bfloat16)
        firsts[pl.ds((r * sources + chunk * some) * windows, TILE), :] = updated
        return updated

    def side_by_side(values):
        return jnp.concatenate(values, axis=1)

    def estimates_by_source():
        parts_of_rows = []
        for r, chunk in turns:
            starts = [(r * windows + w) * sources + chunk * some for w in range(windows)]
            rows_of_part = [estimates[start : start + some, :] for start in starts]
            parts_of_rows.append(jnp.concatenate(rows_of_part, axis=0))
        return product(order_sources[...], side_by_side(parts_of_rows))

    def later_update(r, chunk, before):
        first = (r * sources + chunk * some) * windows
        updated = []
        for at in range(0, some, SRC_EXP):
            lags = [delays[k, (chunk * some + at) // SRC_EXP] for k in range(SRC_EXP)]
            spread = firsts[pl.ds(first + at * windows, SRC_EXP * windows), :]
            spread = spread.astype(jnp.float32)
            estimate = [
                tuple(
                    before[(at + k) * windows : (at + k + 1) * windows, columns(half)]
                    for half in range(2)
                )
                for k in range(SRC_EXP)
            ]
            for k in range(SRC_EXP):
                even, odd = estimate[k]
                other = moved_by(*estimate[1 - k], lags[k] - lags[1 - k])
                stays = (row < windows - 1) | (lane < BLK - lags[k])
                even = RELAX * (even - other[0])
                odd = jnp.where(stays, RELAX * (odd - other[1]), odd)
                step = spread[k * windows : (k + 1) * windows]
                updated.append(jnp.concatenate([even, odd], axis=1) + step)
        return jnp.concatenate(updated, axis=0).astype(jnp.bfloat16)

    turns = [(r, chunk) for r in range(receivers) for chunk in range(sources // some)]

    def update_and_forward_in_time(sweep):
        if sweep:
            before = estimates_by_source()
            updates = [
                later_update(r, chunk, before[:, at * WIN : (at + 1) * WIN])
                for at, (r, chunk) in enumerate(turns)
            ]
        else:
            updates = [first_update(r, chunk) for r, chunk in turns]
        signal = product(order_windows[...], side_by_side(updates)).astype(jnp.bfloat16)
        signal = [signal[:, at * WIN : (at + 1) * WIN] for at in range(len(turns))]
        spectra = product(jnp.concatenate(signal, axis=0), forward[...])
        nyquists = [jnp.zeros((some, HALF), jnp.float32) for _ in range(sources // some)]
        for at, (r, chunk) in enumerate(turns):
            for w in range(windows):
                group = r * windows + w
                start = at * TILE + w * some
                real, imag = (spectra[start : start + some, columns(half)] for half in range(2))
                moved = pltpu.roll(imag, group, 1) if group else imag
                nyquists[chunk] = jnp.where(lane_of_some == group, moved, nyquists[chunk])
                imag = jnp.where(lane_of_some == 0, 0.0, imag)
                put(field, columns(group), real, imag, chunk * some)
        for chunk, nyquist in enumerate(nyquists):
            put(field, columns(groups), nyquist, jnp.zeros_like(nyquist), chunk * some)

    def put(ref, where, real, imag, first=0):
        real_high, real_low = halves(real)
        imag_high, imag_low = halves(imag)
        for at, value in enumerate((real_high, imag_high, real_low, imag_low)):
            start = at * sources + first
            ref[start : start + value.shape[0], where] = value

    def mixing(table, ref):
        total = product(table[...], ref[...])
        return total[:sources], total[sources:]

    def shrink(sweep):
        limit = limits[sweep : sweep + 1, :] * (limit_scale * kept_scale)
        p = lax.broadcasted_iota(jnp.int32, (sources, sources), 0)
        q = lax.broadcasted_iota(jnp.int32, (sources, sources), 1)
        bound = jnp.sum(jnp.where(p == q, limit, 0.0), axis=1, keepdims=True)
        mirrored = (p + q == 0) | (p + q == sources)
        bound_mirrored = jnp.sum(jnp.where(mirrored, limit, 0.0), axis=1, keepdims=True)
        real, imag = mixing(onward, field)
        inverse_size = lax.rsqrt(real * real + imag * imag)
        factor = jnp.maximum(kept_scale - bound * inverse_size, 0.0) + jnp.maximum(
            kept_scale - bound_mirrored * inverse_size, 0.0
        )
        put(mixed, slice(None), real * factor, imag * factor)

    def back_in_source():
        real, imag = mixing(backward, mixed)
        nyquist = real[:, columns(groups)]
        for group in range(groups):
            moved = pltpu.roll(nyquist, HALF - group, 1) if group else nyquist
            own_imag = jnp.where(lane_of_group == 0, moved, imag[:, columns(group)])
            rows_of_group = slice(group * sources, (group + 1) * sources)
            for half, value in enumerate((real[:, columns(group)], own_imag)):
                back[rows_of_group, columns(half)] = value.astype(jnp.bfloat16)

    def swapped(value):
        return pltpu.roll(value, SUB // 2, 1)

    def deliver(r, w, restored):
        low = lax.broadcasted_iota(jnp.int32, (sources // SUB, SUB, BLK), 1) < SUB // 2
        pieces = []
        for part in range(2):
            window = restored[part * sources : (part + 1) * sources]
            even = window[:, :BLK].reshape(sources // SUB, SUB, BLK)
            odd = window[:, BLK:].reshape(sources // SUB, SUB, BLK)
            pieces.append(
                (jnp.where(low, even, swapped(odd)), jnp.where(low, swapped(even), odd))
            )
        block, inside = w // parts, w % parts
        for side in range(2):
            both = jnp.concatenate([pieces[0][side], pieces[1][side]], axis=1)
            both = both.astype(jnp.bfloat16)
            for k in range(sources // SUB):
                target = (2 * k + side) * blocks_of_time + block
                out[target, r, inside * SUB : (inside + 2) * SUB, :] = both[k]

    for sweep in range(ITERS):
        update_and_forward_in_time(sweep)
        shrink(sweep)
        back_in_source()
        restored = product(back[...], inverse[...])
        if sweep < ITERS - 1:
            estimates[...] = restored.astype(jnp.bfloat16)
            continue
        for group in range(0, groups, 2):
            pair = restored[group * sources : (group + 2) * sources]
            deliver(group // windows, group % windows, pair)


def cast_kernel(blended, delays, limits, sent, delays_near, limits_near, held, sems):
    pieces = sems.shape[0] - 2
    count = blended.shape[0] // pieces
    spans = [pl.ds(at * count, count) for at in range(pieces)]
    copies = [
        pltpu.make_async_copy(blended.at[span], held.at[span], sems.at[at])
        for at, span in enumerate(spans)
    ]
    small = [
        pltpu.make_async_copy(delays, delays_near, sems.at[pieces]),
        pltpu.make_async_copy(limits, limits_near, sems.at[pieces + 1]),
    ]
    for copy in copies + small:
        copy.start()
    for copy, span in zip(copies, spans):
        copy.wait()
        sent[span] = held[span].astype(jnp.bfloat16)
    for copy in small:
        copy.wait()


def gathers_of_all_samples(shots, blended, delays, thresholds):
    receivers, own, samples = blended.shape
    blocks_of_time = lax.axis_size("tm")
    count = shots * blocks_of_time
    each = receivers // count
    blocks = samples // BLK
    windows = samples * blocks_of_time // WIN
    groups = each * windows
    rows = blocks * own
    sent = blended.reshape(receivers, own, blocks, BLK).transpose(0, 2, 1, 3)
    sent = sent.reshape(count, each, rows, BLK)
    vmem, far = pl.BlockSpec(memory_space=pltpu.VMEM), pl.BlockSpec(memory_space=pl.ANY)

    def kept_far(array):
        return pltpu.with_memory_space_constraint(array, pltpu.HBM)

    sent, delays, thresholds = pl.pallas_call(
        cast_kernel,
        out_shape=(
            jax.ShapeDtypeStruct(sent.shape, jnp.bfloat16),
            jax.ShapeDtypeStruct(delays.T.shape, delays.dtype),
            jax.ShapeDtypeStruct(thresholds.shape, thresholds.dtype),
        ),
        in_specs=[far] * 3,
        out_specs=[vmem] * 3,
        scratch_shapes=[
            pltpu.VMEM(sent.shape, jnp.float32),
            pltpu.SemaphoreType.DMA((4 + 2,)),
        ],
        compiler_params=pltpu.CompilerParams(vmem_limit_bytes=8 * 1024 * 1024),
    )(kept_far(sent), kept_far(delays.T), kept_far(thresholds))
    received = lax.all_to_all(sent, ("shot", "tm"), split_axis=0, concat_axis=0, tiled=True)
    tables, limit_scale, kept_scale = half_spectrum_tables()
    tables = np.concatenate(tables[:2] + order_tables(windows, own) + tables[2:], axis=0)
    held = SRC // shots
    restored = pl.pallas_call(
        functools.partial(gather_kernel, shots, float(limit_scale), float(kept_scale)),
        out_shape=jax.ShapeDtypeStruct((count, each, blocks * held, BLK), jnp.bfloat16),
        in_specs=[pl.BlockSpec(memory_space=pl.ANY)] + [vmem] * 3,
        out_specs=vmem,
        scratch_shapes=[
            pltpu.SMEM(delays.shape, jnp.int32),
            pltpu.VMEM((TILE, SRC * windows // TILE * each * BLK), jnp.float32),
            pltpu.VMEM((4 * SRC, (groups + 1) * HALF), jnp.bfloat16),
            pltpu.VMEM((4 * SRC, (groups + 1) * HALF), jnp.bfloat16),
            pltpu.VMEM((groups * SRC, WIN), jnp.bfloat16),
            pltpu.VMEM((groups * SRC, WIN), jnp.bfloat16),
            pltpu.VMEM((groups * SRC, WIN), jnp.bfloat16),
            pltpu.SemaphoreType.DMA(()),
        ],
        compiler_params=pltpu.CompilerParams(vmem_limit_bytes=40 * 1024 * 1024),
        cost_estimate=pl.CostEstimate(
            flops=2 * ITERS * groups * SRC * WIN * WIN * 5,
            bytes_accessed=2 * 1024 * 1024,
            transcendentals=ITERS * groups * SRC * HALF,
        ),
    )(delays, thresholds, received, jnp.asarray(tables))
    final = lax.all_to_all(restored, ("shot", "tm"), split_axis=0, concat_axis=0, tiled=True)
    final = final.reshape(receivers, blocks, held, BLK).transpose(0, 2, 1, 3)
    return final.reshape(receivers, held, samples)


def shifted(array, axis, by):
    count = lax.axis_size(axis)
    pairs = [(i, i + by) for i in range(count) if 0 <= i + by < count]
    return lax.ppermute(array, axis, pairs)


def phase_table(length_first, length_second, period):
    first_index = jnp.arange(length_first, dtype=jnp.int32)[:, None]
    second_index = jnp.arange(length_second, dtype=jnp.int32)[None, :]
    return (first_index * second_index % period).astype(jnp.float32) * (2.0 * math.pi / period)


def make_tables():
    time_angle = phase_table(WIN, WIN, WIN)
    time_scale = 1.0 / math.sqrt(WIN)
    cos_forward = jnp.cos(time_angle).astype(jnp.bfloat16)
    sin_forward = -jnp.sin(time_angle).astype(jnp.bfloat16)
    cos_inverse = jnp.cos(time_angle) * time_scale
    sin_inverse = -jnp.sin(time_angle) * time_scale
    source_angle = phase_table(SRC, SRC, SRC)
    cos_source = jnp.cos(source_angle) / math.sqrt(SRC)
    sin_source = jnp.sin(source_angle) / math.sqrt(SRC)
    return (cos_forward, sin_forward, cos_inverse, sin_inverse, cos_source, sin_source)


def blend(estimate, own_delays):
    receivers, sources, samples = estimate.shape
    blocks = samples // BLK
    experiments = sources // SRC_EXP
    earlier = shifted(estimate[:, :, samples - BLK :], "tm", 1)
    upper = estimate.reshape(receivers, sources, blocks, BLK)
    shifts = own_delays.reshape(-1)
    row_index = jnp.arange(BLK, dtype=jnp.int32)[None, :, None]
    column_index = jnp.arange(BLK, dtype=jnp.int32)[None, None, :]
    select_same = (row_index == column_index - shifts[:, None, None]).astype(jnp.bfloat16)
    select_prior = (row_index == BLK + column_index - shifts[:, None, None]).astype(jnp.bfloat16)
    same = jnp.einsum("rsnb,sbi->rsni", upper, select_same, preferred_element_type=jnp.float32)
    onward = jnp.einsum("rsnb,sbi->rsni", upper, select_prior, preferred_element_type=jnp.float32)
    edge_part = jnp.einsum(
        "rsb,sbi->rsi", earlier, select_prior, preferred_element_type=jnp.float32
    )
    same = jnp.sum(same.reshape(receivers, experiments, SRC_EXP, blocks, BLK), axis=2)
    onward = jnp.sum(onward.reshape(receivers, experiments, SRC_EXP, blocks, BLK), axis=2)
    edge_part = jnp.sum(edge_part.reshape(receivers, experiments, SRC_EXP, BLK), axis=2)
    carried = jnp.concatenate([edge_part[:, :, None], onward[:, :, : blocks - 1]], axis=2)
    return (same + carried).reshape(receivers, experiments, samples)


def spread(residual, own_delays):
    receivers, experiments, samples = residual.shape
    blocks = samples // BLK
    later = shifted(residual[:, :, :BLK], "tm", -1)
    lower = residual.reshape(receivers, experiments, blocks, BLK)
    row_index = jnp.arange(BLK, dtype=jnp.int32)[None, None, :, None]
    column_index = jnp.arange(BLK, dtype=jnp.int32)[None, None, None, :]
    select_same = (row_index == column_index + own_delays[:, :, None, None]).astype(jnp.bfloat16)
    select_next = (row_index + BLK == column_index + own_delays[:, :, None, None]).astype(
        jnp.bfloat16
    )
    same = jnp.einsum("rena,ekai->rekni", lower, select_same, preferred_element_type=jnp.float32)
    backward = jnp.einsum(
        "rena,ekai->rekni", lower, select_next, preferred_element_type=jnp.float32
    )
    edge_part = jnp.einsum("rea,ekai->reki", later, select_next, preferred_element_type=jnp.float32)
    carried = jnp.concatenate([backward[:, :, :, 1:], edge_part[:, :, :, None]], axis=3)
    return (same + carried).reshape(receivers, experiments * SRC_EXP, samples)


def coherence(gathers, limits, tables):
    cos_forward, sin_forward, cos_inverse, sin_inverse, cos_source, sin_source = tables
    receivers, sources, samples = gathers.shape
    windows = samples // WIN
    careful = lax.Precision.HIGH
    scale = 1.0 / math.sqrt(WIN)
    signal = gathers.reshape(receivers * sources * windows, WIN)
    real_time = (jnp.dot(signal, cos_forward, preferred_element_type=jnp.float32) * scale).reshape(
        receivers, sources, samples
    )
    imag_time = (jnp.dot(signal, sin_forward, preferred_element_type=jnp.float32) * scale).reshape(
        receivers, sources, samples
    )

    def mixing(table, field):
        return jnp.einsum(
            "ps,rsx->rpx", table, field, precision=careful, preferred_element_type=jnp.float32
        )

    real_part = mixing(cos_source, real_time) + mixing(sin_source, imag_time)
    imag_part = mixing(cos_source, imag_time) - mixing(sin_source, real_time)
    magnitude = jnp.sqrt(real_part * real_part + imag_part * imag_part)
    bound = limits[None, :, None]
    factor = jnp.maximum(magnitude - bound, 0.0) / jnp.maximum(magnitude, bound)
    kept_real = real_part * factor
    kept_imag = imag_part * factor
    back_real = mixing(cos_source, kept_real) - mixing(sin_source, kept_imag)
    back_imag = mixing(cos_source, kept_imag) + mixing(sin_source, kept_real)
    restored = jnp.dot(
        back_real.reshape(-1, WIN),
        cos_inverse,
        precision=careful,
        preferred_element_type=jnp.float32,
    )
    restored = restored + jnp.dot(
        back_imag.reshape(-1, WIN),
        sin_inverse,
        precision=careful,
        preferred_element_type=jnp.float32,
    )
    return restored.reshape(receivers, sources, samples)


def gathers_of_own_samples(blended, delays, thresholds):
    tables = make_tables()
    local_count = blended.shape[1]
    own_delays = lax.dynamic_slice_in_dim(
        delays, lax.axis_index("shot") * local_count, local_count, 0
    )
    estimate = None
    for sweep in range(ITERS):
        if sweep == 0:
            residual = blended.astype(jnp.bfloat16)
            update = (RELAX * spread(residual, own_delays)).astype(jnp.bfloat16)
        else:
            residual = (blended - blend(estimate, own_delays)).astype(jnp.bfloat16)
            update = (estimate.astype(jnp.float32) + RELAX * spread(residual, own_delays)).astype(
                jnp.bfloat16
            )
        gathers = lax.all_to_all(update, "shot", split_axis=0, concat_axis=1, tiled=True)
        filtered = coherence(gathers, thresholds[sweep], tables).astype(jnp.bfloat16)
        estimate = lax.all_to_all(filtered, "shot", split_axis=1, concat_axis=0, tiled=True)
    return estimate


def whole_receivers_fit(shots, blocks_of_time, receivers, samples):
    held, windows = SRC // shots, samples // WIN
    return (
        receivers % (shots * blocks_of_time) == 0
        and held * 2 == SUB
        and windows % 2 == 0
        and windows * blocks_of_time == SUB
        and receivers // (shots * blocks_of_time) * SUB <= HALF
    )


def local(blended, delays, thresholds):
    shots, blocks_of_time = lax.axis_size("shot"), lax.axis_size("tm")
    if whole_receivers_fit(shots, blocks_of_time, blended.shape[0], blended.shape[2]):
        return gathers_of_all_samples(shots, blended, delays, thresholds)
    return gathers_of_own_samples(blended, delays, thresholds)


def solution(mesh):
    return jax.shard_map(
        local,
        mesh=mesh,
        in_specs=(P(None, "shot", "tm"), P(), P()),
        out_specs=P(None, "shot", "tm"),
        check_vma=False,
    )
```

```python
import functools
import math

import jax
import jax.numpy as jnp
import ml_dtypes
import numpy as np
from jax import lax
from jax.experimental import pallas as pl
from jax.experimental.pallas import tpu as pltpu
from jax.sharding import PartitionSpec as P

SRC = 64
SRC_EXP = 2
WIN = 256
BLK = 128
ITERS = 2


RELAX = 0.5
HALF = WIN // 2
SUB = 8
TILE = 256


def bfloat_scale(table):
    values = np.unique(np.abs(table).round(12))
    factors = 1.0 + np.arange(4096) / 4096.0
    scaled = factors[:, None] * values
    lost = scaled.astype(ml_dtypes.bfloat16).astype(np.float64) - scaled
    return factors[np.argmin(np.sum((lost / factors[:, None]) ** 2, axis=1))]


def half_spectrum_tables():
    moment = np.arange(WIN)
    angle = (moment[:, None] * np.arange(HALF)[None, :] % WIN) * (2.0 * math.pi / WIN)
    nyquist = np.where(moment % 2 == 0, 1.0, -1.0)
    sine = -np.sin(angle)
    sine[:, 0] = nyquist
    forward = np.concatenate([np.cos(angle), sine], axis=1).astype(ml_dtypes.bfloat16)
    inverse = np.concatenate([np.cos(angle), sine], axis=1).T / math.sqrt(WIN)
    inverse[0] *= 0.5
    inverse[HALF] *= 0.5
    source = np.arange(SRC)
    turn = (source[:, None] * source[None, :] % SRC) * (2.0 * math.pi / SRC)
    cosine, sine = np.cos(turn) / math.sqrt(SRC), np.sin(turn) / math.sqrt(SRC)
    onward = np.block([[cosine, sine], [-sine, cosine]])
    source_scale, time_scale = bfloat_scale(onward), bfloat_scale(inverse)
    onward = onward * source_scale
    tables = (
        forward,
        inverse * time_scale,
        np.concatenate([onward, onward], axis=1) / math.sqrt(WIN),
        np.concatenate([onward.T, onward.T], axis=1),
    )
    tables = tuple(table.astype(ml_dtypes.bfloat16) for table in tables)
    return tables, source_scale, 1.0 / (source_scale * source_scale * time_scale)


def rearranging(shape, axes):
    order = np.arange(math.prod(shape)).reshape(shape).transpose(axes).reshape(-1)
    return np.eye(order.size)[order].astype(ml_dtypes.bfloat16)


def order_tables(windows, own):
    shots, sources = TILE // (2 * windows * own), TILE // windows
    return (
        rearranging((shots, windows, 2, own), (0, 3, 2, 1)),
        rearranging((sources, windows), (1, 0)),
        rearranging((windows, sources), (1, 0)),
    )


def halves(value):
    high = value.astype(jnp.bfloat16)
    return high, (value - high.astype(jnp.float32)).astype(jnp.bfloat16)


def product(left, right):
    return jnp.dot(left, right, preferred_element_type=jnp.float32)


def gather_kernel(
    shots,
    limit_scale,
    kept_scale,
    delays_far,
    limits,
    received,
    tables,
    out,
    delays,
    records,
    field,
    mixed,
    back,
    firsts,
    estimates,
    sem,
):
    copy = pltpu.make_async_copy(delays_far, delays, sem)
    copy.start()
    forward, inverse, order_arrived, order_windows, order_sources = (
        tables.at[pl.ds(at * TILE, TILE)] for at in range(5)
    )
    onward, backward = (
        tables.at[pl.ds(5 * TILE + at * 2 * SRC, 2 * SRC)] for at in range(2)
    )
    count, receivers, rows, _ = received.shape
    blocks_of_time = count // shots
    experiments, sources = delays.shape[1], SRC
    windows = blocks_of_time * rows * shots // (2 * experiments)
    groups = receivers * windows
    parts = windows // blocks_of_time
    some = TILE // windows
    lane = lax.broadcasted_iota(jnp.int32, (windows, BLK), 1)
    row = lax.broadcasted_iota(jnp.int32, (windows, BLK), 0)
    lane_of_group = lax.broadcasted_iota(jnp.int32, (sources, HALF), 1)
    lane_of_some = lax.broadcasted_iota(jnp.int32, (some, HALF), 1)

    arrived = [
        received[slice(chunk * TILE // rows, (chunk + 1) * TILE // rows), r].reshape(TILE, BLK)
        for chunk in range(sources // some)
        for r in range(receivers)
    ]
    records[...] = product(order_arrived[...], jnp.concatenate(arrived, axis=1))

    copy.wait()

    def advanced(even, odd, delay):
        by = (BLK - delay) & (BLK - 1)
        even, odd = pltpu.roll(even, by, 1), pltpu.roll(odd, by, 1)
        after = jnp.where(row < windows - 1, pltpu.roll(even, windows - 1, 0), 0.0)
        same = lane < BLK - delay
        return jnp.where(same, even, odd), jnp.where(same, odd, after)

    def moved_by(even, odd, ahead_by):
        ahead = ahead_by >= 0
        by = (BLK - ahead_by) & (BLK - 1)
        even, odd = pltpu.roll(even, by, 1), pltpu.roll(odd, by, 1)
        other = pltpu.roll(jnp.where(ahead, even, odd), jnp.where(ahead, windows - 1, 1), 0)
        other = jnp.where(row != jnp.where(ahead, windows - 1, 0), other, 0.0)
        same = ((lane + ahead_by) & -BLK) == 0
        return (
            jnp.where(same, even, jnp.where(ahead, odd, other)),
            jnp.where(same, odd, jnp.where(ahead, other, even)),
        )

    def columns(group):
        return slice(group * HALF, (group + 1) * HALF)

    def first_update(r, chunk):
        updated = []
        for at in range(0, some, SRC_EXP):
            even, odd = (
                records[pl.ds((at + half) * windows, windows), columns(chunk * receivers + r)]
                for half in range(2)
            )
            for k in range(SRC_EXP):
                early = advanced(even, odd, delays[k, (chunk * some + at) // SRC_EXP])
                updated.append(jnp.concatenate([RELAX * x for x in early], axis=1))
        updated = jnp.concatenate(updated, axis=0).astype(jnp.bfloat16)
        firsts[pl.ds((r * sources + chunk * some) * windows, TILE), :] = updated
        return updated

    def side_by_side(values):
        return jnp.concatenate(values, axis=1)

    def estimates_by_source():
        parts_of_rows = []
        for r, chunk in turns:
            starts = [(r * windows + w) * sources + chunk * some for w in range(windows)]
            rows_of_part = [estimates[start : start + some, :] for start in starts]
            parts_of_rows.append(jnp.concatenate(rows_of_part, axis=0))
        return product(order_sources[...], side_by_side(parts_of_rows))

    def later_update(r, chunk, before):
        first = (r * sources + chunk * some) * windows
        updated = []
        for at in range(0, some, SRC_EXP):
            lags = [delays[k, (chunk * some + at) // SRC_EXP] for k in range(SRC_EXP)]
            spread = firsts[pl.ds(first + at * windows, SRC_EXP * windows), :]
            spread = spread.astype(jnp.float32)
            estimate = [
                tuple(
                    before[(at + k) * windows : (at + k + 1) * windows, columns(half)]
                    for half in range(2)
                )
                for k in range(SRC_EXP)
            ]
            for k in range(SRC_EXP):
                even, odd = estimate[k]
                other = moved_by(*estimate[1 - k], lags[k] - lags[1 - k])
                stays = (row < windows - 1) | (lane < BLK - lags[k])
                even = RELAX * (even - other[0])
                odd = jnp.where(stays, RELAX * (odd - other[1]), odd)
                step = spread[k * windows : (k + 1) * windows]
                updated.append(jnp.concatenate([even, odd], axis=1) + step)
        return jnp.concatenate(updated, axis=0).astype(jnp.bfloat16)

    turns = [(r, chunk) for r in range(receivers) for chunk in range(sources // some)]

    def update_and_forward_in_time(sweep):
        if sweep:
            before = estimates_by_source()
            updates = [
                later_update(r, chunk, before[:, at * WIN : (at + 1) * WIN])
                for at, (r, chunk) in enumerate(turns)
            ]
        else:
            updates = [first_update(r, chunk) for r, chunk in turns]
        signal = product(order_windows[...], side_by_side(updates)).astype(jnp.bfloat16)
        signal = [signal[:, at * WIN : (at + 1) * WIN] for at in range(len(turns))]
        spectra = product(jnp.concatenate(signal, axis=0), forward[...])
        nyquists = [jnp.zeros((some, HALF), jnp.float32) for _ in range(sources // some)]
        for at, (r, chunk) in enumerate(turns):
            for w in range(windows):
                group = r * windows + w
                start = at * TILE + w * some
                real, imag = (spectra[start : start + some, columns(half)] for half in range(2))
                moved = pltpu.roll(imag, group, 1) if group else imag
                nyquists[chunk] = jnp.where(lane_of_some == group, moved, nyquists[chunk])
                imag = jnp.where(lane_of_some == 0, 0.0, imag)
                put(field, columns(group), real, imag, chunk * some)
        for chunk, nyquist in enumerate(nyquists):
            put(field, columns(groups), nyquist, jnp.zeros_like(nyquist), chunk * some)

    def put(ref, where, real, imag, first=0):
        real_high, real_low = halves(real)
        imag_high, imag_low = halves(imag)
        for at, value in enumerate((real_high, imag_high, real_low, imag_low)):
            start = at * sources + first
            ref[start : start + value.shape[0], where] = value

    def mixing(table, ref):
        total = product(table[...], ref[...])
        return total[:sources], total[sources:]

    def shrink(sweep):
        limit = limits[sweep : sweep + 1, :] * (limit_scale * kept_scale)
        p = lax.broadcasted_iota(jnp.int32, (sources, sources), 0)
        q = lax.broadcasted_iota(jnp.int32, (sources, sources), 1)
        bound = jnp.sum(jnp.where(p == q, limit, 0.0), axis=1, keepdims=True)
        mirrored = (p + q == 0) | (p + q == sources)
        bound_mirrored = jnp.sum(jnp.where(mirrored, limit, 0.0), axis=1, keepdims=True)
        all_real, all_imag = mixing(onward, field)
        for group in range(groups + 1):
            real, imag = all_real[:, columns(group)], all_imag[:, columns(group)]
            inverse_size = lax.rsqrt(real * real + imag * imag)
            factor = jnp.maximum(kept_scale - bound * inverse_size, 0.0) + jnp.maximum(
                kept_scale - bound_mirrored * inverse_size, 0.0
            )
            put(mixed, columns(group), real * factor, imag * factor)

    def back_in_source():
        real, imag = mixing(backward, mixed)
        nyquist = real[:, columns(groups)]
        for group in range(groups):
            moved = pltpu.roll(nyquist, HALF - group, 1) if group else nyquist
            own_imag = jnp.where(lane_of_group == 0, moved, imag[:, columns(group)])
            rows_of_group = slice(group * sources, (group + 1) * sources)
            for half, value in enumerate((real[:, columns(group)], own_imag)):
                back[rows_of_group, columns(half)] = value.astype(jnp.bfloat16)

    def swapped(value):
        return pltpu.roll(value, SUB // 2, 1)

    def deliver(r, w, restored):
        low = lax.broadcasted_iota(jnp.int32, (sources // SUB, SUB, BLK), 1) < SUB // 2
        pieces = []
        for part in range(2):
            window = restored[part * sources : (part + 1) * sources]
            even = window[:, :BLK].reshape(sources // SUB, SUB, BLK)
            odd = window[:, BLK:].reshape(sources // SUB, SUB, BLK)
            pieces.append(
                (jnp.where(low, even, swapped(odd)), jnp.where(low, swapped(even), odd))
            )
        block, inside = w // parts, w % parts
        for side in range(2):
            both = jnp.concatenate([pieces[0][side], pieces[1][side]], axis=1)
            both = both.astype(jnp.bfloat16)
            for k in range(sources // SUB):
                target = (2 * k + side) * blocks_of_time + block
                out[target, r, inside * SUB : (inside + 2) * SUB, :] = both[k]

    for sweep in range(ITERS):
        update_and_forward_in_time(sweep)
        shrink(sweep)
        back_in_source()
        restored = product(back[...], inverse[...])
        if sweep < ITERS - 1:
            estimates[...] = restored.astype(jnp.bfloat16)
            continue
        for group in range(0, groups, 2):
            pair = restored[group * sources : (group + 2) * sources]
            deliver(group // windows, group % windows, pair)


def cast_kernel(blended, delays, limits, sent, delays_near, limits_near, held, sems):
    pieces = sems.shape[0] - 2
    count = blended.shape[0] // pieces
    spans = [pl.ds(at * count, count) for at in range(pieces)]
    copies = [
        pltpu.make_async_copy(blended.at[span], held.at[span], sems.at[at])
        for at, span in enumerate(spans)
    ]
    small = [
        pltpu.make_async_copy(delays, delays_near, sems.at[pieces]),
        pltpu.make_async_copy(limits, limits_near, sems.at[pieces + 1]),
    ]
    for copy in small + copies:
        copy.start()
    for copy, span in zip(copies, spans):
        copy.wait()
        sent[span] = held[span].astype(jnp.bfloat16)
    for copy in small:
        copy.wait()


def gathers_of_all_samples(shots, blended, delays, thresholds):
    receivers, own, samples = blended.shape
    blocks_of_time = lax.axis_size("tm")
    count = shots * blocks_of_time
    each = receivers // count
    blocks = samples // BLK
    windows = samples * blocks_of_time // WIN
    groups = each * windows
    rows = blocks * own
    sent = blended.reshape(receivers, own, blocks, BLK).transpose(0, 2, 1, 3)
    sent = sent.reshape(count, each, rows, BLK)
    vmem, far = pl.BlockSpec(memory_space=pltpu.VMEM), pl.BlockSpec(memory_space=pl.ANY)

    def kept_far(array):
        return pltpu.with_memory_space_constraint(array, pltpu.HBM)

    sent, delays, thresholds = pl.pallas_call(
        cast_kernel,
        out_shape=(
            jax.ShapeDtypeStruct(sent.shape, jnp.bfloat16),
            jax.ShapeDtypeStruct(delays.T.shape, delays.dtype),
            jax.ShapeDtypeStruct(thresholds.shape, thresholds.dtype),
        ),
        in_specs=[far] * 3,
        out_specs=[vmem] * 3,
        scratch_shapes=[
            pltpu.VMEM(sent.shape, jnp.float32),
            pltpu.SemaphoreType.DMA((4 + 2,)),
        ],
        compiler_params=pltpu.CompilerParams(vmem_limit_bytes=8 * 1024 * 1024),
    )(kept_far(sent), kept_far(delays.T), kept_far(thresholds))
    received = lax.all_to_all(sent, ("shot", "tm"), split_axis=0, concat_axis=0, tiled=True)
    tables, limit_scale, kept_scale = half_spectrum_tables()
    tables = np.concatenate(tables[:2] + order_tables(windows, own) + tables[2:], axis=0)
    held = SRC // shots
    restored = pl.pallas_call(
        functools.partial(gather_kernel, shots, float(limit_scale), float(kept_scale)),
        out_shape=jax.ShapeDtypeStruct((count, each, blocks * held, BLK), jnp.bfloat16),
        in_specs=[pl.BlockSpec(memory_space=pl.ANY)] + [vmem] * 3,
        out_specs=vmem,
        scratch_shapes=[
            pltpu.SMEM(delays.shape, jnp.int32),
            pltpu.VMEM((TILE, SRC * windows // TILE * each * BLK), jnp.float32),
            pltpu.VMEM((4 * SRC, (groups + 1) * HALF), jnp.bfloat16),
            pltpu.VMEM((4 * SRC, (groups + 1) * HALF), jnp.bfloat16),
            pltpu.VMEM((groups * SRC, WIN), jnp.bfloat16),
            pltpu.VMEM((groups * SRC, WIN), jnp.bfloat16),
            pltpu.VMEM((groups * SRC, WIN), jnp.bfloat16),
            pltpu.SemaphoreType.DMA(()),
        ],
        compiler_params=pltpu.CompilerParams(vmem_limit_bytes=40 * 1024 * 1024),
        cost_estimate=pl.CostEstimate(
            flops=2 * ITERS * groups * SRC * WIN * WIN * 5,
            bytes_accessed=2 * 1024 * 1024,
            transcendentals=ITERS * groups * SRC * HALF,
        ),
    )(delays, thresholds, received, jnp.asarray(tables))
    final = lax.all_to_all(restored, ("shot", "tm"), split_axis=0, concat_axis=0, tiled=True)
    final = final.reshape(receivers, blocks, held, BLK).transpose(0, 2, 1, 3)
    return final.reshape(receivers, held, samples)


def shifted(array, axis, by):
    count = lax.axis_size(axis)
    pairs = [(i, i + by) for i in range(count) if 0 <= i + by < count]
    return lax.ppermute(array, axis, pairs)


def phase_table(length_first, length_second, period):
    first_index = jnp.arange(length_first, dtype=jnp.int32)[:, None]
    second_index = jnp.arange(length_second, dtype=jnp.int32)[None, :]
    return (first_index * second_index % period).astype(jnp.float32) * (2.0 * math.pi / period)


def make_tables():
    time_angle = phase_table(WIN, WIN, WIN)
    time_scale = 1.0 / math.sqrt(WIN)
    cos_forward = jnp.cos(time_angle).astype(jnp.bfloat16)
    sin_forward = -jnp.sin(time_angle).astype(jnp.bfloat16)
    cos_inverse = jnp.cos(time_angle) * time_scale
    sin_inverse = -jnp.sin(time_angle) * time_scale
    source_angle = phase_table(SRC, SRC, SRC)
    cos_source = jnp.cos(source_angle) / math.sqrt(SRC)
    sin_source = jnp.sin(source_angle) / math.sqrt(SRC)
    return (cos_forward, sin_forward, cos_inverse, sin_inverse, cos_source, sin_source)


def blend(estimate, own_delays):
    receivers, sources, samples = estimate.shape
    blocks = samples // BLK
    experiments = sources // SRC_EXP
    earlier = shifted(estimate[:, :, samples - BLK :], "tm", 1)
    upper = estimate.reshape(receivers, sources, blocks, BLK)
    shifts = own_delays.reshape(-1)
    row_index = jnp.arange(BLK, dtype=jnp.int32)[None, :, None]
    column_index = jnp.arange(BLK, dtype=jnp.int32)[None, None, :]
    select_same = (row_index == column_index - shifts[:, None, None]).astype(jnp.bfloat16)
    select_prior = (row_index == BLK + column_index - shifts[:, None, None]).astype(jnp.bfloat16)
    same = jnp.einsum("rsnb,sbi->rsni", upper, select_same, preferred_element_type=jnp.float32)
    onward = jnp.einsum("rsnb,sbi->rsni", upper, select_prior, preferred_element_type=jnp.float32)
    edge_part = jnp.einsum(
        "rsb,sbi->rsi", earlier, select_prior, preferred_element_type=jnp.float32
    )
    same = jnp.sum(same.reshape(receivers, experiments, SRC_EXP, blocks, BLK), axis=2)
    onward = jnp.sum(onward.reshape(receivers, experiments, SRC_EXP, blocks, BLK), axis=2)
    edge_part = jnp.sum(edge_part.reshape(receivers, experiments, SRC_EXP, BLK), axis=2)
    carried = jnp.concatenate([edge_part[:, :, None], onward[:, :, : blocks - 1]], axis=2)
    return (same + carried).reshape(receivers, experiments, samples)


def spread(residual, own_delays):
    receivers, experiments, samples = residual.shape
    blocks = samples // BLK
    later = shifted(residual[:, :, :BLK], "tm", -1)
    lower = residual.reshape(receivers, experiments, blocks, BLK)
    row_index = jnp.arange(BLK, dtype=jnp.int32)[None, None, :, None]
    column_index = jnp.arange(BLK, dtype=jnp.int32)[None, None, None, :]
    select_same = (row_index == column_index + own_delays[:, :, None, None]).astype(jnp.bfloat16)
    select_next = (row_index + BLK == column_index + own_delays[:, :, None, None]).astype(
        jnp.bfloat16
    )
    same = jnp.einsum("rena,ekai->rekni", lower, select_same, preferred_element_type=jnp.float32)
    backward = jnp.einsum(
        "rena,ekai->rekni", lower, select_next, preferred_element_type=jnp.float32
    )
    edge_part = jnp.einsum("rea,ekai->reki", later, select_next, preferred_element_type=jnp.float32)
    carried = jnp.concatenate([backward[:, :, :, 1:], edge_part[:, :, :, None]], axis=3)
    return (same + carried).reshape(receivers, experiments * SRC_EXP, samples)


def coherence(gathers, limits, tables):
    cos_forward, sin_forward, cos_inverse, sin_inverse, cos_source, sin_source = tables
    receivers, sources, samples = gathers.shape
    windows = samples // WIN
    careful = lax.Precision.HIGH
    scale = 1.0 / math.sqrt(WIN)
    signal = gathers.reshape(receivers * sources * windows, WIN)
    real_time = (jnp.dot(signal, cos_forward, preferred_element_type=jnp.float32) * scale).reshape(
        receivers, sources, samples
    )
    imag_time = (jnp.dot(signal, sin_forward, preferred_element_type=jnp.float32) * scale).reshape(
        receivers, sources, samples
    )

    def mixing(table, field):
        return jnp.einsum(
            "ps,rsx->rpx", table, field, precision=careful, preferred_element_type=jnp.float32
        )

    real_part = mixing(cos_source, real_time) + mixing(sin_source, imag_time)
    imag_part = mixing(cos_source, imag_time) - mixing(sin_source, real_time)
    magnitude = jnp.sqrt(real_part * real_part + imag_part * imag_part)
    bound = limits[None, :, None]
    factor = jnp.maximum(magnitude - bound, 0.0) / jnp.maximum(magnitude, bound)
    kept_real = real_part * factor
    kept_imag = imag_part * factor
    back_real = mixing(cos_source, kept_real) - mixing(sin_source, kept_imag)
    back_imag = mixing(cos_source, kept_imag) + mixing(sin_source, kept_real)
    restored = jnp.dot(
        back_real.reshape(-1, WIN),
        cos_inverse,
        precision=careful,
        preferred_element_type=jnp.float32,
    )
    restored = restored + jnp.dot(
        back_imag.reshape(-1, WIN),
        sin_inverse,
        precision=careful,
        preferred_element_type=jnp.float32,
    )
    return restored.reshape(receivers, sources, samples)


def gathers_of_own_samples(blended, delays, thresholds):
    tables = make_tables()
    local_count = blended.shape[1]
    own_delays = lax.dynamic_slice_in_dim(
        delays, lax.axis_index("shot") * local_count, local_count, 0
    )
    estimate = None
    for sweep in range(ITERS):
        if sweep == 0:
            residual = blended.astype(jnp.bfloat16)
            update = (RELAX * spread(residual, own_delays)).astype(jnp.bfloat16)
        else:
            residual = (blended - blend(estimate, own_delays)).astype(jnp.bfloat16)
            update = (estimate.astype(jnp.float32) + RELAX * spread(residual, own_delays)).astype(
                jnp.bfloat16
            )
        gathers = lax.all_to_all(update, "shot", split_axis=0, concat_axis=1, tiled=True)
        filtered = coherence(gathers, thresholds[sweep], tables).astype(jnp.bfloat16)
        estimate = lax.all_to_all(filtered, "shot", split_axis=1, concat_axis=0, tiled=True)
    return estimate


def whole_receivers_fit(shots, blocks_of_time, receivers, samples):
    held, windows = SRC // shots, samples // WIN
    return (
        receivers % (shots * blocks_of_time) == 0
        and held * 2 == SUB
        and windows % 2 == 0
        and windows * blocks_of_time == SUB
        and receivers // (shots * blocks_of_time) * SUB <= HALF
    )


def local(blended, delays, thresholds):
    shots, blocks_of_time = lax.axis_size("shot"), lax.axis_size("tm")
    if whole_receivers_fit(shots, blocks_of_time, blended.shape[0], blended.shape[2]):
        return gathers_of_all_samples(shots, blended, delays, thresholds)
    return gathers_of_own_samples(blended, delays, thresholds)


def solution(mesh):
    return jax.shard_map(
        local,
        mesh=mesh,
        in_specs=(P(None, "shot", "tm"), P(), P()),
        out_specs=P(None, "shot", "tm"),
        check_vma=False,
    )
```

```python
import functools
import math

import jax
import jax.numpy as jnp
import ml_dtypes
import numpy as np
from jax import lax
from jax.experimental import pallas as pl
from jax.experimental.pallas import tpu as pltpu
from jax.sharding import PartitionSpec as P

SRC = 64
SRC_EXP = 2
WIN = 256
BLK = 128
ITERS = 2


RELAX = 0.5
HALF = WIN // 2
SUB = 8
TILE = 256


def bfloat_scale(table):
    values = np.unique(np.abs(table).round(12))
    factors = 1.0 + np.arange(4096) / 4096.0
    scaled = factors[:, None] * values
    lost = scaled.astype(ml_dtypes.bfloat16).astype(np.float64) - scaled
    return factors[np.argmin(np.sum((lost / factors[:, None]) ** 2, axis=1))]


def half_spectrum_tables():
    moment = np.arange(WIN)
    angle = (moment[:, None] * np.arange(HALF)[None, :] % WIN) * (2.0 * math.pi / WIN)
    nyquist = np.where(moment % 2 == 0, 1.0, -1.0)
    sine = -np.sin(angle)
    sine[:, 0] = nyquist
    forward = np.concatenate([np.cos(angle), sine], axis=1).astype(ml_dtypes.bfloat16)
    inverse = np.concatenate([np.cos(angle), sine], axis=1).T / math.sqrt(WIN)
    inverse[0] *= 0.5
    inverse[HALF] *= 0.5
    source = np.arange(SRC)
    turn = (source[:, None] * source[None, :] % SRC) * (2.0 * math.pi / SRC)
    cosine, sine = np.cos(turn) / math.sqrt(SRC), np.sin(turn) / math.sqrt(SRC)
    onward = np.block([[cosine, sine], [-sine, cosine]])
    time_scale = bfloat_scale(inverse)
    forward, inverse = (x.astype(ml_dtypes.bfloat16) for x in (forward, inverse * time_scale))
    tables = forward, inverse, high_and_low(onward / math.sqrt(WIN)), high_and_low(onward.T)
    return tables, 1.0 / time_scale


def high_and_low(table):
    high = table.astype(ml_dtypes.bfloat16)
    low = (table - high.astype(np.float64)).astype(ml_dtypes.bfloat16)
    return np.concatenate([high, low], axis=1)


def rearranging(shape, axes):
    order = np.arange(math.prod(shape)).reshape(shape).transpose(axes).reshape(-1)
    return np.eye(order.size)[order].astype(ml_dtypes.bfloat16)


def order_tables(windows, own):
    shots, sources = TILE // (2 * windows * own), TILE // windows
    return (
        rearranging((shots, windows, 2, own), (0, 3, 2, 1)),
        rearranging((sources, windows), (1, 0)),
        rearranging((windows, sources), (1, 0)),
    )


def product(left, right):
    return jnp.dot(left, right, preferred_element_type=jnp.float32)


def gather_kernel(
    shots,
    kept_scale,
    delays_far,
    limits,
    received,
    tables,
    out,
    delays,
    records,
    field,
    mixed,
    back,
    firsts,
    estimates,
    sem,
):
    copy = pltpu.make_async_copy(delays_far, delays, sem)
    copy.start()
    forward, inverse, order_arrived, order_windows, order_sources = (
        tables.at[pl.ds(at * TILE, TILE)] for at in range(5)
    )
    onward, backward = (
        tables.at[pl.ds(5 * TILE + at * 2 * SRC, 2 * SRC)] for at in range(2)
    )
    count, receivers, rows, _ = received.shape
    blocks_of_time = count // shots
    experiments, sources = delays.shape[1], SRC
    windows = blocks_of_time * rows * shots // (2 * experiments)
    groups = receivers * windows
    parts = windows // blocks_of_time
    some = TILE // windows
    lane = lax.broadcasted_iota(jnp.int32, (windows, BLK), 1)
    row = lax.broadcasted_iota(jnp.int32, (windows, BLK), 0)
    lane_of_group = lax.broadcasted_iota(jnp.int32, (sources, HALF), 1)
    lane_of_some = lax.broadcasted_iota(jnp.int32, (some, HALF), 1)

    arrived = [
        received[slice(chunk * TILE // rows, (chunk + 1) * TILE // rows), r].reshape(TILE, BLK)
        for chunk in range(sources // some)
        for r in range(receivers)
    ]
    records[...] = product(order_arrived[...], jnp.concatenate(arrived, axis=1))

    copy.wait()

    def advanced(even, odd, delay):
        by = (BLK - delay) & (BLK - 1)
        even, odd = pltpu.roll(even, by, 1), pltpu.roll(odd, by, 1)
        after = jnp.where(row < windows - 1, pltpu.roll(even, windows - 1, 0), 0.0)
        same = lane < BLK - delay
        return jnp.where(same, even, odd), jnp.where(same, odd, after)

    def moved_by(even, odd, ahead_by):
        ahead = ahead_by >= 0
        by = (BLK - ahead_by) & (BLK - 1)
        even, odd = pltpu.roll(even, by, 1), pltpu.roll(odd, by, 1)
        other = pltpu.roll(jnp.where(ahead, even, odd), jnp.where(ahead, windows - 1, 1), 0)
        other = jnp.where(row != jnp.where(ahead, windows - 1, 0), other, 0.0)
        same = ((lane + ahead_by) & -BLK) == 0
        return (
            jnp.where(same, even, jnp.where(ahead, odd, other)),
            jnp.where(same, odd, jnp.where(ahead, other, even)),
        )

    def columns(group):
        return slice(group * HALF, (group + 1) * HALF)

    def first_update(r, chunk):
        updated = []
        for at in range(0, some, SRC_EXP):
            even, odd = (
                records[pl.ds((at + half) * windows, windows), columns(chunk * receivers + r)]
                for half in range(2)
            )
            for k in range(SRC_EXP):
                early = advanced(even, odd, delays[k, (chunk * some + at) // SRC_EXP])
                updated.append(jnp.concatenate([RELAX * x for x in early], axis=1))
        updated = jnp.concatenate(updated, axis=0).astype(jnp.bfloat16)
        firsts[pl.ds((r * sources + chunk * some) * windows, TILE), :] = updated
        return updated

    def side_by_side(values):
        return jnp.concatenate(values, axis=1)

    def estimates_by_source():
        parts_of_rows = []
        for r, chunk in turns:
            starts = [(r * windows + w) * sources + chunk * some for w in range(windows)]
            rows_of_part = [estimates[start : start + some, :] for start in starts]
            parts_of_rows.append(jnp.concatenate(rows_of_part, axis=0))
        return product(order_sources[...], side_by_side(parts_of_rows))

    def later_update(r, chunk, before):
        first = (r * sources + chunk * some) * windows
        updated = []
        for at in range(0, some, SRC_EXP):
            lags = [delays[k, (chunk * some + at) // SRC_EXP] for k in range(SRC_EXP)]
            spread = firsts[pl.ds(first + at * windows, SRC_EXP * windows), :]
            spread = spread.astype(jnp.float32)
            estimate = [
                tuple(
                    before[(at + k) * windows : (at + k + 1) * windows, columns(half)]
                    for half in range(2)
                )
                for k in range(SRC_EXP)
            ]
            for k in range(SRC_EXP):
                even, odd = estimate[k]
                other = moved_by(*estimate[1 - k], lags[k] - lags[1 - k])
                stays = (row < windows - 1) | (lane < BLK - lags[k])
                even = RELAX * (even - other[0])
                odd = jnp.where(stays, RELAX * (odd - other[1]), odd)
                step = spread[k * windows : (k + 1) * windows]
                updated.append(jnp.concatenate([even, odd], axis=1) + step)
        return jnp.concatenate(updated, axis=0).astype(jnp.bfloat16)

    turns = [(r, chunk) for r in range(receivers) for chunk in range(sources // some)]

    def update_and_forward_in_time(sweep):
        if sweep:
            before = estimates_by_source()
            updates = [
                later_update(r, chunk, before[:, at * WIN : (at + 1) * WIN])
                for at, (r, chunk) in enumerate(turns)
            ]
        else:
            updates = [first_update(r, chunk) for r, chunk in turns]
        signal = product(order_windows[...], side_by_side(updates)).astype(jnp.bfloat16)
        signal = [signal[:, at * WIN : (at + 1) * WIN] for at in range(len(turns))]
        spectra = product(jnp.concatenate(signal, axis=0), forward[...])
        nyquists = [jnp.zeros((some, HALF), jnp.float32) for _ in range(sources // some)]
        for at, (r, chunk) in enumerate(turns):
            for w in range(windows):
                group = r * windows + w
                start = at * TILE + w * some
                real, imag = (spectra[start : start + some, columns(half)] for half in range(2))
                moved = pltpu.roll(imag, group, 1) if group else imag
                nyquists[chunk] = jnp.where(lane_of_some == group, moved, nyquists[chunk])
                imag = jnp.where(lane_of_some == 0, 0.0, imag)
                put(field, columns(group), real, imag, chunk * some)
        for chunk, nyquist in enumerate(nyquists):
            put(field, columns(groups), nyquist, jnp.zeros_like(nyquist), chunk * some)

    def put(ref, where, real, imag, first=0):
        for at, value in enumerate((real, imag)):
            start = at * sources + first
            ref[start : start + value.shape[0], where] = value.astype(jnp.bfloat16)

    def mixing(table, ref):
        values = ref[...]
        total = product(table[...], jnp.concatenate([values, values], axis=0))
        return total[:sources], total[sources:]

    def shrink(sweep):
        limit = limits[sweep : sweep + 1, :] * kept_scale
        p = lax.broadcasted_iota(jnp.int32, (sources, sources), 0)
        q = lax.broadcasted_iota(jnp.int32, (sources, sources), 1)
        bound = jnp.sum(jnp.where(p == q, limit, 0.0), axis=1, keepdims=True)
        mirrored = (p + q == 0) | (p + q == sources)
        bound_mirrored = jnp.sum(jnp.where(mirrored, limit, 0.0), axis=1, keepdims=True)
        real, imag = mixing(onward, field)
        inverse_size = lax.rsqrt(real * real + imag * imag)
        factor = jnp.maximum(kept_scale - bound * inverse_size, 0.0) + jnp.maximum(
            kept_scale - bound_mirrored * inverse_size, 0.0
        )
        put(mixed, slice(None), real * factor, imag * factor)

    def back_in_source():
        real, imag = mixing(backward, mixed)
        nyquist = real[:, columns(groups)]
        for group in range(groups):
            moved = pltpu.roll(nyquist, HALF - group, 1) if group else nyquist
            own_imag = jnp.where(lane_of_group == 0, moved, imag[:, columns(group)])
            rows_of_group = slice(group * sources, (group + 1) * sources)
            for half, value in enumerate((real[:, columns(group)], own_imag)):
                back[rows_of_group, columns(half)] = value.astype(jnp.bfloat16)

    def swapped(value):
        return pltpu.roll(value, SUB // 2, 1)

    def deliver(r, w, restored):
        low = lax.broadcasted_iota(jnp.int32, (sources // SUB, SUB, BLK), 1) < SUB // 2
        pieces = []
        for part in range(2):
            window = restored[part * sources : (part + 1) * sources]
            even = window[:, :BLK].reshape(sources // SUB, SUB, BLK)
            odd = window[:, BLK:].reshape(sources // SUB, SUB, BLK)
            pieces.append(
                (jnp.where(low, even, swapped(odd)), jnp.where(low, swapped(even), odd))
            )
        block, inside = w // parts, w % parts
        for side in range(2):
            both = jnp.concatenate([pieces[0][side], pieces[1][side]], axis=1)
            both = both.astype(jnp.bfloat16)
            for k in range(sources // SUB):
                target = (2 * k + side) * blocks_of_time + block
                out[target, r, inside * SUB : (inside + 2) * SUB, :] = both[k]

    for sweep in range(ITERS):
        update_and_forward_in_time(sweep)
        shrink(sweep)
        back_in_source()
        restored = product(back[...], inverse[...])
        if sweep < ITERS - 1:
            estimates[...] = restored.astype(jnp.bfloat16)
            continue
        for group in range(0, groups, 2):
            pair = restored[group * sources : (group + 2) * sources]
            deliver(group // windows, group % windows, pair)


def cast_kernel(blended, delays, limits, sent, delays_near, limits_near, held, sems):
    pieces = sems.shape[0] - 2
    count = blended.shape[0] // pieces
    spans = [pl.ds(at * count, count) for at in range(pieces)]
    copies = [
        pltpu.make_async_copy(blended.at[span], held.at[span], sems.at[at])
        for at, span in enumerate(spans)
    ]
    small = [
        pltpu.make_async_copy(delays, delays_near, sems.at[pieces]),
        pltpu.make_async_copy(limits, limits_near, sems.at[pieces + 1]),
    ]
    for copy in copies + small:
        copy.start()
    for copy, span in zip(copies, spans):
        copy.wait()
        sent[span] = held[span].astype(jnp.bfloat16)
    for copy in small:
        copy.wait()


def gathers_of_all_samples(shots, blended, delays, thresholds):
    receivers, own, samples = blended.shape
    blocks_of_time = lax.axis_size("tm")
    count = shots * blocks_of_time
    each = receivers // count
    blocks = samples // BLK
    windows = samples * blocks_of_time // WIN
    groups = each * windows
    rows = blocks * own
    sent = blended.reshape(receivers, own, blocks, BLK).transpose(0, 2, 1, 3)
    sent = sent.reshape(count, each, rows, BLK)
    vmem, far = pl.BlockSpec(memory_space=pltpu.VMEM), pl.BlockSpec(memory_space=pl.ANY)

    def kept_far(array):
        return pltpu.with_memory_space_constraint(array, pltpu.HBM)

    sent, delays, thresholds = pl.pallas_call(
        cast_kernel,
        out_shape=(
            jax.ShapeDtypeStruct(sent.shape, jnp.bfloat16),
            jax.ShapeDtypeStruct(delays.T.shape, delays.dtype),
            jax.ShapeDtypeStruct(thresholds.shape, thresholds.dtype),
        ),
        in_specs=[far] * 3,
        out_specs=[vmem] * 3,
        scratch_shapes=[
            pltpu.VMEM(sent.shape, jnp.float32),
            pltpu.SemaphoreType.DMA((4 + 2,)),
        ],
        compiler_params=pltpu.CompilerParams(vmem_limit_bytes=8 * 1024 * 1024),
    )(kept_far(sent), kept_far(delays.T), kept_far(thresholds))
    received = lax.all_to_all(sent, ("shot", "tm"), split_axis=0, concat_axis=0, tiled=True)
    tables, kept_scale = half_spectrum_tables()
    tables = np.concatenate(tables[:2] + order_tables(windows, own) + tables[2:], axis=0)
    held = SRC // shots
    restored = pl.pallas_call(
        functools.partial(gather_kernel, shots, float(kept_scale)),
        out_shape=jax.ShapeDtypeStruct((count, each, blocks * held, BLK), jnp.bfloat16),
        in_specs=[pl.BlockSpec(memory_space=pl.ANY)] + [vmem] * 3,
        out_specs=vmem,
        scratch_shapes=[
            pltpu.SMEM(delays.shape, jnp.int32),
            pltpu.VMEM((TILE, SRC * windows // TILE * each * BLK), jnp.float32),
            pltpu.VMEM((2 * SRC, (groups + 1) * HALF), jnp.bfloat16),
            pltpu.VMEM((2 * SRC, (groups + 1) * HALF), jnp.bfloat16),
            pltpu.VMEM((groups * SRC, WIN), jnp.bfloat16),
            pltpu.VMEM((groups * SRC, WIN), jnp.bfloat16),
            pltpu.VMEM((groups * SRC, WIN), jnp.bfloat16),
            pltpu.SemaphoreType.DMA(()),
        ],
        compiler_params=pltpu.CompilerParams(vmem_limit_bytes=40 * 1024 * 1024),
        cost_estimate=pl.CostEstimate(
            flops=2 * ITERS * groups * SRC * WIN * WIN * 5,
            bytes_accessed=2 * 1024 * 1024,
            transcendentals=ITERS * groups * SRC * HALF,
        ),
    )(delays, thresholds, received, jnp.asarray(tables))
    final = lax.all_to_all(restored, ("shot", "tm"), split_axis=0, concat_axis=0, tiled=True)
    final = final.reshape(receivers, blocks, held, BLK).transpose(0, 2, 1, 3)
    return final.reshape(receivers, held, samples)


def shifted(array, axis, by):
    count = lax.axis_size(axis)
    pairs = [(i, i + by) for i in range(count) if 0 <= i + by < count]
    return lax.ppermute(array, axis, pairs)


def phase_table(length_first, length_second, period):
    first_index = jnp.arange(length_first, dtype=jnp.int32)[:, None]
    second_index = jnp.arange(length_second, dtype=jnp.int32)[None, :]
    return (first_index * second_index % period).astype(jnp.float32) * (2.0 * math.pi / period)


def make_tables():
    time_angle = phase_table(WIN, WIN, WIN)
    time_scale = 1.0 / math.sqrt(WIN)
    cos_forward = jnp.cos(time_angle).astype(jnp.bfloat16)
    sin_forward = -jnp.sin(time_angle).astype(jnp.bfloat16)
    cos_inverse = jnp.cos(time_angle) * time_scale
    sin_inverse = -jnp.sin(time_angle) * time_scale
    source_angle = phase_table(SRC, SRC, SRC)
    cos_source = jnp.cos(source_angle) / math.sqrt(SRC)
    sin_source = jnp.sin(source_angle) / math.sqrt(SRC)
    return (cos_forward, sin_forward, cos_inverse, sin_inverse, cos_source, sin_source)


def blend(estimate, own_delays):
    receivers, sources, samples = estimate.shape
    blocks = samples // BLK
    experiments = sources // SRC_EXP
    earlier = shifted(estimate[:, :, samples - BLK :], "tm", 1)
    upper = estimate.reshape(receivers, sources, blocks, BLK)
    shifts = own_delays.reshape(-1)
    row_index = jnp.arange(BLK, dtype=jnp.int32)[None, :, None]
    column_index = jnp.arange(BLK, dtype=jnp.int32)[None, None, :]
    select_same = (row_index == column_index - shifts[:, None, None]).astype(jnp.bfloat16)
    select_prior = (row_index == BLK + column_index - shifts[:, None, None]).astype(jnp.bfloat16)
    same = jnp.einsum("rsnb,sbi->rsni", upper, select_same, preferred_element_type=jnp.float32)
    onward = jnp.einsum("rsnb,sbi->rsni", upper, select_prior, preferred_element_type=jnp.float32)
    edge_part = jnp.einsum(
        "rsb,sbi->rsi", earlier, select_prior, preferred_element_type=jnp.float32
    )
    same = jnp.sum(same.reshape(receivers, experiments, SRC_EXP, blocks, BLK), axis=2)
    onward = jnp.sum(onward.reshape(receivers, experiments, SRC_EXP, blocks, BLK), axis=2)
    edge_part = jnp.sum(edge_part.reshape(receivers, experiments, SRC_EXP, BLK), axis=2)
    carried = jnp.concatenate([edge_part[:, :, None], onward[:, :, : blocks - 1]], axis=2)
    return (same + carried).reshape(receivers, experiments, samples)


def spread(residual, own_delays):
    receivers, experiments, samples = residual.shape
    blocks = samples // BLK
    later = shifted(residual[:, :, :BLK], "tm", -1)
    lower = residual.reshape(receivers, experiments, blocks, BLK)
    row_index = jnp.arange(BLK, dtype=jnp.int32)[None, None, :, None]
    column_index = jnp.arange(BLK, dtype=jnp.int32)[None, None, None, :]
    select_same = (row_index == column_index + own_delays[:, :, None, None]).astype(jnp.bfloat16)
    select_next = (row_index + BLK == column_index + own_delays[:, :, None, None]).astype(
        jnp.bfloat16
    )
    same = jnp.einsum("rena,ekai->rekni", lower, select_same, preferred_element_type=jnp.float32)
    backward = jnp.einsum(
        "rena,ekai->rekni", lower, select_next, preferred_element_type=jnp.float32
    )
    edge_part = jnp.einsum("rea,ekai->reki", later, select_next, preferred_element_type=jnp.float32)
    carried = jnp.concatenate([backward[:, :, :, 1:], edge_part[:, :, :, None]], axis=3)
    return (same + carried).reshape(receivers, experiments * SRC_EXP, samples)


def coherence(gathers, limits, tables):
    cos_forward, sin_forward, cos_inverse, sin_inverse, cos_source, sin_source = tables
    receivers, sources, samples = gathers.shape
    windows = samples // WIN
    careful = lax.Precision.HIGH
    scale = 1.0 / math.sqrt(WIN)
    signal = gathers.reshape(receivers * sources * windows, WIN)
    real_time = (jnp.dot(signal, cos_forward, preferred_element_type=jnp.float32) * scale).reshape(
        receivers, sources, samples
    )
    imag_time = (jnp.dot(signal, sin_forward, preferred_element_type=jnp.float32) * scale).reshape(
        receivers, sources, samples
    )

    def mixing(table, field):
        return jnp.einsum(
            "ps,rsx->rpx", table, field, precision=careful, preferred_element_type=jnp.float32
        )

    real_part = mixing(cos_source, real_time) + mixing(sin_source, imag_time)
    imag_part = mixing(cos_source, imag_time) - mixing(sin_source, real_time)
    magnitude = jnp.sqrt(real_part * real_part + imag_part * imag_part)
    bound = limits[None, :, None]
    factor = jnp.maximum(magnitude - bound, 0.0) / jnp.maximum(magnitude, bound)
    kept_real = real_part * factor
    kept_imag = imag_part * factor
    back_real = mixing(cos_source, kept_real) - mixing(sin_source, kept_imag)
    back_imag = mixing(cos_source, kept_imag) + mixing(sin_source, kept_real)
    restored = jnp.dot(
        back_real.reshape(-1, WIN),
        cos_inverse,
        precision=careful,
        preferred_element_type=jnp.float32,
    )
    restored = restored + jnp.dot(
        back_imag.reshape(-1, WIN),
        sin_inverse,
        precision=careful,
        preferred_element_type=jnp.float32,
    )
    return restored.reshape(receivers, sources, samples)


def gathers_of_own_samples(blended, delays, thresholds):
    tables = make_tables()
    local_count = blended.shape[1]
    own_delays = lax.dynamic_slice_in_dim(
        delays, lax.axis_index("shot") * local_count, local_count, 0
    )
    estimate = None
    for sweep in range(ITERS):
        if sweep == 0:
            residual = blended.astype(jnp.bfloat16)
            update = (RELAX * spread(residual, own_delays)).astype(jnp.bfloat16)
        else:
            residual = (blended - blend(estimate, own_delays)).astype(jnp.bfloat16)
            update = (estimate.astype(jnp.float32) + RELAX * spread(residual, own_delays)).astype(
                jnp.bfloat16
            )
        gathers = lax.all_to_all(update, "shot", split_axis=0, concat_axis=1, tiled=True)
        filtered = coherence(gathers, thresholds[sweep], tables).astype(jnp.bfloat16)
        estimate = lax.all_to_all(filtered, "shot", split_axis=1, concat_axis=0, tiled=True)
    return estimate


def whole_receivers_fit(shots, blocks_of_time, receivers, samples):
    held, windows = SRC // shots, samples // WIN
    return (
        receivers % (shots * blocks_of_time) == 0
        and held * 2 == SUB
        and windows % 2 == 0
        and windows * blocks_of_time == SUB
        and receivers // (shots * blocks_of_time) * SUB <= HALF
    )


def local(blended, delays, thresholds):
    shots, blocks_of_time = lax.axis_size("shot"), lax.axis_size("tm")
    if whole_receivers_fit(shots, blocks_of_time, blended.shape[0], blended.shape[2]):
        return gathers_of_all_samples(shots, blended, delays, thresholds)
    return gathers_of_own_samples(blended, delays, thresholds)


def solution(mesh):
    return jax.shard_map(
        local,
        mesh=mesh,
        in_specs=(P(None, "shot", "tm"), P(), P()),
        out_specs=P(None, "shot", "tm"),
        check_vma=False,
    )
```

```python
import functools
import math

import jax
import jax.numpy as jnp
import ml_dtypes
import numpy as np
from jax import lax
from jax.experimental import pallas as pl
from jax.experimental.pallas import tpu as pltpu
from jax.sharding import PartitionSpec as P

SRC = 64
SRC_EXP = 2
WIN = 256
BLK = 128
ITERS = 2


RELAX = 0.5
HALF = WIN // 2
SUB = 8
TILE = 256


def bfloat_scale(table):
    values = np.unique(np.abs(table).round(12))
    factors = 1.0 + np.arange(4096) / 4096.0
    scaled = factors[:, None] * values
    lost = scaled.astype(ml_dtypes.bfloat16).astype(np.float64) - scaled
    return factors[np.argmin(np.sum((lost / factors[:, None]) ** 2, axis=1))]


def half_spectrum_tables():
    moment = np.arange(WIN)
    angle = (moment[:, None] * np.arange(HALF)[None, :] % WIN) * (2.0 * math.pi / WIN)
    nyquist = np.where(moment % 2 == 0, 1.0, -1.0)
    sine = -np.sin(angle)
    sine[:, 0] = nyquist
    forward = np.concatenate([np.cos(angle), sine], axis=1).astype(ml_dtypes.bfloat16)
    inverse = np.concatenate([np.cos(angle), sine], axis=1).T / math.sqrt(WIN)
    inverse[0] *= 0.5
    inverse[HALF] *= 0.5
    source = np.arange(SRC)
    turn = (source[:, None] * source[None, :] % SRC) * (2.0 * math.pi / SRC)
    cosine, sine = np.cos(turn) / math.sqrt(SRC), np.sin(turn) / math.sqrt(SRC)
    onward = np.block([[cosine, sine], [-sine, cosine]])
    time_scale = bfloat_scale(inverse)
    forward, inverse = (x.astype(ml_dtypes.bfloat16) for x in (forward, inverse * time_scale))
    tables = forward, inverse, high_and_low(onward / math.sqrt(WIN)), high_and_low(onward.T)
    return tables, 1.0 / time_scale


def high_and_low(table):
    high = table.astype(ml_dtypes.bfloat16)
    low = (table - high.astype(np.float64)).astype(ml_dtypes.bfloat16)
    return np.concatenate([high, low], axis=1)


def rearranging(shape, axes):
    order = np.arange(math.prod(shape)).reshape(shape).transpose(axes).reshape(-1)
    return np.eye(order.size)[order].astype(ml_dtypes.bfloat16)


def order_tables(windows, own, blocks_of_time):
    shots, sources = TILE // (2 * windows * own), TILE // windows
    return (
        rearranging(
            (blocks_of_time, shots, windows // blocks_of_time, 2, own), (1, 4, 3, 0, 2)
        ),
        rearranging((sources, windows), (1, 0)),
        rearranging((windows, sources), (1, 0)),
    )


def product(left, right):
    return jnp.dot(left, right, preferred_element_type=jnp.float32)


def gather_kernel(
    shots,
    kept_scale,
    delays_far,
    limits,
    received,
    tables,
    out,
    delays,
    records,
    field,
    mixed,
    back,
    firsts,
    estimates,
    sem,
):
    copy = pltpu.make_async_copy(delays_far, delays, sem)
    copy.start()
    forward, inverse, order_arrived, order_windows, order_sources = (
        tables.at[pl.ds(at * TILE, TILE)] for at in range(5)
    )
    onward, backward = (
        tables.at[pl.ds(5 * TILE + at * 2 * SRC, 2 * SRC)] for at in range(2)
    )
    count, receivers, rows, _ = received.shape
    blocks_of_time = count // shots
    experiments, sources = delays.shape[1], SRC
    windows = blocks_of_time * rows * shots // (2 * experiments)
    groups = receivers * windows
    parts = windows // blocks_of_time
    some = TILE // windows
    lane = lax.broadcasted_iota(jnp.int32, (windows, BLK), 1)
    row = lax.broadcasted_iota(jnp.int32, (windows, BLK), 0)
    lane_of_group = lax.broadcasted_iota(jnp.int32, (sources, HALF), 1)
    lane_of_some = lax.broadcasted_iota(jnp.int32, (some, HALF), 1)

    senders = TILE // (rows * blocks_of_time)
    bounds = []
    for sweep in range(ITERS):
        limit = limits[sweep : sweep + 1, :] * kept_scale
        p = lax.broadcasted_iota(jnp.int32, (sources, sources), 0)
        q = lax.broadcasted_iota(jnp.int32, (sources, sources), 1)
        bound = jnp.sum(jnp.where(p == q, limit, 0.0), axis=1, keepdims=True)
        mirrored = (p + q == 0) | (p + q == sources)
        bound_mirrored = jnp.sum(jnp.where(mirrored, limit, 0.0), axis=1, keepdims=True)
        bounds.append((bound, bound_mirrored))

    arrived = [
        jnp.concatenate(
            [
                received[pl.ds(block * shots + chunk * senders, senders), r].reshape(-1, BLK)
                for block in range(blocks_of_time)
            ],
            axis=0,
        )
        for chunk in range(sources // some)
        for r in range(receivers)
    ]
    records[...] = product(order_arrived[...], jnp.concatenate(arrived, axis=1))

    copy.wait()

    def advanced(even, odd, delay):
        by = (BLK - delay) & (BLK - 1)
        even, odd = pltpu.roll(even, by, 1), pltpu.roll(odd, by, 1)
        after = jnp.where(row < windows - 1, pltpu.roll(even, windows - 1, 0), 0.0)
        same = lane < BLK - delay
        return jnp.where(same, even, odd), jnp.where(same, odd, after)

    def moved_by(even, odd, ahead_by):
        ahead = ahead_by >= 0
        by = (BLK - ahead_by) & (BLK - 1)
        even, odd = pltpu.roll(even, by, 1), pltpu.roll(odd, by, 1)
        other = pltpu.roll(jnp.where(ahead, even, odd), jnp.where(ahead, windows - 1, 1), 0)
        other = jnp.where(row != jnp.where(ahead, windows - 1, 0), other, 0.0)
        same = ((lane + ahead_by) & -BLK) == 0
        return (
            jnp.where(same, even, jnp.where(ahead, odd, other)),
            jnp.where(same, odd, jnp.where(ahead, other, even)),
        )

    def columns(group):
        return slice(group * HALF, (group + 1) * HALF)

    def first_update(r, chunk):
        updated = []
        for at in range(0, some, SRC_EXP):
            even, odd = (
                records[pl.ds((at + half) * windows, windows), columns(chunk * receivers + r)]
                for half in range(2)
            )
            for k in range(SRC_EXP):
                early = advanced(even, odd, delays[k, (chunk * some + at) // SRC_EXP])
                updated.append(jnp.concatenate([RELAX * x for x in early], axis=1))
        updated = jnp.concatenate(updated, axis=0).astype(jnp.bfloat16)
        firsts[pl.ds((r * sources + chunk * some) * windows, TILE), :] = updated
        return updated

    def side_by_side(values):
        return jnp.concatenate(values, axis=1)

    def estimates_by_source():
        parts_of_rows = []
        for r, chunk in turns:
            starts = [(r * windows + w) * sources + chunk * some for w in range(windows)]
            rows_of_part = [estimates[start : start + some, :] for start in starts]
            parts_of_rows.append(jnp.concatenate(rows_of_part, axis=0))
        return product(order_sources[...], side_by_side(parts_of_rows))

    def later_update(r, chunk, before):
        first = (r * sources + chunk * some) * windows
        updated = []
        for at in range(0, some, SRC_EXP):
            lags = [delays[k, (chunk * some + at) // SRC_EXP] for k in range(SRC_EXP)]
            spread = firsts[pl.ds(first + at * windows, SRC_EXP * windows), :]
            spread = spread.astype(jnp.float32)
            estimate = [
                tuple(
                    before[(at + k) * windows : (at + k + 1) * windows, columns(half)]
                    for half in range(2)
                )
                for k in range(SRC_EXP)
            ]
            for k in range(SRC_EXP):
                even, odd = estimate[k]
                other = moved_by(*estimate[1 - k], lags[k] - lags[1 - k])
                stays = (row < windows - 1) | (lane < BLK - lags[k])
                even = RELAX * (even - other[0])
                odd = jnp.where(stays, RELAX * (odd - other[1]), odd)
                step = spread[k * windows : (k + 1) * windows]
                updated.append(jnp.concatenate([even, odd], axis=1) + step)
        return jnp.concatenate(updated, axis=0).astype(jnp.bfloat16)

    turns = [(r, chunk) for r in range(receivers) for chunk in range(sources // some)]

    def update_and_forward_in_time(sweep):
        if sweep:
            before = estimates_by_source()
            updates = [
                later_update(r, chunk, before[:, at * WIN : (at + 1) * WIN])
                for at, (r, chunk) in enumerate(turns)
            ]
        else:
            updates = [first_update(r, chunk) for r, chunk in turns]
        signal = product(order_windows[...], side_by_side(updates)).astype(jnp.bfloat16)
        signal = [signal[:, at * WIN : (at + 1) * WIN] for at in range(len(turns))]
        spectra = product(jnp.concatenate(signal, axis=0), forward[...])
        nyquists = [jnp.zeros((some, HALF), jnp.float32) for _ in range(sources // some)]
        for at, (r, chunk) in enumerate(turns):
            for w in range(windows):
                group = r * windows + w
                start = at * TILE + w * some
                real, imag = (spectra[start : start + some, columns(half)] for half in range(2))
                moved = pltpu.roll(imag, group, 1) if group else imag
                nyquists[chunk] = jnp.where(lane_of_some == group, moved, nyquists[chunk])
                imag = jnp.where(lane_of_some == 0, 0.0, imag)
                put(field, columns(group), real, imag, chunk * some)
        for chunk, nyquist in enumerate(nyquists):
            put(field, columns(groups), nyquist, jnp.zeros_like(nyquist), chunk * some)

    def put(ref, where, real, imag, first=0):
        for at, value in enumerate((real, imag)):
            start = at * sources + first
            ref[start : start + value.shape[0], where] = value.astype(jnp.bfloat16)

    def mixing(table, ref):
        values = ref[...]
        total = product(table[...], jnp.concatenate([values, values], axis=0))
        return total[:sources], total[sources:]

    def shrink(sweep):
        bound, bound_mirrored = bounds[sweep]
        real, imag = mixing(onward, field)
        inverse_size = lax.rsqrt(real * real + imag * imag)
        factor = jnp.maximum(kept_scale - bound * inverse_size, 0.0) + jnp.maximum(
            kept_scale - bound_mirrored * inverse_size, 0.0
        )
        put(mixed, slice(None), real * factor, imag * factor)

    def back_in_source():
        real, imag = mixing(backward, mixed)
        nyquist = real[:, columns(groups)]
        for group in range(groups):
            moved = pltpu.roll(nyquist, HALF - group, 1) if group else nyquist
            own_imag = jnp.where(lane_of_group == 0, moved, imag[:, columns(group)])
            rows_of_group = slice(group * sources, (group + 1) * sources)
            for half, value in enumerate((real[:, columns(group)], own_imag)):
                back[rows_of_group, columns(half)] = value.astype(jnp.bfloat16)

    def swapped(value):
        return pltpu.roll(value, SUB // 2, 1)

    def deliver(r, w, restored):
        low = lax.broadcasted_iota(jnp.int32, (sources // SUB, SUB, BLK), 1) < SUB // 2
        pieces = []
        for part in range(2):
            window = restored[part * sources : (part + 1) * sources]
            even = window[:, :BLK].reshape(sources // SUB, SUB, BLK)
            odd = window[:, BLK:].reshape(sources // SUB, SUB, BLK)
            pieces.append(
                (jnp.where(low, even, swapped(odd)), jnp.where(low, swapped(even), odd))
            )
        block, inside = w // parts, w % parts
        for side in range(2):
            both = jnp.concatenate([pieces[0][side], pieces[1][side]], axis=1)
            both = both.astype(jnp.bfloat16)
            for k in range(sources // SUB):
                target = block * shots + 2 * k + side
                out[target, r, inside * SUB : (inside + 2) * SUB, :] = both[k]

    for sweep in range(ITERS):
        update_and_forward_in_time(sweep)
        shrink(sweep)
        back_in_source()
        restored = product(back[...], inverse[...])
        if sweep < ITERS - 1:
            estimates[...] = restored.astype(jnp.bfloat16)
            continue
        for group in range(0, groups, 2):
            pair = restored[group * sources : (group + 2) * sources]
            deliver(group // windows, group % windows, pair)


def cast_kernel(blended, delays, limits, sent, delays_near, limits_near, held, sems):
    pieces = sems.shape[0] - 2
    count = blended.shape[0] // pieces
    spans = [pl.ds(at * count, count) for at in range(pieces)]
    copies = [
        pltpu.make_async_copy(blended.at[span], held.at[span], sems.at[at])
        for at, span in enumerate(spans)
    ]
    small = [
        pltpu.make_async_copy(delays, delays_near, sems.at[pieces]),
        pltpu.make_async_copy(limits, limits_near, sems.at[pieces + 1]),
    ]
    for copy in copies + small:
        copy.start()
    for copy, span in zip(copies, spans):
        copy.wait()
        sent[span] = held[span].astype(jnp.bfloat16)
    for copy in small:
        copy.wait()


def gathers_of_all_samples(shots, blended, delays, thresholds):
    receivers, own, samples = blended.shape
    blocks_of_time = lax.axis_size("tm")
    count = shots * blocks_of_time
    each = receivers // count
    blocks = samples // BLK
    windows = samples * blocks_of_time // WIN
    groups = each * windows
    rows = blocks * own
    sent = blended.reshape(receivers, own, blocks, BLK).transpose(0, 2, 1, 3)
    sent = sent.reshape(count, each, rows, BLK)
    vmem, far = pl.BlockSpec(memory_space=pltpu.VMEM), pl.BlockSpec(memory_space=pl.ANY)

    def kept_far(array):
        return pltpu.with_memory_space_constraint(array, pltpu.HBM)

    sent, delays, thresholds = pl.pallas_call(
        cast_kernel,
        out_shape=(
            jax.ShapeDtypeStruct(sent.shape, jnp.bfloat16),
            jax.ShapeDtypeStruct(delays.T.shape, delays.dtype),
            jax.ShapeDtypeStruct(thresholds.shape, thresholds.dtype),
        ),
        in_specs=[far] * 3,
        out_specs=[vmem] * 3,
        scratch_shapes=[
            pltpu.VMEM(sent.shape, jnp.float32),
            pltpu.SemaphoreType.DMA((1 + 2,)),
        ],
        compiler_params=pltpu.CompilerParams(vmem_limit_bytes=8 * 1024 * 1024),
    )(kept_far(sent), kept_far(delays.T), kept_far(thresholds))
    received = lax.all_to_all(sent, ("tm", "shot"), split_axis=0, concat_axis=0, tiled=True)
    tables, kept_scale = half_spectrum_tables()
    tables = np.concatenate(tables[:2] + order_tables(windows, own, blocks_of_time) + tables[2:], axis=0)
    held = SRC // shots
    restored = pl.pallas_call(
        functools.partial(gather_kernel, shots, float(kept_scale)),
        out_shape=jax.ShapeDtypeStruct((count, each, blocks * held, BLK), jnp.bfloat16),
        in_specs=[pl.BlockSpec(memory_space=pl.ANY)] + [vmem] * 3,
        out_specs=vmem,
        scratch_shapes=[
            pltpu.SMEM(delays.shape, jnp.int32),
            pltpu.VMEM((TILE, SRC * windows // TILE * each * BLK), jnp.float32),
            pltpu.VMEM((2 * SRC, (groups + 1) * HALF), jnp.bfloat16),
            pltpu.VMEM((2 * SRC, (groups + 1) * HALF), jnp.bfloat16),
            pltpu.VMEM((groups * SRC, WIN), jnp.bfloat16),
            pltpu.VMEM((groups * SRC, WIN), jnp.bfloat16),
            pltpu.VMEM((groups * SRC, WIN), jnp.bfloat16),
            pltpu.SemaphoreType.DMA(()),
        ],
        compiler_params=pltpu.CompilerParams(vmem_limit_bytes=40 * 1024 * 1024),
        cost_estimate=pl.CostEstimate(
            flops=2 * ITERS * groups * SRC * WIN * WIN * 5,
            bytes_accessed=2 * 1024 * 1024,
            transcendentals=ITERS * groups * SRC * HALF,
        ),
    )(delays, thresholds, received, jnp.asarray(tables))
    final = lax.all_to_all(restored, ("tm", "shot"), split_axis=0, concat_axis=0, tiled=True)
    final = final.reshape(receivers, blocks, held, BLK).transpose(0, 2, 1, 3)
    return final.reshape(receivers, held, samples)


def shifted(array, axis, by):
    count = lax.axis_size(axis)
    pairs = [(i, i + by) for i in range(count) if 0 <= i + by < count]
    return lax.ppermute(array, axis, pairs)


def phase_table(length_first, length_second, period):
    first_index = jnp.arange(length_first, dtype=jnp.int32)[:, None]
    second_index = jnp.arange(length_second, dtype=jnp.int32)[None, :]
    return (first_index * second_index % period).astype(jnp.float32) * (2.0 * math.pi / period)


def make_tables():
    time_angle = phase_table(WIN, WIN, WIN)
    time_scale = 1.0 / math.sqrt(WIN)
    cos_forward = jnp.cos(time_angle).astype(jnp.bfloat16)
    sin_forward = -jnp.sin(time_angle).astype(jnp.bfloat16)
    cos_inverse = jnp.cos(time_angle) * time_scale
    sin_inverse = -jnp.sin(time_angle) * time_scale
    source_angle = phase_table(SRC, SRC, SRC)
    cos_source = jnp.cos(source_angle) / math.sqrt(SRC)
    sin_source = jnp.sin(source_angle) / math.sqrt(SRC)
    return (cos_forward, sin_forward, cos_inverse, sin_inverse, cos_source, sin_source)


def blend(estimate, own_delays):
    receivers, sources, samples = estimate.shape
    blocks = samples // BLK
    experiments = sources // SRC_EXP
    earlier = shifted(estimate[:, :, samples - BLK :], "tm", 1)
    upper = estimate.reshape(receivers, sources, blocks, BLK)
    shifts = own_delays.reshape(-1)
    row_index = jnp.arange(BLK, dtype=jnp.int32)[None, :, None]
    column_index = jnp.arange(BLK, dtype=jnp.int32)[None, None, :]
    select_same = (row_index == column_index - shifts[:, None, None]).astype(jnp.bfloat16)
    select_prior = (row_index == BLK + column_index - shifts[:, None, None]).astype(jnp.bfloat16)
    same = jnp.einsum("rsnb,sbi->rsni", upper, select_same, preferred_element_type=jnp.float32)
    onward = jnp.einsum("rsnb,sbi->rsni", upper, select_prior, preferred_element_type=jnp.float32)
    edge_part = jnp.einsum(
        "rsb,sbi->rsi", earlier, select_prior, preferred_element_type=jnp.float32
    )
    same = jnp.sum(same.reshape(receivers, experiments, SRC_EXP, blocks, BLK), axis=2)
    onward = jnp.sum(onward.reshape(receivers, experiments, SRC_EXP, blocks, BLK), axis=2)
    edge_part = jnp.sum(edge_part.reshape(receivers, experiments, SRC_EXP, BLK), axis=2)
    carried = jnp.concatenate([edge_part[:, :, None], onward[:, :, : blocks - 1]], axis=2)
    return (same + carried).reshape(receivers, experiments, samples)


def spread(residual, own_delays):
    receivers, experiments, samples = residual.shape
    blocks = samples // BLK
    later = shifted(residual[:, :, :BLK], "tm", -1)
    lower = residual.reshape(receivers, experiments, blocks, BLK)
    row_index = jnp.arange(BLK, dtype=jnp.int32)[None, None, :, None]
    column_index = jnp.arange(BLK, dtype=jnp.int32)[None, None, None, :]
    select_same = (row_index == column_index + own_delays[:, :, None, None]).astype(jnp.bfloat16)
    select_next = (row_index + BLK == column_index + own_delays[:, :, None, None]).astype(
        jnp.bfloat16
    )
    same = jnp.einsum("rena,ekai->rekni", lower, select_same, preferred_element_type=jnp.float32)
    backward = jnp.einsum(
        "rena,ekai->rekni", lower, select_next, preferred_element_type=jnp.float32
    )
    edge_part = jnp.einsum("rea,ekai->reki", later, select_next, preferred_element_type=jnp.float32)
    carried = jnp.concatenate([backward[:, :, :, 1:], edge_part[:, :, :, None]], axis=3)
    return (same + carried).reshape(receivers, experiments * SRC_EXP, samples)


def coherence(gathers, limits, tables):
    cos_forward, sin_forward, cos_inverse, sin_inverse, cos_source, sin_source = tables
    receivers, sources, samples = gathers.shape
    windows = samples // WIN
    careful = lax.Precision.HIGH
    scale = 1.0 / math.sqrt(WIN)
    signal = gathers.reshape(receivers * sources * windows, WIN)
    real_time = (jnp.dot(signal, cos_forward, preferred_element_type=jnp.float32) * scale).reshape(
        receivers, sources, samples
    )
    imag_time = (jnp.dot(signal, sin_forward, preferred_element_type=jnp.float32) * scale).reshape(
        receivers, sources, samples
    )

    def mixing(table, field):
        return jnp.einsum(
            "ps,rsx->rpx", table, field, precision=careful, preferred_element_type=jnp.float32
        )

    real_part = mixing(cos_source, real_time) + mixing(sin_source, imag_time)
    imag_part = mixing(cos_source, imag_time) - mixing(sin_source, real_time)
    magnitude = jnp.sqrt(real_part * real_part + imag_part * imag_part)
    bound = limits[None, :, None]
    factor = jnp.maximum(magnitude - bound, 0.0) / jnp.maximum(magnitude, bound)
    kept_real = real_part * factor
    kept_imag = imag_part * factor
    back_real = mixing(cos_source, kept_real) - mixing(sin_source, kept_imag)
    back_imag = mixing(cos_source, kept_imag) + mixing(sin_source, kept_real)
    restored = jnp.dot(
        back_real.reshape(-1, WIN),
        cos_inverse,
        precision=careful,
        preferred_element_type=jnp.float32,
    )
    restored = restored + jnp.dot(
        back_imag.reshape(-1, WIN),
        sin_inverse,
        precision=careful,
        preferred_element_type=jnp.float32,
    )
    return restored.reshape(receivers, sources, samples)


def gathers_of_own_samples(blended, delays, thresholds):
    tables = make_tables()
    local_count = blended.shape[1]
    own_delays = lax.dynamic_slice_in_dim(
        delays, lax.axis_index("shot") * local_count, local_count, 0
    )
    estimate = None
    for sweep in range(ITERS):
        if sweep == 0:
            residual = blended.astype(jnp.bfloat16)
            update = (RELAX * spread(residual, own_delays)).astype(jnp.bfloat16)
        else:
            residual = (blended - blend(estimate, own_delays)).astype(jnp.bfloat16)
            update = (estimate.astype(jnp.float32) + RELAX * spread(residual, own_delays)).astype(
                jnp.bfloat16
            )
        gathers = lax.all_to_all(update, "shot", split_axis=0, concat_axis=1, tiled=True)
        filtered = coherence(gathers, thresholds[sweep], tables).astype(jnp.bfloat16)
        estimate = lax.all_to_all(filtered, "shot", split_axis=1, concat_axis=0, tiled=True)
    return estimate


def whole_receivers_fit(shots, blocks_of_time, receivers, samples):
    held, windows = SRC // shots, samples // WIN
    return (
        receivers % (shots * blocks_of_time) == 0
        and held * 2 == SUB
        and windows % 2 == 0
        and windows * blocks_of_time == SUB
        and receivers // (shots * blocks_of_time) * SUB <= HALF
    )


def local(blended, delays, thresholds):
    shots, blocks_of_time = lax.axis_size("shot"), lax.axis_size("tm")
    if whole_receivers_fit(shots, blocks_of_time, blended.shape[0], blended.shape[2]):
        return gathers_of_all_samples(shots, blended, delays, thresholds)
    return gathers_of_own_samples(blended, delays, thresholds)


def solution(mesh):
    return jax.shard_map(
        local,
        mesh=mesh,
        in_specs=(P(None, "shot", "tm"), P(), P()),
        out_specs=P(None, "shot", "tm"),
        check_vma=False,
    )
```

```python
import functools
import math

import jax
import jax.numpy as jnp
import ml_dtypes
import numpy as np
from jax import lax
from jax.experimental import pallas as pl
from jax.experimental.pallas import tpu as pltpu
from jax.sharding import PartitionSpec as P

SRC = 64
SRC_EXP = 2
WIN = 256
BLK = 128
ITERS = 2


RELAX = 0.5
HALF = WIN // 2
SUB = 8
TILE = 256
NEAR = 4


def bfloat_scale(table):
    values = np.unique(np.abs(table).round(12))
    factors = 1.0 + np.arange(4096) / 4096.0
    scaled = factors[:, None] * values
    lost = scaled.astype(ml_dtypes.bfloat16).astype(np.float64) - scaled
    return factors[np.argmin(np.sum((lost / factors[:, None]) ** 2, axis=1))]


def half_spectrum_tables():
    moment = np.arange(WIN)
    angle = (moment[:, None] * np.arange(HALF)[None, :] % WIN) * (2.0 * math.pi / WIN)
    nyquist = np.where(moment % 2 == 0, 1.0, -1.0)
    sine = -np.sin(angle)
    sine[:, 0] = nyquist
    forward = np.concatenate([np.cos(angle), sine], axis=1).astype(ml_dtypes.bfloat16)
    inverse = np.concatenate([np.cos(angle), sine], axis=1).T / math.sqrt(WIN)
    inverse[0] *= 0.5
    inverse[HALF] *= 0.5
    source = np.arange(SRC)
    turn = (source[:, None] * source[None, :] % SRC) * (2.0 * math.pi / SRC)
    cosine, sine = np.cos(turn) / math.sqrt(SRC), np.sin(turn) / math.sqrt(SRC)
    onward = np.block([[cosine, sine], [-sine, cosine]])
    time_scale = bfloat_scale(inverse)
    forward, inverse = (x.astype(ml_dtypes.bfloat16) for x in (forward, inverse * time_scale))
    tables = forward, inverse, high_and_low(onward / math.sqrt(WIN)), high_and_low(onward.T)
    return tables, 1.0 / time_scale


def high_and_low(table):
    high = table.astype(ml_dtypes.bfloat16)
    low = (table - high.astype(np.float64)).astype(ml_dtypes.bfloat16)
    return np.concatenate([high, low], axis=1)


def rearranging(shape, axes):
    order = np.arange(math.prod(shape)).reshape(shape).transpose(axes).reshape(-1)
    return np.eye(order.size)[order].astype(ml_dtypes.bfloat16)


def order_tables(windows, own, blocks_of_time):
    shots, sources = TILE // (2 * windows * own), TILE // windows
    return (
        rearranging(
            (blocks_of_time, NEAR, shots // NEAR, windows // blocks_of_time, 2, own),
            (2, 1, 5, 4, 0, 3),
        ),
        rearranging((sources, windows), (1, 0)),
        rearranging((windows, sources), (1, 0)),
    )


def product(left, right):
    return jnp.dot(left, right, preferred_element_type=jnp.float32)


def gather_kernel(
    shots,
    kept_scale,
    delays_far,
    limits,
    received,
    tables,
    out,
    delays,
    records,
    field,
    mixed,
    back,
    firsts,
    estimates,
    sem,
):
    copy = pltpu.make_async_copy(delays_far, delays, sem)
    copy.start()
    forward, inverse, order_arrived, order_windows, order_sources = (
        tables.at[pl.ds(at * TILE, TILE)] for at in range(5)
    )
    onward, backward = (
        tables.at[pl.ds(5 * TILE + at * 2 * SRC, 2 * SRC)] for at in range(2)
    )
    count, receivers, rows, _ = received.shape
    blocks_of_time = count // shots
    experiments, sources = delays.shape[1], SRC
    windows = blocks_of_time * rows * shots // (2 * experiments)
    groups = receivers * windows
    parts = windows // blocks_of_time
    some = TILE // windows
    lane = lax.broadcasted_iota(jnp.int32, (windows, BLK), 1)
    row = lax.broadcasted_iota(jnp.int32, (windows, BLK), 0)
    lane_of_group = lax.broadcasted_iota(jnp.int32, (sources, HALF), 1)
    lane_of_some = lax.broadcasted_iota(jnp.int32, (some, HALF), 1)

    planes, some_planes = shots // NEAR, TILE // (rows * blocks_of_time * NEAR)
    bounds = []
    for sweep in range(ITERS):
        limit = limits[sweep : sweep + 1, :] * kept_scale
        p = lax.broadcasted_iota(jnp.int32, (sources, sources), 0)
        q = lax.broadcasted_iota(jnp.int32, (sources, sources), 1)
        bound = jnp.sum(jnp.where(p == q, limit, 0.0), axis=1, keepdims=True)
        mirrored = (p + q == 0) | (p + q == sources)
        bound_mirrored = jnp.sum(jnp.where(mirrored, limit, 0.0), axis=1, keepdims=True)
        bounds.append((bound, bound_mirrored))

    arrived = [
        jnp.concatenate(
            [
                received[pl.ds(side * planes + chunk * some_planes, some_planes), r].reshape(-1, BLK)
                for side in range(blocks_of_time * NEAR)
            ],
            axis=0,
        )
        for chunk in range(sources // some)
        for r in range(receivers)
    ]
    records[...] = product(order_arrived[...], jnp.concatenate(arrived, axis=1))

    copy.wait()

    def advanced(even, odd, delay):
        by = (BLK - delay) & (BLK - 1)
        even, odd = pltpu.roll(even, by, 1), pltpu.roll(odd, by, 1)
        after = jnp.where(row < windows - 1, pltpu.roll(even, windows - 1, 0), 0.0)
        same = lane < BLK - delay
        return jnp.where(same, even, odd), jnp.where(same, odd, after)

    def moved_by(even, odd, ahead_by):
        ahead = ahead_by >= 0
        by = (BLK - ahead_by) & (BLK - 1)
        even, odd = pltpu.roll(even, by, 1), pltpu.roll(odd, by, 1)
        other = pltpu.roll(jnp.where(ahead, even, odd), jnp.where(ahead, windows - 1, 1), 0)
        other = jnp.where(row != jnp.where(ahead, windows - 1, 0), other, 0.0)
        same = ((lane + ahead_by) & -BLK) == 0
        return (
            jnp.where(same, even, jnp.where(ahead, odd, other)),
            jnp.where(same, odd, jnp.where(ahead, other, even)),
        )

    def columns(group):
        return slice(group * HALF, (group + 1) * HALF)

    def first_update(r, chunk):
        updated = []
        for at in range(0, some, SRC_EXP):
            even, odd = (
                records[pl.ds((at + half) * windows, windows), columns(chunk * receivers + r)]
                for half in range(2)
            )
            for k in range(SRC_EXP):
                early = advanced(even, odd, delays[k, (chunk * some + at) // SRC_EXP])
                updated.append(jnp.concatenate([RELAX * x for x in early], axis=1))
        updated = jnp.concatenate(updated, axis=0).astype(jnp.bfloat16)
        firsts[pl.ds((r * sources + chunk * some) * windows, TILE), :] = updated
        return updated

    def side_by_side(values):
        return jnp.concatenate(values, axis=1)

    def estimates_by_source():
        parts_of_rows = []
        for r, chunk in turns:
            starts = [(r * windows + w) * sources + chunk * some for w in range(windows)]
            rows_of_part = [estimates[start : start + some, :] for start in starts]
            parts_of_rows.append(jnp.concatenate(rows_of_part, axis=0))
        return product(order_sources[...], side_by_side(parts_of_rows))

    def later_update(r, chunk, before):
        first = (r * sources + chunk * some) * windows
        updated = []
        for at in range(0, some, SRC_EXP):
            lags = [delays[k, (chunk * some + at) // SRC_EXP] for k in range(SRC_EXP)]
            spread = firsts[pl.ds(first + at * windows, SRC_EXP * windows), :]
            spread = spread.astype(jnp.float32)
            estimate = [
                tuple(
                    before[(at + k) * windows : (at + k + 1) * windows, columns(half)]
                    for half in range(2)
                )
                for k in range(SRC_EXP)
            ]
            for k in range(SRC_EXP):
                even, odd = estimate[k]
                other = moved_by(*estimate[1 - k], lags[k] - lags[1 - k])
                stays = (row < windows - 1) | (lane < BLK - lags[k])
                even = RELAX * (even - other[0])
                odd = jnp.where(stays, RELAX * (odd - other[1]), odd)
                step = spread[k * windows : (k + 1) * windows]
                updated.append(jnp.concatenate([even, odd], axis=1) + step)
        return jnp.concatenate(updated, axis=0).astype(jnp.bfloat16)

    turns = [(r, chunk) for r in range(receivers) for chunk in range(sources // some)]

    def update_and_forward_in_time(sweep):
        if sweep:
            before = estimates_by_source()
            updates = [
                later_update(r, chunk, before[:, at * WIN : (at + 1) * WIN])
                for at, (r, chunk) in enumerate(turns)
            ]
        else:
            updates = [first_update(r, chunk) for r, chunk in turns]
        signal = product(order_windows[...], side_by_side(updates)).astype(jnp.bfloat16)
        signal = [signal[:, at * WIN : (at + 1) * WIN] for at in range(len(turns))]
        spectra = product(jnp.concatenate(signal, axis=0), forward[...])
        nyquists = [jnp.zeros((some, HALF), jnp.float32) for _ in range(sources // some)]
        for at, (r, chunk) in enumerate(turns):
            for w in range(windows):
                group = r * windows + w
                start = at * TILE + w * some
                real, imag = (spectra[start : start + some, columns(half)] for half in range(2))
                moved = pltpu.roll(imag, group, 1) if group else imag
                nyquists[chunk] = jnp.where(lane_of_some == group, moved, nyquists[chunk])
                imag = jnp.where(lane_of_some == 0, 0.0, imag)
                put(field, columns(group), real, imag, chunk * some)
        for chunk, nyquist in enumerate(nyquists):
            put(field, columns(groups), nyquist, jnp.zeros_like(nyquist), chunk * some)

    def put(ref, where, real, imag, first=0):
        for at, value in enumerate((real, imag)):
            start = at * sources + first
            ref[start : start + value.shape[0], where] = value.astype(jnp.bfloat16)

    def mixing(table, ref):
        values = ref[...]
        total = product(table[...], jnp.concatenate([values, values], axis=0))
        return total[:sources], total[sources:]

    def shrink(sweep):
        bound, bound_mirrored = bounds[sweep]
        real, imag = mixing(onward, field)
        inverse_size = lax.rsqrt(real * real + imag * imag)
        factor = jnp.maximum(kept_scale - bound * inverse_size, 0.0) + jnp.maximum(
            kept_scale - bound_mirrored * inverse_size, 0.0
        )
        put(mixed, slice(None), real * factor, imag * factor)

    def back_in_source():
        real, imag = mixing(backward, mixed)
        nyquist = real[:, columns(groups)]
        for group in range(groups):
            moved = pltpu.roll(nyquist, HALF - group, 1) if group else nyquist
            own_imag = jnp.where(lane_of_group == 0, moved, imag[:, columns(group)])
            rows_of_group = slice(group * sources, (group + 1) * sources)
            for half, value in enumerate((real[:, columns(group)], own_imag)):
                back[rows_of_group, columns(half)] = value.astype(jnp.bfloat16)

    def swapped(value):
        return pltpu.roll(value, SUB // 2, 1)

    def deliver(r, w, restored):
        low = lax.broadcasted_iota(jnp.int32, (sources // SUB, SUB, BLK), 1) < SUB // 2
        pieces = []
        for part in range(2):
            window = restored[part * sources : (part + 1) * sources]
            even = window[:, :BLK].reshape(sources // SUB, SUB, BLK)
            odd = window[:, BLK:].reshape(sources // SUB, SUB, BLK)
            pieces.append(
                (jnp.where(low, even, swapped(odd)), jnp.where(low, swapped(even), odd))
            )
        block, inside = w // parts, w % parts
        for side in range(2):
            both = jnp.concatenate([pieces[0][side], pieces[1][side]], axis=1)
            both = both.astype(jnp.bfloat16)
            for k in range(sources // SUB):
                plane, near = divmod(2 * k + side, NEAR)
                target = (block * NEAR + near) * planes + plane
                out[target, r, inside * SUB : (inside + 2) * SUB, :] = both[k]

    for sweep in range(ITERS):
        update_and_forward_in_time(sweep)
        shrink(sweep)
        back_in_source()
        restored = product(back[...], inverse[...])
        if sweep < ITERS - 1:
            estimates[...] = restored.astype(jnp.bfloat16)
            continue
        for group in range(0, groups, 2):
            pair = restored[group * sources : (group + 2) * sources]
            deliver(group // windows, group % windows, pair)


def cast_kernel(blended, delays, limits, sent, delays_near, limits_near, held, sems):
    pieces = sems.shape[0] - 2
    count = blended.shape[0] // pieces
    spans = [pl.ds(at * count, count) for at in range(pieces)]
    copies = [
        pltpu.make_async_copy(blended.at[span], held.at[span], sems.at[at])
        for at, span in enumerate(spans)
    ]
    small = [
        pltpu.make_async_copy(delays, delays_near, sems.at[pieces]),
        pltpu.make_async_copy(limits, limits_near, sems.at[pieces + 1]),
    ]
    for copy in copies + small:
        copy.start()
    for copy, span in zip(copies, spans):
        copy.wait()
        sent[span] = held[span].astype(jnp.bfloat16)
    for copy in small:
        copy.wait()


def gathers_of_all_samples(shots, blended, delays, thresholds):
    receivers, own, samples = blended.shape
    blocks_of_time = lax.axis_size("tm")
    count = shots * blocks_of_time
    each = receivers // count
    blocks = samples // BLK
    windows = samples * blocks_of_time // WIN
    groups = each * windows
    rows = blocks * own
    sent = blended.reshape(receivers, own, blocks, BLK).transpose(0, 2, 1, 3)
    sent = sent.reshape(count, each, rows, BLK)
    vmem, far = pl.BlockSpec(memory_space=pltpu.VMEM), pl.BlockSpec(memory_space=pl.ANY)

    def kept_far(array):
        return pltpu.with_memory_space_constraint(array, pltpu.HBM)

    sent, delays, thresholds = pl.pallas_call(
        cast_kernel,
        out_shape=(
            jax.ShapeDtypeStruct(sent.shape, jnp.bfloat16),
            jax.ShapeDtypeStruct(delays.T.shape, delays.dtype),
            jax.ShapeDtypeStruct(thresholds.shape, thresholds.dtype),
        ),
        in_specs=[far] * 3,
        out_specs=[vmem] * 3,
        scratch_shapes=[
            pltpu.VMEM(sent.shape, jnp.float32),
            pltpu.SemaphoreType.DMA((1 + 2,)),
        ],
        compiler_params=pltpu.CompilerParams(vmem_limit_bytes=8 * 1024 * 1024),
    )(kept_far(sent), kept_far(delays.T), kept_far(thresholds))
    order = [
        (plane * NEAR + near) * blocks_of_time + block
        for block in range(blocks_of_time)
        for near in range(NEAR)
        for plane in range(shots // NEAR)
    ]

    def exchanged(array):
        return lax.all_to_all(
            array, ("shot", "tm"), 0, 0, axis_index_groups=[order], tiled=True
        )

    received = exchanged(sent)
    tables, kept_scale = half_spectrum_tables()
    tables = np.concatenate(tables[:2] + order_tables(windows, own, blocks_of_time) + tables[2:], axis=0)
    held = SRC // shots
    restored = pl.pallas_call(
        functools.partial(gather_kernel, shots, float(kept_scale)),
        out_shape=jax.ShapeDtypeStruct((count, each, blocks * held, BLK), jnp.bfloat16),
        in_specs=[pl.BlockSpec(memory_space=pl.ANY)] + [vmem] * 3,
        out_specs=vmem,
        scratch_shapes=[
            pltpu.SMEM(delays.shape, jnp.int32),
            pltpu.VMEM((TILE, SRC * windows // TILE * each * BLK), jnp.float32),
            pltpu.VMEM((2 * SRC, (groups + 1) * HALF), jnp.bfloat16),
            pltpu.VMEM((2 * SRC, (groups + 1) * HALF), jnp.bfloat16),
            pltpu.VMEM((groups * SRC, WIN), jnp.bfloat16),
            pltpu.VMEM((groups * SRC, WIN), jnp.bfloat16),
            pltpu.VMEM((groups * SRC, WIN), jnp.bfloat16),
            pltpu.SemaphoreType.DMA(()),
        ],
        compiler_params=pltpu.CompilerParams(vmem_limit_bytes=40 * 1024 * 1024),
        cost_estimate=pl.CostEstimate(
            flops=2 * ITERS * groups * SRC * WIN * WIN * 5,
            bytes_accessed=2 * 1024 * 1024,
            transcendentals=ITERS * groups * SRC * HALF,
        ),
    )(delays, thresholds, received, jnp.asarray(tables))
    final = exchanged(restored)
    final = final.reshape(receivers, blocks, held, BLK).transpose(0, 2, 1, 3)
    return final.reshape(receivers, held, samples)


def shifted(array, axis, by):
    count = lax.axis_size(axis)
    pairs = [(i, i + by) for i in range(count) if 0 <= i + by < count]
    return lax.ppermute(array, axis, pairs)


def phase_table(length_first, length_second, period):
    first_index = jnp.arange(length_first, dtype=jnp.int32)[:, None]
    second_index = jnp.arange(length_second, dtype=jnp.int32)[None, :]
    return (first_index * second_index % period).astype(jnp.float32) * (2.0 * math.pi / period)


def make_tables():
    time_angle = phase_table(WIN, WIN, WIN)
    time_scale = 1.0 / math.sqrt(WIN)
    cos_forward = jnp.cos(time_angle).astype(jnp.bfloat16)
    sin_forward = -jnp.sin(time_angle).astype(jnp.bfloat16)
    cos_inverse = jnp.cos(time_angle) * time_scale
    sin_inverse = -jnp.sin(time_angle) * time_scale
    source_angle = phase_table(SRC, SRC, SRC)
    cos_source = jnp.cos(source_angle) / math.sqrt(SRC)
    sin_source = jnp.sin(source_angle) / math.sqrt(SRC)
    return (cos_forward, sin_forward, cos_inverse, sin_inverse, cos_source, sin_source)


def blend(estimate, own_delays):
    receivers, sources, samples = estimate.shape
    blocks = samples // BLK
    experiments = sources // SRC_EXP
    earlier = shifted(estimate[:, :, samples - BLK :], "tm", 1)
    upper = estimate.reshape(receivers, sources, blocks, BLK)
    shifts = own_delays.reshape(-1)
    row_index = jnp.arange(BLK, dtype=jnp.int32)[None, :, None]
    column_index = jnp.arange(BLK, dtype=jnp.int32)[None, None, :]
    select_same = (row_index == column_index - shifts[:, None, None]).astype(jnp.bfloat16)
    select_prior = (row_index == BLK + column_index - shifts[:, None, None]).astype(jnp.bfloat16)
    same = jnp.einsum("rsnb,sbi->rsni", upper, select_same, preferred_element_type=jnp.float32)
    onward = jnp.einsum("rsnb,sbi->rsni", upper, select_prior, preferred_element_type=jnp.float32)
    edge_part = jnp.einsum(
        "rsb,sbi->rsi", earlier, select_prior, preferred_element_type=jnp.float32
    )
    same = jnp.sum(same.reshape(receivers, experiments, SRC_EXP, blocks, BLK), axis=2)
    onward = jnp.sum(onward.reshape(receivers, experiments, SRC_EXP, blocks, BLK), axis=2)
    edge_part = jnp.sum(edge_part.reshape(receivers, experiments, SRC_EXP, BLK), axis=2)
    carried = jnp.concatenate([edge_part[:, :, None], onward[:, :, : blocks - 1]], axis=2)
    return (same + carried).reshape(receivers, experiments, samples)


def spread(residual, own_delays):
    receivers, experiments, samples = residual.shape
    blocks = samples // BLK
    later = shifted(residual[:, :, :BLK], "tm", -1)
    lower = residual.reshape(receivers, experiments, blocks, BLK)
    row_index = jnp.arange(BLK, dtype=jnp.int32)[None, None, :, None]
    column_index = jnp.arange(BLK, dtype=jnp.int32)[None, None, None, :]
    select_same = (row_index == column_index + own_delays[:, :, None, None]).astype(jnp.bfloat16)
    select_next = (row_index + BLK == column_index + own_delays[:, :, None, None]).astype(
        jnp.bfloat16
    )
    same = jnp.einsum("rena,ekai->rekni", lower, select_same, preferred_element_type=jnp.float32)
    backward = jnp.einsum(
        "rena,ekai->rekni", lower, select_next, preferred_element_type=jnp.float32
    )
    edge_part = jnp.einsum("rea,ekai->reki", later, select_next, preferred_element_type=jnp.float32)
    carried = jnp.concatenate([backward[:, :, :, 1:], edge_part[:, :, :, None]], axis=3)
    return (same + carried).reshape(receivers, experiments * SRC_EXP, samples)


def coherence(gathers, limits, tables):
    cos_forward, sin_forward, cos_inverse, sin_inverse, cos_source, sin_source = tables
    receivers, sources, samples = gathers.shape
    windows = samples // WIN
    careful = lax.Precision.HIGH
    scale = 1.0 / math.sqrt(WIN)
    signal = gathers.reshape(receivers * sources * windows, WIN)
    real_time = (jnp.dot(signal, cos_forward, preferred_element_type=jnp.float32) * scale).reshape(
        receivers, sources, samples
    )
    imag_time = (jnp.dot(signal, sin_forward, preferred_element_type=jnp.float32) * scale).reshape(
        receivers, sources, samples
    )

    def mixing(table, field):
        return jnp.einsum(
            "ps,rsx->rpx", table, field, precision=careful, preferred_element_type=jnp.float32
        )

    real_part = mixing(cos_source, real_time) + mixing(sin_source, imag_time)
    imag_part = mixing(cos_source, imag_time) - mixing(sin_source, real_time)
    magnitude = jnp.sqrt(real_part * real_part + imag_part * imag_part)
    bound = limits[None, :, None]
    factor = jnp.maximum(magnitude - bound, 0.0) / jnp.maximum(magnitude, bound)
    kept_real = real_part * factor
    kept_imag = imag_part * factor
    back_real = mixing(cos_source, kept_real) - mixing(sin_source, kept_imag)
    back_imag = mixing(cos_source, kept_imag) + mixing(sin_source, kept_real)
    restored = jnp.dot(
        back_real.reshape(-1, WIN),
        cos_inverse,
        precision=careful,
        preferred_element_type=jnp.float32,
    )
    restored = restored + jnp.dot(
        back_imag.reshape(-1, WIN),
        sin_inverse,
        precision=careful,
        preferred_element_type=jnp.float32,
    )
    return restored.reshape(receivers, sources, samples)


def gathers_of_own_samples(blended, delays, thresholds):
    tables = make_tables()
    local_count = blended.shape[1]
    own_delays = lax.dynamic_slice_in_dim(
        delays, lax.axis_index("shot") * local_count, local_count, 0
    )
    estimate = None
    for sweep in range(ITERS):
        if sweep == 0:
            residual = blended.astype(jnp.bfloat16)
            update = (RELAX * spread(residual, own_delays)).astype(jnp.bfloat16)
        else:
            residual = (blended - blend(estimate, own_delays)).astype(jnp.bfloat16)
            update = (estimate.astype(jnp.float32) + RELAX * spread(residual, own_delays)).astype(
                jnp.bfloat16
            )
        gathers = lax.all_to_all(update, "shot", split_axis=0, concat_axis=1, tiled=True)
        filtered = coherence(gathers, thresholds[sweep], tables).astype(jnp.bfloat16)
        estimate = lax.all_to_all(filtered, "shot", split_axis=1, concat_axis=0, tiled=True)
    return estimate


def whole_receivers_fit(shots, blocks_of_time, receivers, samples):
    held, windows = SRC // shots, samples // WIN
    return (
        receivers % (shots * blocks_of_time) == 0
        and shots % (2 * NEAR) == 0
        and held * 2 == SUB
        and windows % 2 == 0
        and windows * blocks_of_time == SUB
        and receivers // (shots * blocks_of_time) * SUB <= HALF
    )


def local(blended, delays, thresholds):
    shots, blocks_of_time = lax.axis_size("shot"), lax.axis_size("tm")
    if whole_receivers_fit(shots, blocks_of_time, blended.shape[0], blended.shape[2]):
        return gathers_of_all_samples(shots, blended, delays, thresholds)
    return gathers_of_own_samples(blended, delays, thresholds)


def solution(mesh):
    return jax.shard_map(
        local,
        mesh=mesh,
        in_specs=(P(None, "shot", "tm"), P(), P()),
        out_specs=P(None, "shot", "tm"),
        check_vma=False,
    )
```

```python
import functools
import math

import jax
import jax.numpy as jnp
import ml_dtypes
import numpy as np
from jax import lax
from jax.experimental import pallas as pl
from jax.experimental.pallas import tpu as pltpu
from jax.sharding import PartitionSpec as P

SRC = 64
SRC_EXP = 2
WIN = 256
BLK = 128
ITERS = 2


RELAX = 0.5
HALF = WIN // 2
SUB = 8
TILE = 256
NEAR = 4


def bfloat_scale(table):
    values = np.unique(np.abs(table).round(12))
    factors = 1.0 + np.arange(4096) / 4096.0
    scaled = factors[:, None] * values
    lost = scaled.astype(ml_dtypes.bfloat16).astype(np.float64) - scaled
    return factors[np.argmin(np.sum((lost / factors[:, None]) ** 2, axis=1))]


def half_spectrum_tables():
    moment = np.arange(WIN)
    angle = (moment[:, None] * np.arange(HALF)[None, :] % WIN) * (2.0 * math.pi / WIN)
    nyquist = np.where(moment % 2 == 0, 1.0, -1.0)
    sine = -np.sin(angle)
    sine[:, 0] = nyquist
    forward = np.concatenate([np.cos(angle), sine], axis=1).astype(ml_dtypes.bfloat16)
    inverse = np.concatenate([np.cos(angle), sine], axis=1).T / math.sqrt(WIN)
    inverse[0] *= 0.5
    inverse[HALF] *= 0.5
    source = np.arange(SRC)
    turn = (source[:, None] * source[None, :] % SRC) * (2.0 * math.pi / SRC)
    cosine, sine = np.cos(turn) / math.sqrt(SRC), np.sin(turn) / math.sqrt(SRC)
    onward = np.block([[cosine, sine], [-sine, cosine]])
    time_scale = bfloat_scale(inverse)
    forward, inverse = (x.astype(ml_dtypes.bfloat16) for x in (forward, inverse * time_scale))
    tables = forward, inverse, high_and_low(onward / math.sqrt(WIN)), high_and_low(onward.T)
    return tables, 1.0 / time_scale


def high_and_low(table):
    high = table.astype(ml_dtypes.bfloat16)
    low = (table - high.astype(np.float64)).astype(ml_dtypes.bfloat16)
    return np.concatenate([high, low], axis=1)


def rearranging(shape, axes):
    order = np.arange(math.prod(shape)).reshape(shape).transpose(axes).reshape(-1)
    return np.eye(order.size)[order].astype(ml_dtypes.bfloat16)


def order_tables(windows, own, blocks_of_time):
    shots, sources = TILE // (2 * windows * own), TILE // windows
    return (
        rearranging(
            (NEAR, blocks_of_time, shots // NEAR, windows // blocks_of_time, 2, own),
            (2, 0, 5, 4, 1, 3),
        ),
        rearranging((sources, windows), (1, 0)),
        rearranging((windows, sources), (1, 0)),
    )


def product(left, right):
    return jnp.dot(left, right, preferred_element_type=jnp.float32)


def gather_kernel(
    shots,
    kept_scale,
    delays_far,
    limits,
    received,
    tables,
    out,
    delays,
    records,
    field,
    mixed,
    back,
    firsts,
    estimates,
    sem,
):
    copy = pltpu.make_async_copy(delays_far, delays, sem)
    copy.start()
    forward, inverse, order_arrived, order_windows, order_sources = (
        tables.at[pl.ds(at * TILE, TILE)] for at in range(5)
    )
    onward, backward = (
        tables.at[pl.ds(5 * TILE + at * 2 * SRC, 2 * SRC)] for at in range(2)
    )
    count, receivers, rows, _ = received.shape
    blocks_of_time = count // shots
    experiments, sources = delays.shape[1], SRC
    windows = blocks_of_time * rows * shots // (2 * experiments)
    groups = receivers * windows
    parts = windows // blocks_of_time
    some = TILE // windows
    lane = lax.broadcasted_iota(jnp.int32, (windows, BLK), 1)
    row = lax.broadcasted_iota(jnp.int32, (windows, BLK), 0)
    lane_of_group = lax.broadcasted_iota(jnp.int32, (sources, HALF), 1)
    lane_of_some = lax.broadcasted_iota(jnp.int32, (some, HALF), 1)

    planes, some_planes = shots // NEAR, TILE // (rows * blocks_of_time * NEAR)
    bounds = []
    for sweep in range(ITERS):
        limit = limits[sweep : sweep + 1, :] * kept_scale
        p = lax.broadcasted_iota(jnp.int32, (sources, sources), 0)
        q = lax.broadcasted_iota(jnp.int32, (sources, sources), 1)
        bound = jnp.sum(jnp.where(p == q, limit, 0.0), axis=1, keepdims=True)
        mirrored = (p + q == 0) | (p + q == sources)
        bound_mirrored = jnp.sum(jnp.where(mirrored, limit, 0.0), axis=1, keepdims=True)
        bounds.append((bound, bound_mirrored))

    arrived = [
        jnp.concatenate(
            [
                received[pl.ds(side * planes + chunk * some_planes, some_planes), r].reshape(-1, BLK)
                for side in range(blocks_of_time * NEAR)
            ],
            axis=0,
        )
        for chunk in range(sources // some)
        for r in range(receivers)
    ]
    records[...] = product(order_arrived[...], jnp.concatenate(arrived, axis=1))

    copy.wait()

    def advanced(even, odd, delay):
        by = (BLK - delay) & (BLK - 1)
        even, odd = pltpu.roll(even, by, 1), pltpu.roll(odd, by, 1)
        after = jnp.where(row < windows - 1, pltpu.roll(even, windows - 1, 0), 0.0)
        same = lane < BLK - delay
        return jnp.where(same, even, odd), jnp.where(same, odd, after)

    def moved_by(even, odd, ahead_by):
        ahead = ahead_by >= 0
        by = (BLK - ahead_by) & (BLK - 1)
        even, odd = pltpu.roll(even, by, 1), pltpu.roll(odd, by, 1)
        other = pltpu.roll(jnp.where(ahead, even, odd), jnp.where(ahead, windows - 1, 1), 0)
        other = jnp.where(row != jnp.where(ahead, windows - 1, 0), other, 0.0)
        same = ((lane + ahead_by) & -BLK) == 0
        return (
            jnp.where(same, even, jnp.where(ahead, odd, other)),
            jnp.where(same, odd, jnp.where(ahead, other, even)),
        )

    def columns(group):
        return slice(group * HALF, (group + 1) * HALF)

    def first_update(r, chunk):
        updated = []
        for at in range(0, some, SRC_EXP):
            even, odd = (
                records[pl.ds((at + half) * windows, windows), columns(chunk * receivers + r)]
                for half in range(2)
            )
            for k in range(SRC_EXP):
                early = advanced(even, odd, delays[k, (chunk * some + at) // SRC_EXP])
                updated.append(jnp.concatenate([RELAX * x for x in early], axis=1))
        updated = jnp.concatenate(updated, axis=0).astype(jnp.bfloat16)
        firsts[pl.ds((r * sources + chunk * some) * windows, TILE), :] = updated
        return updated

    def side_by_side(values):
        return jnp.concatenate(values, axis=1)

    def estimates_by_source():
        parts_of_rows = []
        for r, chunk in turns:
            starts = [(r * windows + w) * sources + chunk * some for w in range(windows)]
            rows_of_part = [estimates[start : start + some, :] for start in starts]
            parts_of_rows.append(jnp.concatenate(rows_of_part, axis=0))
        return product(order_sources[...], side_by_side(parts_of_rows))

    def later_update(r, chunk, before):
        first = (r * sources + chunk * some) * windows
        updated = []
        for at in range(0, some, SRC_EXP):
            lags = [delays[k, (chunk * some + at) // SRC_EXP] for k in range(SRC_EXP)]
            spread = firsts[pl.ds(first + at * windows, SRC_EXP * windows), :]
            spread = spread.astype(jnp.float32)
            estimate = [
                tuple(
                    before[(at + k) * windows : (at + k + 1) * windows, columns(half)]
                    for half in range(2)
                )
                for k in range(SRC_EXP)
            ]
            for k in range(SRC_EXP):
                even, odd = estimate[k]
                other = moved_by(*estimate[1 - k], lags[k] - lags[1 - k])
                stays = (row < windows - 1) | (lane < BLK - lags[k])
                even = RELAX * (even - other[0])
                odd = jnp.where(stays, RELAX * (odd - other[1]), odd)
                step = spread[k * windows : (k + 1) * windows]
                updated.append(jnp.concatenate([even, odd], axis=1) + step)
        return jnp.concatenate(updated, axis=0).astype(jnp.bfloat16)

    turns = [(r, chunk) for r in range(receivers) for chunk in range(sources // some)]

    def update_and_forward_in_time(sweep):
        if sweep:
            before = estimates_by_source()
            updates = [
                later_update(r, chunk, before[:, at * WIN : (at + 1) * WIN])
                for at, (r, chunk) in enumerate(turns)
            ]
        else:
            updates = [first_update(r, chunk) for r, chunk in turns]
        signal = product(order_windows[...], side_by_side(updates)).astype(jnp.bfloat16)
        signal = [signal[:, at * WIN : (at + 1) * WIN] for at in range(len(turns))]
        spectra = product(jnp.concatenate(signal, axis=0), forward[...])
        nyquists = [jnp.zeros((some, HALF), jnp.float32) for _ in range(sources // some)]
        for at, (r, chunk) in enumerate(turns):
            for w in range(windows):
                group = r * windows + w
                start = at * TILE + w * some
                real, imag = (spectra[start : start + some, columns(half)] for half in range(2))
                moved = pltpu.roll(imag, group, 1) if group else imag
                nyquists[chunk] = jnp.where(lane_of_some == group, moved, nyquists[chunk])
                imag = jnp.where(lane_of_some == 0, 0.0, imag)
                put(field, columns(group), real, imag, chunk * some)
        for chunk, nyquist in enumerate(nyquists):
            put(field, columns(groups), nyquist, jnp.zeros_like(nyquist), chunk * some)

    def put(ref, where, real, imag, first=0):
        for at, value in enumerate((real, imag)):
            start = at * sources + first
            ref[start : start + value.shape[0], where] = value.astype(jnp.bfloat16)

    def mixing(table, ref):
        values = ref[...]
        total = product(table[...], jnp.concatenate([values, values], axis=0))
        return total[:sources], total[sources:]

    def shrink(sweep):
        bound, bound_mirrored = bounds[sweep]
        real, imag = mixing(onward, field)
        inverse_size = lax.rsqrt(real * real + imag * imag)
        factor = jnp.maximum(kept_scale - bound * inverse_size, 0.0) + jnp.maximum(
            kept_scale - bound_mirrored * inverse_size, 0.0
        )
        put(mixed, slice(None), real * factor, imag * factor)

    def back_in_source():
        real, imag = mixing(backward, mixed)
        nyquist = real[:, columns(groups)]
        for group in range(groups):
            moved = pltpu.roll(nyquist, HALF - group, 1) if group else nyquist
            own_imag = jnp.where(lane_of_group == 0, moved, imag[:, columns(group)])
            rows_of_group = slice(group * sources, (group + 1) * sources)
            for half, value in enumerate((real[:, columns(group)], own_imag)):
                back[rows_of_group, columns(half)] = value.astype(jnp.bfloat16)

    def swapped(value):
        return pltpu.roll(value, SUB // 2, 1)

    def deliver(r, w, restored):
        low = lax.broadcasted_iota(jnp.int32, (sources // SUB, SUB, BLK), 1) < SUB // 2
        pieces = []
        for part in range(2):
            window = restored[part * sources : (part + 1) * sources]
            even = window[:, :BLK].reshape(sources // SUB, SUB, BLK)
            odd = window[:, BLK:].reshape(sources // SUB, SUB, BLK)
            pieces.append(
                (jnp.where(low, even, swapped(odd)), jnp.where(low, swapped(even), odd))
            )
        block, inside = w // parts, w % parts
        for side in range(2):
            both = jnp.concatenate([pieces[0][side], pieces[1][side]], axis=1)
            both = both.astype(jnp.bfloat16)
            for k in range(sources // SUB):
                plane, near = divmod(2 * k + side, NEAR)
                target = (near * blocks_of_time + block) * planes + plane
                out[target, r, inside * SUB : (inside + 2) * SUB, :] = both[k]

    for sweep in range(ITERS):
        update_and_forward_in_time(sweep)
        shrink(sweep)
        back_in_source()
        restored = product(back[...], inverse[...])
        if sweep < ITERS - 1:
            estimates[...] = restored.astype(jnp.bfloat16)
            continue
        for group in range(0, groups, 2):
            pair = restored[group * sources : (group + 2) * sources]
            deliver(group // windows, group % windows, pair)


def cast_kernel(blended, delays, limits, sent, delays_near, limits_near, held, sems):
    pieces = sems.shape[0] - 2
    count = blended.shape[0] // pieces
    spans = [pl.ds(at * count, count) for at in range(pieces)]
    copies = [
        pltpu.make_async_copy(blended.at[span], held.at[span], sems.at[at])
        for at, span in enumerate(spans)
    ]
    small = [
        pltpu.make_async_copy(delays, delays_near, sems.at[pieces]),
        pltpu.make_async_copy(limits, limits_near, sems.at[pieces + 1]),
    ]
    for copy in copies + small:
        copy.start()
    for copy, span in zip(copies, spans):
        copy.wait()
        sent[span] = held[span].astype(jnp.bfloat16)
    for copy in small:
        copy.wait()


def gathers_of_all_samples(shots, blended, delays, thresholds):
    receivers, own, samples = blended.shape
    blocks_of_time = lax.axis_size("tm")
    count = shots * blocks_of_time
    each = receivers // count
    blocks = samples // BLK
    windows = samples * blocks_of_time // WIN
    groups = each * windows
    rows = blocks * own
    sent = blended.reshape(receivers, own, blocks, BLK).transpose(0, 2, 1, 3)
    sent = sent.reshape(count, each, rows, BLK)
    vmem, far = pl.BlockSpec(memory_space=pltpu.VMEM), pl.BlockSpec(memory_space=pl.ANY)

    def kept_far(array):
        return pltpu.with_memory_space_constraint(array, pltpu.HBM)

    sent, delays, thresholds = pl.pallas_call(
        cast_kernel,
        out_shape=(
            jax.ShapeDtypeStruct(sent.shape, jnp.bfloat16),
            jax.ShapeDtypeStruct(delays.T.shape, delays.dtype),
            jax.ShapeDtypeStruct(thresholds.shape, thresholds.dtype),
        ),
        in_specs=[far] * 3,
        out_specs=[vmem] * 3,
        scratch_shapes=[
            pltpu.VMEM(sent.shape, jnp.float32),
            pltpu.SemaphoreType.DMA((1 + 2,)),
        ],
        compiler_params=pltpu.CompilerParams(vmem_limit_bytes=8 * 1024 * 1024),
    )(kept_far(sent), kept_far(delays.T), kept_far(thresholds))
    order = [
        (plane * NEAR + near) * blocks_of_time + block
        for near in range(NEAR)
        for block in range(blocks_of_time)
        for plane in range(shots // NEAR)
    ]

    def exchanged(array):
        return lax.all_to_all(
            array, ("shot", "tm"), 0, 0, axis_index_groups=[order], tiled=True
        )

    received = exchanged(sent)
    tables, kept_scale = half_spectrum_tables()
    tables = np.concatenate(tables[:2] + order_tables(windows, own, blocks_of_time) + tables[2:], axis=0)
    held = SRC // shots
    restored = pl.pallas_call(
        functools.partial(gather_kernel, shots, float(kept_scale)),
        out_shape=jax.ShapeDtypeStruct((count, each, blocks * held, BLK), jnp.bfloat16),
        in_specs=[pl.BlockSpec(memory_space=pl.ANY)] + [vmem] * 3,
        out_specs=vmem,
        scratch_shapes=[
            pltpu.SMEM(delays.shape, jnp.int32),
            pltpu.VMEM((TILE, SRC * windows // TILE * each * BLK), jnp.float32),
            pltpu.VMEM((2 * SRC, (groups + 1) * HALF), jnp.bfloat16),
            pltpu.VMEM((2 * SRC, (groups + 1) * HALF), jnp.bfloat16),
            pltpu.VMEM((groups * SRC, WIN), jnp.bfloat16),
            pltpu.VMEM((groups * SRC, WIN), jnp.bfloat16),
            pltpu.VMEM((groups * SRC, WIN), jnp.bfloat16),
            pltpu.SemaphoreType.DMA(()),
        ],
        compiler_params=pltpu.CompilerParams(vmem_limit_bytes=40 * 1024 * 1024),
        cost_estimate=pl.CostEstimate(
            flops=2 * ITERS * groups * SRC * WIN * WIN * 5,
            bytes_accessed=2 * 1024 * 1024,
            transcendentals=ITERS * groups * SRC * HALF,
        ),
    )(delays, thresholds, received, jnp.asarray(tables))
    final = exchanged(restored)
    final = final.reshape(receivers, blocks, held, BLK).transpose(0, 2, 1, 3)
    return final.reshape(receivers, held, samples)


def shifted(array, axis, by):
    count = lax.axis_size(axis)
    pairs = [(i, i + by) for i in range(count) if 0 <= i + by < count]
    return lax.ppermute(array, axis, pairs)


def phase_table(length_first, length_second, period):
    first_index = jnp.arange(length_first, dtype=jnp.int32)[:, None]
    second_index = jnp.arange(length_second, dtype=jnp.int32)[None, :]
    return (first_index * second_index % period).astype(jnp.float32) * (2.0 * math.pi / period)


def make_tables():
    time_angle = phase_table(WIN, WIN, WIN)
    time_scale = 1.0 / math.sqrt(WIN)
    cos_forward = jnp.cos(time_angle).astype(jnp.bfloat16)
    sin_forward = -jnp.sin(time_angle).astype(jnp.bfloat16)
    cos_inverse = jnp.cos(time_angle) * time_scale
    sin_inverse = -jnp.sin(time_angle) * time_scale
    source_angle = phase_table(SRC, SRC, SRC)
    cos_source = jnp.cos(source_angle) / math.sqrt(SRC)
    sin_source = jnp.sin(source_angle) / math.sqrt(SRC)
    return (cos_forward, sin_forward, cos_inverse, sin_inverse, cos_source, sin_source)


def blend(estimate, own_delays):
    receivers, sources, samples = estimate.shape
    blocks = samples // BLK
    experiments = sources // SRC_EXP
    earlier = shifted(estimate[:, :, samples - BLK :], "tm", 1)
    upper = estimate.reshape(receivers, sources, blocks, BLK)
    shifts = own_delays.reshape(-1)
    row_index = jnp.arange(BLK, dtype=jnp.int32)[None, :, None]
    column_index = jnp.arange(BLK, dtype=jnp.int32)[None, None, :]
    select_same = (row_index == column_index - shifts[:, None, None]).astype(jnp.bfloat16)
    select_prior = (row_index == BLK + column_index - shifts[:, None, None]).astype(jnp.bfloat16)
    same = jnp.einsum("rsnb,sbi->rsni", upper, select_same, preferred_element_type=jnp.float32)
    onward = jnp.einsum("rsnb,sbi->rsni", upper, select_prior, preferred_element_type=jnp.float32)
    edge_part = jnp.einsum(
        "rsb,sbi->rsi", earlier, select_prior, preferred_element_type=jnp.float32
    )
    same = jnp.sum(same.reshape(receivers, experiments, SRC_EXP, blocks, BLK), axis=2)
    onward = jnp.sum(onward.reshape(receivers, experiments, SRC_EXP, blocks, BLK), axis=2)
    edge_part = jnp.sum(edge_part.reshape(receivers, experiments, SRC_EXP, BLK), axis=2)
    carried = jnp.concatenate([edge_part[:, :, None], onward[:, :, : blocks - 1]], axis=2)
    return (same + carried).reshape(receivers, experiments, samples)


def spread(residual, own_delays):
    receivers, experiments, samples = residual.shape
    blocks = samples // BLK
    later = shifted(residual[:, :, :BLK], "tm", -1)
    lower = residual.reshape(receivers, experiments, blocks, BLK)
    row_index = jnp.arange(BLK, dtype=jnp.int32)[None, None, :, None]
    column_index = jnp.arange(BLK, dtype=jnp.int32)[None, None, None, :]
    select_same = (row_index == column_index + own_delays[:, :, None, None]).astype(jnp.bfloat16)
    select_next = (row_index + BLK == column_index + own_delays[:, :, None, None]).astype(
        jnp.bfloat16
    )
    same = jnp.einsum("rena,ekai->rekni", lower, select_same, preferred_element_type=jnp.float32)
    backward = jnp.einsum(
        "rena,ekai->rekni", lower, select_next, preferred_element_type=jnp.float32
    )
    edge_part = jnp.einsum("rea,ekai->reki", later, select_next, preferred_element_type=jnp.float32)
    carried = jnp.concatenate([backward[:, :, :, 1:], edge_part[:, :, :, None]], axis=3)
    return (same + carried).reshape(receivers, experiments * SRC_EXP, samples)


def coherence(gathers, limits, tables):
    cos_forward, sin_forward, cos_inverse, sin_inverse, cos_source, sin_source = tables
    receivers, sources, samples = gathers.shape
    windows = samples // WIN
    careful = lax.Precision.HIGH
    scale = 1.0 / math.sqrt(WIN)
    signal = gathers.reshape(receivers * sources * windows, WIN)
    real_time = (jnp.dot(signal, cos_forward, preferred_element_type=jnp.float32) * scale).reshape(
        receivers, sources, samples
    )
    imag_time = (jnp.dot(signal, sin_forward, preferred_element_type=jnp.float32) * scale).reshape(
        receivers, sources, samples
    )

    def mixing(table, field):
        return jnp.einsum(
            "ps,rsx->rpx", table, field, precision=careful, preferred_element_type=jnp.float32
        )

    real_part = mixing(cos_source, real_time) + mixing(sin_source, imag_time)
    imag_part = mixing(cos_source, imag_time) - mixing(sin_source, real_time)
    magnitude = jnp.sqrt(real_part * real_part + imag_part * imag_part)
    bound = limits[None, :, None]
    factor = jnp.maximum(magnitude - bound, 0.0) / jnp.maximum(magnitude, bound)
    kept_real = real_part * factor
    kept_imag = imag_part * factor
    back_real = mixing(cos_source, kept_real) - mixing(sin_source, kept_imag)
    back_imag = mixing(cos_source, kept_imag) + mixing(sin_source, kept_real)
    restored = jnp.dot(
        back_real.reshape(-1, WIN),
        cos_inverse,
        precision=careful,
        preferred_element_type=jnp.float32,
    )
    restored = restored + jnp.dot(
        back_imag.reshape(-1, WIN),
        sin_inverse,
        precision=careful,
        preferred_element_type=jnp.float32,
    )
    return restored.reshape(receivers, sources, samples)


def gathers_of_own_samples(blended, delays, thresholds):
    tables = make_tables()
    local_count = blended.shape[1]
    own_delays = lax.dynamic_slice_in_dim(
        delays, lax.axis_index("shot") * local_count, local_count, 0
    )
    estimate = None
    for sweep in range(ITERS):
        if sweep == 0:
            residual = blended.astype(jnp.bfloat16)
            update = (RELAX * spread(residual, own_delays)).astype(jnp.bfloat16)
        else:
            residual = (blended - blend(estimate, own_delays)).astype(jnp.bfloat16)
            update = (estimate.astype(jnp.float32) + RELAX * spread(residual, own_delays)).astype(
                jnp.bfloat16
            )
        gathers = lax.all_to_all(update, "shot", split_axis=0, concat_axis=1, tiled=True)
        filtered = coherence(gathers, thresholds[sweep], tables).astype(jnp.bfloat16)
        estimate = lax.all_to_all(filtered, "shot", split_axis=1, concat_axis=0, tiled=True)
    return estimate


def whole_receivers_fit(shots, blocks_of_time, receivers, samples):
    held, windows = SRC // shots, samples // WIN
    return (
        receivers % (shots * blocks_of_time) == 0
        and shots % (2 * NEAR) == 0
        and held * 2 == SUB
        and windows % 2 == 0
        and windows * blocks_of_time == SUB
        and receivers // (shots * blocks_of_time) * SUB <= HALF
    )


def local(blended, delays, thresholds):
    shots, blocks_of_time = lax.axis_size("shot"), lax.axis_size("tm")
    if whole_receivers_fit(shots, blocks_of_time, blended.shape[0], blended.shape[2]):
        return gathers_of_all_samples(shots, blended, delays, thresholds)
    return gathers_of_own_samples(blended, delays, thresholds)


def solution(mesh):
    return jax.shard_map(
        local,
        mesh=mesh,
        in_specs=(P(None, "shot", "tm"), P(), P()),
        out_specs=P(None, "shot", "tm"),
        check_vma=False,
    )
```
